32 devices in a mesh: seq: 8 (over y, x, core), rows: 4 (over z).
Axes of the slice: x: 2, y: 2, z: 4, core: 2. Of those that a mesh axis runs over, the one named last changes fastest.
Arguments:
- dec_input: bfloat16 [4, 2048, 512], P('rows', 'seq'), may hold values from -6 to 6
- encoded: bfloat16 [4, 2048, 512], P('rows', 'seq'), may hold values from -6 to 6
- segment_ids: int32 [4, 2048], P('rows', 'seq'), may hold values from 0 to 3, as said below
- pair_tags: int32 [4, 4], P('rows'), may hold values from 0 to 15
- enc_lengths: int32 [4, 4], P('rows'), may hold values from 1 to 2045, as said below
- out_grad: bfloat16 [4, 2048, 512], P('rows', 'seq'), may hold values from -6 to 6
- tag_table: bfloat16 [16, 512], replicated, may hold values from -3 to 3
- self_qkv: bfloat16 [512, 1536], replicated, may hold values from -0.25 to 0.25
- self_out: bfloat16 [512, 512], replicated, may hold values from -3 to 3
- cross_query: bfloat16 [512, 512], replicated, may hold values from -0.25 to 0.25
- cross_kv: bfloat16 [512, 1024], replicated, may hold values from -0.25 to 0.25
- cross_out: bfloat16 [512, 512], replicated, may hold values from -3 to 3
- ffn_in: bfloat16 [512, 2048], replicated, may hold values from -0.25 to 0.25
- ffn_in_bias: bfloat16 [2048], replicated, may hold values from -3 to 3
- ffn_out: bfloat16 [2048, 512], replicated, may hold values from -0.125 to 0.125
- ffn_out_bias: bfloat16 [512], replicated, may hold values from -2 to 2
- norm_gain: bfloat16 [3, 512], replicated, may hold values from 0.5 to 1.5
- norm_bias: bfloat16 [3, 512], replicated, may hold values from -2 to 2
Outputs:
- layer_out: bfloat16 [4, 2048, 512], P('rows', 'seq')
- input_grad: float32 [4, 2048, 512], P('rows', 'seq')
- encoded_grad: float32 [4, 2048, 512], P('rows', 'seq')
- tag_table_grad: float32 [16, 512], P('rows')
- self_qkv_grad: float32 [512, 1536], P('rows')
- self_out_grad: float32 [512, 512], P('rows')
- cross_query_grad: float32 [512, 512], P('rows')
- cross_kv_grad: float32 [512, 1024], P('rows')
- cross_out_grad: float32 [512, 512], P('rows')
- ffn_in_grad: float32 [512, 2048], P('rows')
- ffn_in_bias_grad: float32 [2048], P('rows')
- ffn_out_grad: float32 [2048, 512], P('rows')
- ffn_out_bias_grad: float32 [512], P('rows')
- norm_gain_grad: float32 [3, 512], P(None, 'rows')
- norm_bias_grad: float32 [3, 512], P(None, 'rows')
The draws below stay inside these ranges and needn't reach their ends.
Inputs may be any that keep to these rules, and one draw needn't show every extreme that they name: `segment_ids`: in each row the document numbers never fall, start at 0 and reach 3; in every row one document starts within the first 256 tokens and ends within the last 256. `enc_lengths`: each row's 4 lengths are positive and sum to 2048; the document that spans a row's decoder tokens from the first 256 to the last 256 also spans its encoder tokens from the first 256 to the last 256.
All inputs are finite; a program needn't handle non-finite values.
Results may differ from the reference program's by a relative error of at most 0.035.
Values may be sent and summed in bfloat16 or wider, within the bound.
No kernel may reach another device: no remote copies, remote signals or barrier semaphores. Data moves between devices by JAX's collectives and lax.ppermute only.
A program may use at most 192 MiB of HBM per device.

```python
import math
import jax
import jax.numpy as jnp
from jax import lax

D = 512
H = 8
HD = 64
FF = 2048
TOK_DEV = 256
KBLK = 512
SEGS = 4
NTAGS = 16
SEQ_LEN = 2048
ENC_LEN = 2048
NROWS = 4


def long_slots(key):
    return jax.random.randint(jax.random.fold_in(key, 71), (NROWS,), 0, SEGS)


def row_lengths(key, long_index, total_length):
    shorter = jax.random.randint(key, (NROWS, SEGS), 1, TOK_DEV // 4 + 1)
    is_long = jnp.arange(SEGS, dtype=jnp.int32)[None, :] == long_index[:, None]
    shorter = jnp.where(is_long, 0, shorter)
    remainder = total_length - jnp.sum(shorter, axis=1, keepdims=True)
    return jnp.where(is_long, remainder, shorter).astype(jnp.int32)


def draw_segment_ids(key, part):
    leading = long_slots(key)
    key = jax.random.fold_in(key, 3)
    lengths = row_lengths(key, leading, SEQ_LEN)
    segment_ends = jnp.cumsum(lengths, axis=1)
    positions = jnp.arange(SEQ_LEN, dtype=jnp.int32)
    boundary_marks = (positions[None, :, None] >= segment_ends[:, None, :SEGS - 1]).astype(jnp.int32)
    return jnp.sum(boundary_marks, axis=2).astype(jnp.int32)


def draw_enc_lengths(key, part):
    leading = long_slots(key)
    key = jax.random.fold_in(key, 5)
    return row_lengths(key, leading, ENC_LEN)


def set_ends(result, own_key, smallest, top_value):
    dims = result.shape
    place = [jax.random.randint(jax.random.fold_in(own_key, axis), (), 0, dims[axis]) for axis in range(len(dims))]
    result = result.at[tuple(place)].set(smallest)
    longest = dims.index(max(dims))
    place[longest] = (place[longest] + 1) % dims[longest]
    return result.at[tuple(place)].set(top_value)


def block_scale(key, extent, shards, smallest, top_value):
    level, own = 1.0, jax.random.fold_in(key, 6)
    for axis_at, parts in shards:
        draws = jnp.exp(jax.random.uniform(jax.random.fold_in(own, axis_at), (parts,), jnp.float32, smallest / len(shards), top_value / len(shards)))
        level = level * jnp.repeat(draws, extent[axis_at] // parts).reshape([-1 if axis == axis_at else 1 for axis in range(len(extent))])
    return level


def normal_values(stream_key, dims, width, reach, split=(), held_as=jnp.bfloat16):
    result = width * jax.random.normal(stream_key, dims, jnp.float32)
    if split:
        result = result * block_scale(stream_key, dims, split, -0.22, 0.18)
    return jnp.clip(result, -reach, reach).astype(held_as)


def setup_inputs(seed: int = 0) -> dict:
    arg_keys = jax.random.split(jax.random.key(seed), 19)
    dec_input = normal_values(arg_keys[0], (NROWS, SEQ_LEN, D), 1.0, 6.0, ((0, 4), (1, 8)))
    encoded = normal_values(arg_keys[1], (NROWS, ENC_LEN, D), 1.0, 6.0, ((0, 4), (1, 8)))
    segment_ids = draw_segment_ids(jax.random.fold_in(arg_keys[18], 71), 0)
    pair_tags = set_ends(jax.random.randint(arg_keys[3], (NROWS, SEGS), 0, NTAGS), jax.random.fold_in(arg_keys[3], 1), 0, NTAGS - 1).astype(jnp.int32)
    enc_lengths = draw_enc_lengths(jax.random.fold_in(arg_keys[18], 71), 0)
    out_grad = normal_values(arg_keys[5], (NROWS, SEQ_LEN, D), 1.0, 6.0, ((0, 4), (1, 8)))
    tag_table = normal_values(arg_keys[6], (NTAGS, D), 0.5, 3.0)
    self_qkv = normal_values(arg_keys[7], (D, 3 * D), D ** -0.5, 0.25)
    self_out = normal_values(arg_keys[8], (D, D), 4 ** -0.5, 3.0)
    cross_query = normal_values(arg_keys[9], (D, D), D ** -0.5, 0.25)
    cross_kv = normal_values(arg_keys[10], (D, 2 * D), D ** -0.5, 0.25)
    cross_out = normal_values(arg_keys[11], (D, D), 4 ** -0.5, 3.0)
    ffn_in = normal_values(arg_keys[12], (D, FF), D ** -0.5, 0.25)
    ffn_in_bias = normal_values(arg_keys[13], (FF,), 0.5, 3.0)
    ffn_out = normal_values(arg_keys[14], (FF, D), FF ** -0.5, 0.125)
    ffn_out_bias = normal_values(arg_keys[15], (D,), 0.3, 2.0)
    norm_gain = jnp.clip(1.0 + 0.1 * jax.random.normal(arg_keys[16], (3, D), jnp.float32), 0.5, 1.5).astype(jnp.bfloat16)
    norm_bias = normal_values(arg_keys[17], (3, D), 0.3, 2.0)
    return {"dec_input": dec_input, "encoded": encoded, "segment_ids": segment_ids, "pair_tags": pair_tags, "enc_lengths": enc_lengths, "out_grad": out_grad, "tag_table": tag_table, "self_qkv": self_qkv, "self_out": self_out, "cross_query": cross_query, "cross_kv": cross_kv, "cross_out": cross_out, "ffn_in": ffn_in, "ffn_in_bias": ffn_in_bias, "ffn_out": ffn_out, "ffn_out_bias": ffn_out_bias, "norm_gain": norm_gain, "norm_bias": norm_bias}


norm_eps = 1e-05
masked_value = -1e+30

@jax.custom_vjp
def low(v):
    return lax.optimization_barrier(v.astype(jnp.bfloat16)).astype(jnp.float32)

@jax.custom_vjp
def low_back(v):
    return v

def low_keep(v):
    return (low(v), None)

def low_pass(kept, grad):
    return (grad,)

def back_keep(v):
    return (v, None)

def back_low(kept, grad):
    return (low(grad),)
low.defvjp(low_keep, low_pass)
low_back.defvjp(back_keep, back_low)

def rounded_both(tensor):
    return low(low_back(tensor))

def product(left, right):
    return jnp.dot(left, right, precision=lax.Precision.HIGHEST)

def layer_norm(values, gain_row, shift_row):
    centered = values - lax.optimization_barrier(jnp.mean(values, axis=-1, keepdims=True))
    variance = lax.optimization_barrier(jnp.mean(centered * centered, axis=-1, keepdims=True))
    return centered * lax.rsqrt(variance + norm_eps) * gain_row + shift_row

def attention(query_rows, key_rows, value_rows, query_segments, key_segments, causal):
    query_count = query_rows.shape[0]
    block_count = query_count // KBLK
    query_heads = query_rows.reshape(query_count, H, HD)
    key_heads = key_rows.reshape(key_rows.shape[0], H, HD)
    value_heads = value_rows.reshape(value_rows.shape[0], H, HD)
    key_positions = jnp.arange(key_rows.shape[0], dtype=jnp.int32)
    score_scale = 1.0 / math.sqrt(HD)

    def one_block(block_index):
        block_start = block_index * KBLK
        query_block = lax.dynamic_slice_in_dim(query_heads, block_start, KBLK, 0)
        segment_block = lax.dynamic_slice_in_dim(query_segments, block_start, KBLK, 0)
        scores = jnp.einsum('qhd,khd->hqk', query_block, key_heads, precision=lax.Precision.HIGHEST) * score_scale
        scores = low_back(scores)
        allowed = segment_block[:, None] == key_segments[None, :]
        if causal:
            query_positions = block_start + jnp.arange(KBLK, dtype=jnp.int32)
            allowed = allowed & (query_positions[:, None] >= key_positions[None, :])
        scores = jnp.where(allowed[None], scores, masked_value)
        row_top = lax.optimization_barrier(jnp.max(scores, axis=-1, keepdims=True))
        weights = jnp.where(allowed[None], jnp.exp(scores - row_top), 0.0)
        weights = weights / lax.optimization_barrier(jnp.sum(weights, axis=-1, keepdims=True))
        weights = low(weights)
        mixed_heads = jnp.einsum('hqk,khd->qhd', weights, value_heads, precision=lax.Precision.HIGHEST)
        return mixed_heads.reshape(KBLK, H * HD)
    outputs = lax.map(jax.checkpoint(one_block), jnp.arange(block_count, dtype=jnp.int32))
    return outputs.reshape(query_count, H * HD)

def decoder_layer(floats, segment_row, tag_row, length_row):
    dec_row, enc_row, tag_table, self_qkv, self_out, cross_query, cross_kv, cross_out, ffn_in, ffn_in_bias, ffn_out, ffn_out_bias, norm_gain, norm_bias = floats
    model_width = dec_row.shape[1]
    token_tags = tag_row[segment_row]
    segment_ends = jnp.cumsum(length_row)
    enc_positions = jnp.arange(enc_row.shape[0], dtype=jnp.int32)
    enc_segments = lax.optimization_barrier(jnp.sum((enc_positions[:, None] >= segment_ends[None, :SEGS - 1]).astype(jnp.int32), axis=1))
    start_state = dec_row + tag_table[token_tags]
    start_low = low(start_state)
    projected = rounded_both(product(start_low, self_qkv))
    query_rows = projected[:, :model_width]
    key_rows = projected[:, model_width:2 * model_width]
    value_rows = projected[:, 2 * model_width:]
    mixed_rows = rounded_both(attention(query_rows, key_rows, value_rows, segment_row, segment_row, True))
    branch = low_back(product(mixed_rows, self_out))
    first_norm = layer_norm(start_state + branch, norm_gain[0], norm_bias[0])
    cross_q = rounded_both(product(low(first_norm), cross_query))
    cross_keys = rounded_both(product(enc_row, cross_kv))
    cross_mixed = rounded_both(attention(cross_q, cross_keys[:, :model_width], cross_keys[:, model_width:], segment_row, enc_segments, False))
    cross_branch = low_back(product(cross_mixed, cross_out))
    second_norm = layer_norm(first_norm + cross_branch, norm_gain[1], norm_bias[1])
    hidden_pre = low_back(product(low(second_norm), ffn_in) + ffn_in_bias)
    activated = low(jax.nn.gelu(hidden_pre, approximate=True))
    ffn_branch = low_back(product(activated, ffn_out) + ffn_out_bias)
    return layer_norm(second_norm + ffn_branch, norm_gain[2], norm_bias[2])

def reference(dec_input, encoded, segment_ids, pair_tags, enc_lengths, out_grad, tag_table, self_qkv, self_out, cross_query, cross_kv, cross_out, ffn_in, ffn_in_bias, ffn_out, ffn_out_bias, norm_gain, norm_bias):
    weights = tuple((weight.astype(jnp.float32) for weight in (tag_table, self_qkv, self_out, cross_query, cross_kv, cross_out, ffn_in, ffn_in_bias, ffn_out, ffn_out_bias, norm_gain, norm_bias)))

    def row_step(totals, row_slice):
        dec_row, enc_row, segment_row, tag_row, length_row, grad_row = row_slice
        floats = (dec_row.astype(jnp.float32), enc_row.astype(jnp.float32)) + weights
        output, pullback = jax.vjp(lambda packed: decoder_layer(packed, segment_row, tag_row, length_row), floats)
        gradients = pullback(grad_row.astype(jnp.float32))[0]
        totals = tuple((running + gradient for running, gradient in zip(totals, gradients[2:])))
        return (totals, (output.astype(jnp.bfloat16), gradients[0], gradients[1]))
    initial = tuple((jnp.zeros(weight.shape, jnp.float32) for weight in weights))
    totals, stacked = lax.scan(row_step, initial, (dec_input, encoded, segment_ids, pair_tags, enc_lengths, out_grad))
    return (stacked[0], stacked[1], stacked[2], totals[0], totals[1], totals[2], totals[3], totals[4], totals[5], totals[6], totals[7], totals[8], totals[9], totals[10], totals[11])
```

```python
import jax
import jax.numpy as jnp
from jax import lax
from jax.experimental import pallas as pl
from jax.experimental.pallas import tpu as pltpu
from jax.sharding import PartitionSpec as P

F32 = jnp.float32
BF = jnp.bfloat16
SEGS = 4
NTAGS = 16
BLK = 256
HALF = 128
BIG = -1e30
EPS = 1e-5
NT = (((1,), (1,)), ((), ()))
VM = pl.BlockSpec(memory_space=pltpu.VMEM)
SM = pl.BlockSpec(memory_space=pltpu.SMEM)


def build_blocks(src_ref, extra_ref, dst_ref):
    z = jnp.zeros((64, HALF), BF)
    for p in range(4):
        for h in range(2):
            c = slice(h * HALF, (h + 1) * HALF)
            dst_ref[2 * p + h, 0:64, :] = jnp.concatenate([src_ref[128 * p : 128 * p + 64, c], z], 1)
            dst_ref[2 * p + h, 64:128, :] = jnp.concatenate([z, src_ref[128 * p + 64 : 128 * p + 128, c]], 1)
            if extra_ref is not None:
                e = extra_ref[:, c]
                dst_ref[2 * p + h, 128:144, :] = jnp.concatenate([e, e], 1)
                dst_ref[2 * p + h, 144:256, :] = jnp.zeros((112, 256), BF)


def split_heads(j, a, o_ref):
    p, h = j // 2, j % 2
    o_ref[128 * p : 128 * p + 64, h * HALF : (h + 1) * HALF] = a[0:64, 0:HALF]
    o_ref[128 * p + 64 : 128 * p + 128, h * HALF : (h + 1) * HALF] = a[64:128, HALF:]


def cross_fwd_kernel(i_ref, q_ref, k_ref, vt_ref, khot_ref, qhot_ref, o_ref, lse_ref, qb):
    build_blocks(q_ref, qhot_ref, qb)
    size = 512
    tiles = k_ref.shape[0] // size
    for j in range(8):
        p = j // 2

        def scores(t):
            rows = pl.ds(t * size, size)
            kt = jnp.concatenate([k_ref[rows, 128 * p : 128 * p + 128], khot_ref[rows, :]], 1)
            return jnp.dot(kt, qb[j], preferred_element_type=F32)

        top = jnp.max(scores(0), axis=0, keepdims=True)
        for t in range(1, tiles):
            top = jnp.maximum(top, jnp.max(scores(t), axis=0, keepdims=True))
        total = jnp.zeros((1, 256), F32)
        acc = jnp.zeros((128, 256), F32)
        for t in range(tiles):
            e = jnp.exp(scores(t) - top)
            total = total + jnp.sum(e, axis=0, keepdims=True)
            vt = vt_ref[128 * p : 128 * p + 128, t * size : (t + 1) * size]
            acc = acc + jnp.dot(vt, e.astype(BF), preferred_element_type=F32)
        lse_ref[j] = top + jnp.log(total)
        split_heads(j, acc * (1.0 / total), o_ref)


def cross_bwd_kernel(
    i_ref, q_ref, k_ref, kt_ref, v_ref, khot_ref, qhot_ref, do_ref, lse_ref, dl_ref, dq_ref, dk_ref, dv_ref, qb, db
):
    build_blocks(q_ref, qhot_ref, qb)
    build_blocks(do_ref, None, db)
    size = min(2048, k_ref.shape[0])
    tiles = k_ref.shape[0] // size
    for p in range(4):
        lanes = slice(128 * p, 128 * p + 128)
        dq = [0.0, 0.0]
        for t in range(tiles):
            rows = slice(t * size, (t + 1) * size)
            kt = jnp.concatenate([k_ref[rows, lanes], khot_ref[rows, :]], 1)
            dk = dv = 0.0
            for h in range(2):
                j = 2 * p + h
                s = jnp.dot(kt, qb[j], preferred_element_type=F32)
                pr = jnp.exp(s - lse_ref[j])
                dp = jnp.dot(v_ref[rows, lanes], db[j], preferred_element_type=F32)
                ds = (pr * (dp - dl_ref[j])).astype(BF)
                dv += lax.dot_general(pr.astype(BF), db[j], NT, preferred_element_type=F32)
                dk += lax.dot_general(ds, qb[j, 0:128, :], NT, preferred_element_type=F32)
                dq[h] += jnp.dot(kt_ref[lanes, rows], ds, preferred_element_type=F32)
            dk_ref[rows, lanes] = dk.astype(BF)
            dv_ref[rows, lanes] = dv.astype(BF)
        for h in range(2):
            split_heads(2 * p + h, dq[h] * 0.125, dq_ref)


TILE = 512


def work_item(t, i, blocks):
    first = (i + 2) // 2
    second = (t >= first).astype(jnp.int32)
    tile = t - second * first
    start = jnp.where(second == 1, (blocks - 1 - i) * BLK + HALF, i * BLK)
    return second, tile, start - tile * TILE


def relative_positions(swap):
    k = lax.broadcasted_iota(jnp.int32, (TILE, 2 * HALF), 0)
    q = lax.broadcasted_iota(jnp.int32, (TILE, 2 * HALF), 1) & (HALF - 1)
    return (k ^ swap) - q


def self_fwd_kernel(blocks, i_ref, q_ref, k_ref, vt_ref, khot_ref, qhot_ref, o_ref, lse_ref, qb, m_s, l_s, acc):
    build_blocks(q_ref, qhot_ref, qb)
    i = i_ref[0]
    swap = (i & 1) * BLK
    items = blocks // 2 + 1
    m_s[...] = jnp.full(m_s.shape, -3e38, F32)
    l_s[...] = jnp.zeros(l_s.shape, F32)
    acc[...] = jnp.zeros(acc.shape, F32)

    def scores(t, p):
        h, tile, offset = work_item(t, i, blocks)
        r0 = pl.multiple_of((tile ^ (i >> 1)) * TILE, TILE)
        kt = jnp.concatenate([k_ref[pl.ds(r0, TILE), 128 * p : 128 * p + 128], khot_ref[pl.ds(r0, TILE), :]], 1)
        s = jnp.dot(kt, qb[2 * p + h], preferred_element_type=F32)
        return jnp.where(relative_positions(swap) <= offset, s, BIG), 2 * p + h, r0

    @pl.loop(0, items)
    def _(t):
        for p in range(4):
            s, j, _ = scores(t, p)
            m_s[j] = jnp.maximum(m_s[j], jnp.max(s, axis=0, keepdims=True))

    @pl.loop(0, items)
    def _(t):
        for p in range(4):
            s, j, r0 = scores(t, p)
            e = jnp.exp(s - m_s[j])
            l_s[j] += jnp.sum(e, axis=0, keepdims=True)
            vt = vt_ref[128 * p : 128 * p + 128, pl.ds(r0, TILE)]
            acc[j] += jnp.dot(vt, e.astype(BF), preferred_element_type=F32)

    for j in range(8):
        lse_ref[j] = m_s[j] + jnp.log(l_s[j])
        split_heads(j, acc[j] * (1.0 / l_s[j]), o_ref)


def self_bwd_kernel(
    blocks, i_ref, q_ref, k_ref, kt_ref, v_ref, khot_ref, qhot_ref, do_ref, lse_ref, dl_ref,
    dq_ref, dk_ref, dv_ref, qb, db, dqa, dka, dva,
):
    build_blocks(q_ref, qhot_ref, qb)
    build_blocks(do_ref, None, db)
    i = i_ref[0]
    swap = (i & 1) * BLK
    dqa[...] = jnp.zeros(dqa.shape, F32)
    dka[...] = jnp.zeros(dka.shape, F32)
    dva[...] = jnp.zeros(dva.shape, F32)

    @pl.loop(0, blocks // 2 + 1)
    def _(t):
        h, tile, offset = work_item(t, i, blocks)
        r0 = pl.multiple_of((tile ^ (i >> 1)) * TILE, TILE)
        rows = pl.ds(r0, TILE)
        hot = khot_ref[rows, :]
        for p in range(4):
            j = 2 * p + h
            lanes = slice(128 * p, 128 * p + 128)
            s = jnp.dot(jnp.concatenate([k_ref[rows, lanes], hot], 1), qb[j], preferred_element_type=F32)
            s = jnp.where(relative_positions(swap) <= offset, s, BIG)
            pr = jnp.exp(s - lse_ref[j])
            dp = jnp.dot(v_ref[rows, lanes], db[j], preferred_element_type=F32)
            ds = (pr * (dp - dl_ref[j])).astype(BF)
            dva[rows, lanes] += lax.dot_general(pr.astype(BF), db[j], NT, preferred_element_type=F32)
            dka[rows, lanes] += lax.dot_general(ds, qb[j, 0:128, :], NT, preferred_element_type=F32)
            dqa[j] += jnp.dot(kt_ref[lanes, rows], ds, preferred_element_type=F32)

    dk_ref[...] = dka[...].astype(BF)
    dv_ref[...] = dva[...].astype(BF)
    for j in range(8):
        split_heads(j, dqa[j] * 0.125, dq_ref)


def params(mib=56):
    return pltpu.CompilerParams(vmem_limit_bytes=mib << 20)


def shape(dims, dtype):
    return jax.ShapeDtypeStruct(dims, dtype)


def attend_forward(causal, i, qT, K, VT, khot, qhotT):
    S = K.shape[0]
    scratch = [pltpu.VMEM((8, 256, 256), BF)]
    kernel = cross_fwd_kernel
    if causal:
        scratch += [pltpu.VMEM((8, 1, 256), F32), pltpu.VMEM((8, 1, 256), F32), pltpu.VMEM((8, 128, 256), F32)]
        kernel = lambda *refs: self_fwd_kernel(S // BLK, *refs)
    work = S * 512 * (256 if causal else 512) * 4
    return pl.pallas_call(
        kernel,
        out_shape=(shape((512, 256), F32), shape((8, 1, 256), F32)),
        in_specs=[SM] + [VM] * 5,
        out_specs=(VM, VM),
        scratch_shapes=scratch,
        compiler_params=params(),
        cost_estimate=pl.CostEstimate(flops=2 * work, bytes_accessed=4 * S * 512, transcendentals=work // 256),
        name="self_forward" if causal else "cross_forward",
    )(i, qT, K, VT, khot, qhotT)


def attend_backward(causal, i, qT, K, KT, V, khot, qhotT, doT, lse, delta):
    S = K.shape[0]
    scratch = [pltpu.VMEM((8, 256, 256), BF), pltpu.VMEM((8, 128, 256), BF)]
    kernel = cross_bwd_kernel
    if causal:
        scratch += [pltpu.VMEM((8, 128, 256), F32), pltpu.VMEM((S, 512), F32), pltpu.VMEM((S, 512), F32)]
        kernel = lambda *refs: self_bwd_kernel(S // BLK, *refs)
    work = S * 512 * (256 if causal else 512) * 10
    return pl.pallas_call(
        kernel,
        out_shape=(shape((512, 256), F32), shape((S, 512), BF), shape((S, 512), BF)),
        in_specs=[SM] + [VM] * 9,
        out_specs=(VM, VM, VM),
        scratch_shapes=scratch,
        compiler_params=params(),
        cost_estimate=pl.CostEstimate(flops=2 * work, bytes_accessed=10 * S * 512, transcendentals=work // 512),
        name="self_backward" if causal else "cross_backward",
    )(i, qT, K, KT, V, khot, qhotT, doT, lse, delta)


def dot(a, b, dims=((1,), (0,))):
    return lax.dot_general(a, b, (dims, ((), ())), preferred_element_type=F32)


def exchange(x, axis, k):
    size = lax.axis_size(axis)
    return lax.ppermute(x, axis, [(i, i ^ k) for i in range(size)])


def gather(x):
    n = lax.axis_size("seq")
    parts = {0: x}
    for k in range(2, n, 2):
        parts[k] = exchange(x, "seq", k)
    for k in range(0, n, 2):
        parts[k + 1] = exchange(parts[k], "seq", 1)
    return [parts[k] for k in range(n)]


def total(terms):
    out = terms[0].astype(F32)
    for term in terms[1:]:
        out = out + term.astype(F32)
    return out


def scatter_sum(even, odd):
    got = exchange(odd, "seq", 1)
    mine = [(e.astype(F32) + got[j].astype(F32)).astype(BF) for j, e in enumerate(even)]
    return total([mine[0]] + [exchange(mine[j], "seq", 2 * j) for j in range(1, len(mine))])


def take(x, index):
    return lax.dynamic_index_in_dim(x, index, 0, keepdims=False)


def norm_forward(v, gain, bias):
    centered = v - jnp.mean(v, axis=-1, keepdims=True)
    scale = lax.rsqrt(jnp.mean(centered * centered, axis=-1, keepdims=True) + EPS)
    hat = centered * scale
    return hat * gain + bias, hat, scale


def norm_backward(g, hat, scale, gain):
    gh = g * gain
    out = scale * (gh - jnp.mean(gh, axis=-1, keepdims=True) - hat * jnp.mean(gh * hat, axis=-1, keepdims=True))
    return out, jnp.sum(g * hat, axis=0), jnp.sum(g, axis=0)


def gelu_both(x):
    c = 0.7978845608028654
    t = jnp.tanh(c * (x + 0.044715 * x * x * x))
    return 0.5 * x * (1 + t), 0.5 * (1 + t) + 0.5 * x * (1 - t * t) * c * (1 + 3 * 0.044715 * x * x)


def pair_rows(x):
    x = x.reshape(4, 2, 2, HALF).transpose(0, 2, 1, 3)
    return x.reshape(8, 1, 256)


def seg_bias(seg):
    ids = jnp.arange(16, dtype=jnp.int32)[:, None]
    return jnp.where((ids != seg[None]) & (ids < SEGS), BIG, 0.0).astype(BF)


def one_hot(seg):
    return (seg[:, None] == jnp.arange(128, dtype=jnp.int32)[None]).astype(BF)


def pack(grad, zsize, chips):
    R, C = grad.shape
    parts = grad.astype(BF).reshape(zsize, chips, R // (zsize * chips), 2, C // 512, 256)
    return parts.transpose(3, 1, 0, 4, 2, 5).reshape(2, chips, zsize, -1, 256)


def unpack(parts, R, C):
    chips = parts.shape[0]
    parts = parts.reshape(chips, 2, C // 512, R // chips, 256).transpose(0, 3, 1, 2, 4)
    return parts.reshape(R, C).astype(F32)


def reduce_weights(grads, small, me, zme):
    n, zsize = lax.axis_size("seq"), lax.axis_size("rows")
    chips = n // 2
    chip, core = me // 2, me % 2
    packed = jnp.concatenate([pack(g, zsize, chips) for g in grads], axis=3)
    even = [take(take(packed, core), chip ^ j) for j in range(chips)]
    other = take(packed, 1 - core)
    odd = jnp.stack([take(other, chip ^ j) for j in range(chips)])
    if small is not None:
        even = [jnp.concatenate([e, small], axis=1) for e in even]
        odd = jnp.concatenate([odd, jnp.broadcast_to(small[None], (chips,) + small.shape)], axis=2)
    summed = scatter_sum(even, odd).astype(BF)
    mine = total([take(summed, zme)] + [exchange(take(summed, zme ^ k), "rows", k) for k in range(1, zsize)])
    shards = jnp.stack(gather(mine.astype(BF)))
    rows = shards.shape[1]
    if small is not None:
        rows = rows - small.shape[1]
    places = jnp.arange(n, dtype=jnp.int32) ^ me
    whole = shards[places, :rows].reshape(chips, 2, rows, 256)
    outs, at = [], 0
    for g in grads:
        R, C = g.shape[0] // zsize, g.shape[1]
        size = R // chips * (C // 512)
        outs.append(unpack(whole[:, :, at : at + size], R, C))
        at += size
    return outs, None if small is None else mine[rows:]


def local(
    dec_input, encoded, segment_ids, pair_tags, enc_lengths, out_grad, tag_table, self_qkv, self_out, cross_query,
    cross_kv, cross_out, ffn_in, ffn_in_bias, ffn_out, ffn_out_bias, norm_gain, norm_bias,
):
    n, zsize = lax.axis_size("seq"), lax.axis_size("rows")
    me, zme = lax.axis_index("seq").astype(jnp.int32), lax.axis_index("rows").astype(jnp.int32)
    mirror = n - 1
    gain, bias = norm_gain.astype(F32), norm_bias.astype(F32)
    where = me[None]

    x_all = jnp.concatenate(gather(dec_input[0]))
    seg_parts = gather(segment_ids[0])
    enc_all = jnp.concatenate(gather(encoded[0]))
    S = x_all.shape[0]
    og = jnp.concatenate([out_grad[0, :HALF], exchange(out_grad[0, HALF:], "seq", mirror)]).astype(F32)

    def own(x):
        return jnp.concatenate([x[:HALF], x[S - HALF :]])

    khot = one_hot(jnp.concatenate(seg_parts))
    seg_q = jnp.concatenate([seg_parts[0][:HALF], seg_parts[-1][HALF:]])
    qhotT = seg_bias(seg_q)
    tag_hot = (pair_tags[0][:, None] == jnp.arange(NTAGS, dtype=jnp.int32)[None]).astype(BF)
    tag_rows = dot(tag_hot, tag_table).astype(BF)
    start_all = x_all.astype(F32) + dot(khot[:, :SEGS], tag_rows)
    low_all = start_all.astype(BF)
    start, start_low = own(start_all), own(low_all)
    wq, wk, wv = self_qkv[:, :512], self_qkv[:, 512:1024], self_qkv[:, 1024:]
    TT = ((0,), (1,))
    qT = dot(wq, start_low, TT).astype(BF) * BF(0.125)
    K, V = dot(low_all, wk).astype(BF), dot(low_all, wv).astype(BF)
    KT, VT = K.T, V.T
    oT, lse = attend_forward(True, where, qT, K, VT, khot, qhotT)
    mixedT = oT.astype(BF)
    first, hat1, scale1 = norm_forward(start + dot(mixedT, self_out, ((0,), (0,))), gain[0], bias[0])
    first_low = first.astype(BF)

    block = jnp.arange(S, dtype=jnp.int32) // BLK
    enc_pos = (block ^ me) * BLK + jnp.arange(S, dtype=jnp.int32) % BLK
    ends = jnp.cumsum(enc_lengths[0])
    ehot = one_hot(jnp.sum((enc_pos[:, None] >= ends[None, : SEGS - 1]).astype(jnp.int32), axis=1))
    ck, cv = cross_kv[:, :512], cross_kv[:, 512:]
    EK, EV = dot(enc_all, ck).astype(BF), dot(enc_all, cv).astype(BF)
    EKT, EVT = EK.T, EV.T
    cqT = dot(cross_query, first_low, TT).astype(BF) * BF(0.125)
    coT, clse = attend_forward(False, where, cqT, EK, EVT, ehot, qhotT)
    cmixT = coT.astype(BF)
    second, hat2, scale2 = norm_forward(first + dot(cmixT, cross_out, ((0,), (0,))), gain[1], bias[1])
    second_low = second.astype(BF)
    act, slope = gelu_both(dot(second_low, ffn_in) + ffn_in_bias.astype(F32))
    hidden = act.astype(BF)
    result, hat3, scale3 = norm_forward(
        second + dot(hidden, ffn_out) + ffn_out_bias.astype(F32), gain[2], bias[2]
    )
    low_out = result.astype(BF)
    layer_out = jnp.concatenate([low_out[:HALF], exchange(low_out[HALF:], "seq", mirror)])[None]

    g3, gg3, gb3 = norm_backward(og, hat3, scale3, gain[2])
    g_ffn = g3.astype(BF)
    d_out_bias = jnp.sum(g_ffn.astype(F32), axis=0)
    g_pre = (dot(g_ffn, ffn_out, ((1,), (1,))) * slope).astype(BF)
    d_in_bias = jnp.sum(g_pre.astype(F32), axis=0)
    TN = ((0,), (0,))
    ffn_grads, _ = reduce_weights([dot(second_low, g_pre, TN), dot(hidden, g_ffn, TN)], None, me, zme)
    g_mid, gg2, gb2 = norm_backward(g3 + dot(g_pre, ffn_in, ((1,), (1,))), hat2, scale2, gain[1])
    g_cb = g_mid.astype(BF)
    d_cross_out = dot(cmixT, g_cb)
    gcT = dot(cross_out, g_cb, ((1,), (1,))).astype(BF)
    delta = pair_rows(jnp.sum((gcT.astype(F32) * coT).reshape(8, 64, 256), axis=1))
    dqT, dk, dv = attend_backward(False, where, cqT, EK, EKT, EV, ehot, qhotT, gcT, clse, delta)
    enc_part = (dot(dk, ck, ((1,), (1,))) + dot(dv, cv, ((1,), (1,)))).astype(BF).reshape(n, BLK, 512)
    encoded_grad = scatter_sum([enc_part[k] for k in range(0, n, 2)], enc_part[1::2])[None]
    d_cross_kv = jnp.concatenate([dot(enc_all, dk, TN), dot(enc_all, dv, TN)], axis=1)
    dqT_low = dqT.astype(BF)
    d_cross_query = dot(first_low, dqT_low, ((0,), (1,)))
    g_start, gg1, gb1 = norm_backward(
        g_mid + dot(dqT_low, cross_query, ((0,), (1,))), hat1, scale1, gain[0]
    )
    g_branch = g_start.astype(BF)
    d_self_out = dot(mixedT, g_branch)
    cross_grads, _ = reduce_weights([d_cross_kv, d_cross_out, d_cross_query, d_self_out], None, me, zme)
    gmT = dot(self_out, g_branch, ((1,), (1,))).astype(BF)
    delta = pair_rows(jnp.sum((gmT.astype(F32) * oT).reshape(8, 64, 256), axis=1))
    dqT, dk, dv = attend_backward(True, where, qT, K, KT, V, khot, qhotT, gmT, lse, delta)
    dqT_low = dqT.astype(BF)
    mine = g_start + dot(dqT_low, wq, ((0,), (1,)))
    part = dot(dk, wk, ((1,), (1,))) + dot(dv, wv, ((1,), (1,)))
    part = jnp.concatenate([part[:HALF] + mine[:HALF], part[HALF : S - HALF], part[S - HALF :] + mine[HALF:]])
    part = part.astype(BF)
    seg_sums = dot(khot[:, :SEGS], part, TN)
    d_table = dot(tag_hot.astype(F32), seg_sums, TN)
    part = part.reshape(n, BLK, 512)
    input_grad = scatter_sum([part[k] for k in range(0, n, 2)], part[1::2])[None]
    d_qkv = jnp.concatenate(
        [dot(start_low, dqT_low, ((0,), (1,))), dot(low_all, dk, TN), dot(low_all, dv, TN)], axis=1
    )

    vectors = jnp.stack([gg1, gg2, gg3, gb1, gb2, gb3, d_out_bias])
    lanes = 512 // zsize
    small = jnp.concatenate(
        [
            d_table.reshape(zsize, -1),
            d_in_bias.reshape(zsize, -1),
            vectors.reshape(7, zsize, lanes).transpose(1, 0, 2).reshape(zsize, -1),
        ],
        axis=1,
    )
    small = jnp.pad(small, ((0, 0), (0, 4096 - small.shape[1]))).reshape(zsize, 16, 256).astype(BF)
    (g_qkv,), small = reduce_weights([d_qkv], small, me, zme)
    small = small.reshape(-1)
    tags, inner = NTAGS // zsize * 512, 2048 // zsize
    vectors = small[tags + inner : tags + inner + 7 * lanes].reshape(7, lanes)
    return (
        layer_out,
        input_grad,
        encoded_grad,
        small[:tags].reshape(-1, 512),
        g_qkv,
        cross_grads[3],
        cross_grads[2],
        cross_grads[0],
        cross_grads[1],
        ffn_grads[0],
        small[tags : tags + inner],
        ffn_grads[1],
        vectors[6],
        vectors[0:3],
        vectors[3:6],
    )


def solution(mesh):
    tokens = P("rows", "seq", None)
    placed = (tokens, tokens, P("rows", "seq"), P("rows", None), P("rows", None), tokens) + (P(),) * 12
    rows = P("rows", None)
    return jax.shard_map(
        local,
        mesh=mesh,
        in_specs=placed,
        out_specs=(tokens, tokens, tokens)
        + (rows,) * 7
        + (P("rows"), rows, P("rows"), P(None, "rows"), P(None, "rows")),
        check_vma=False,
    )
```

```python
import jax
import jax.numpy as jnp
from jax import lax
from jax.experimental import pallas as pl
from jax.experimental.pallas import tpu as pltpu
from jax.sharding import PartitionSpec as P

F32 = jnp.float32
BF = jnp.bfloat16
SEGS = 4
NTAGS = 16
BLK = 256
HALF = 128
BIG = -1e30
EPS = 1e-5
NT = (((1,), (1,)), ((), ()))
VM = pl.BlockSpec(memory_space=pltpu.VMEM)
SM = pl.BlockSpec(memory_space=pltpu.SMEM)


def build_blocks(src_ref, extra_ref, dst_ref):
    z = jnp.zeros((64, HALF), BF)
    for p in range(4):
        for h in range(2):
            c = slice(h * HALF, (h + 1) * HALF)
            dst_ref[2 * p + h, 0:64, :] = jnp.concatenate([src_ref[128 * p : 128 * p + 64, c], z], 1)
            dst_ref[2 * p + h, 64:128, :] = jnp.concatenate([z, src_ref[128 * p + 64 : 128 * p + 128, c]], 1)
            if extra_ref is not None:
                e = extra_ref[:, c]
                dst_ref[2 * p + h, 128:144, :] = jnp.concatenate([e, e], 1)
                dst_ref[2 * p + h, 144:256, :] = jnp.zeros((112, 256), BF)


def split_heads(j, a, o_ref):
    p, h = j // 2, j % 2
    o_ref[128 * p : 128 * p + 64, h * HALF : (h + 1) * HALF] = a[0:64, 0:HALF]
    o_ref[128 * p + 64 : 128 * p + 128, h * HALF : (h + 1) * HALF] = a[64:128, HALF:]


def cross_fwd_kernel(i_ref, q_ref, k_ref, vt_ref, khot_ref, qhot_ref, o_ref, lse_ref, qb):
    build_blocks(q_ref, qhot_ref, qb)
    size = 512
    tiles = k_ref.shape[0] // size
    for j in range(8):
        p = j // 2

        def scores(t):
            rows = pl.ds(t * size, size)
            kt = jnp.concatenate([k_ref[rows, 128 * p : 128 * p + 128], khot_ref[rows, :]], 1)
            return jnp.dot(kt, qb[j], preferred_element_type=F32)

        top = jnp.max(scores(0), axis=0, keepdims=True)
        for t in range(1, tiles):
            top = jnp.maximum(top, jnp.max(scores(t), axis=0, keepdims=True))
        total = jnp.zeros((1, 256), F32)
        acc = jnp.zeros((128, 256), F32)
        for t in range(tiles):
            e = jnp.exp(scores(t) - top)
            total = total + jnp.sum(e, axis=0, keepdims=True)
            vt = vt_ref[128 * p : 128 * p + 128, t * size : (t + 1) * size]
            acc = acc + jnp.dot(vt, e.astype(BF), preferred_element_type=F32)
        lse_ref[j] = top + jnp.log(total)
        split_heads(j, acc * (1.0 / total), o_ref)


def cross_bwd_kernel(
    copies, q_ref, k_ref, kt_ref, v_ref, khot_ref, qhot_ref, do_ref, lse_ref, dl_ref, dq_ref, dk_ref, dv_ref, qb, db
):
    build_blocks(q_ref, qhot_ref, qb)
    build_blocks(do_ref, None, db)
    size = min(2048, kt_ref.shape[1])
    tiles = kt_ref.shape[1] // size
    for p in range(4):
        lanes = slice(128 * p, 128 * p + 128)
        dq = [0.0, 0.0]
        for copy in copies[p]:
            copy.wait()
        for t in range(tiles):
            rows = slice(t * size, (t + 1) * size)
            blocks = slice(t * size // BLK, (t + 1) * size // BLK)
            kt = jnp.concatenate([k_ref[p, blocks].reshape(size, 128), khot_ref[rows, :]], 1)
            dk = dv = 0.0
            for h in range(2):
                j = 2 * p + h
                s = jnp.dot(kt, qb[j], preferred_element_type=F32)
                pr = jnp.exp(s - lse_ref[j])
                dp = jnp.dot(v_ref[p, blocks].reshape(size, 128), db[j], preferred_element_type=F32)
                ds = (pr * (dp - dl_ref[j])).astype(BF)
                dv += lax.dot_general(pr.astype(BF), db[j], NT, preferred_element_type=F32)
                dk += lax.dot_general(ds, qb[j, 0:128, :], NT, preferred_element_type=F32)
                dq[h] += jnp.dot(kt_ref[lanes, rows], ds, preferred_element_type=F32)
            dk_ref[rows, lanes] = dk.astype(BF)
            dv_ref[rows, lanes] = dv.astype(BF)
        for h in range(2):
            split_heads(2 * p + h, dq[h] * 0.125, dq_ref)


TILE = 512


def work_item(t, i, blocks):
    first = (i + 2) // 2
    second = (t >= first).astype(jnp.int32)
    tile = t - second * first
    start = jnp.where(second == 1, (blocks - 1 - i) * BLK + HALF, i * BLK)
    return second, tile, start - tile * TILE


def relative_positions(swap):
    k = lax.broadcasted_iota(jnp.int32, (TILE, 2 * HALF), 0)
    q = lax.broadcasted_iota(jnp.int32, (TILE, 2 * HALF), 1) & (HALF - 1)
    return (k ^ swap) - q


def self_fwd_kernel(blocks, i_ref, q_ref, k_ref, vt_ref, khot_ref, qhot_ref, o_ref, lse_ref, qb, m_s, l_s, acc):
    build_blocks(q_ref, qhot_ref, qb)
    i = i_ref[0]
    swap = (i & 1) * BLK
    items = blocks // 2 + 1
    m_s[...] = jnp.full(m_s.shape, -3e38, F32)
    l_s[...] = jnp.zeros(l_s.shape, F32)
    acc[...] = jnp.zeros(acc.shape, F32)

    def scores(t, p):
        h, tile, offset = work_item(t, i, blocks)
        r0 = pl.multiple_of((tile ^ (i >> 1)) * TILE, TILE)
        kt = jnp.concatenate([k_ref[pl.ds(r0, TILE), 128 * p : 128 * p + 128], khot_ref[pl.ds(r0, TILE), :]], 1)
        s = jnp.dot(kt, qb[2 * p + h], preferred_element_type=F32)
        return jnp.where(relative_positions(swap) <= offset, s, BIG), 2 * p + h, r0

    @pl.loop(0, items)
    def _(t):
        for p in range(4):
            s, j, _ = scores(t, p)
            m_s[j] = jnp.maximum(m_s[j], jnp.max(s, axis=0, keepdims=True))

    @pl.loop(0, items)
    def _(t):
        for p in range(4):
            s, j, r0 = scores(t, p)
            e = jnp.exp(s - m_s[j])
            l_s[j] += jnp.sum(e, axis=0, keepdims=True)
            vt = vt_ref[128 * p : 128 * p + 128, pl.ds(r0, TILE)]
            acc[j] += jnp.dot(vt, e.astype(BF), preferred_element_type=F32)

    for j in range(8):
        lse_ref[j] = m_s[j] + jnp.log(l_s[j])
        split_heads(j, acc[j] * (1.0 / l_s[j]), o_ref)


def self_bwd_kernel(
    blocks, i_ref, q_ref, k_ref, kt_ref, v_ref, khot_ref, qhot_ref, do_ref, lse_ref, dl_ref,
    dq_ref, dk_ref, dv_ref, qb, db, dqa, dka, dva,
):
    build_blocks(q_ref, qhot_ref, qb)
    build_blocks(do_ref, None, db)
    i = i_ref[0]
    swap = (i & 1) * BLK
    dqa[...] = jnp.zeros(dqa.shape, F32)
    dka[...] = jnp.zeros(dka.shape, F32)
    dva[...] = jnp.zeros(dva.shape, F32)

    @pl.loop(0, blocks // 2 + 1)
    def _(t):
        h, tile, offset = work_item(t, i, blocks)
        r0 = pl.multiple_of((tile ^ (i >> 1)) * TILE, TILE)
        rows = pl.ds(r0, TILE)
        hot = khot_ref[rows, :]
        for p in range(4):
            j = 2 * p + h
            lanes = slice(128 * p, 128 * p + 128)
            s = jnp.dot(jnp.concatenate([k_ref[rows, lanes], hot], 1), qb[j], preferred_element_type=F32)
            s = jnp.where(relative_positions(swap) <= offset, s, BIG)
            pr = jnp.exp(s - lse_ref[j])
            dp = jnp.dot(v_ref[rows, lanes], db[j], preferred_element_type=F32)
            ds = (pr * (dp - dl_ref[j])).astype(BF)
            dva[rows, lanes] += lax.dot_general(pr.astype(BF), db[j], NT, preferred_element_type=F32)
            dka[rows, lanes] += lax.dot_general(ds, qb[j, 0:128, :], NT, preferred_element_type=F32)
            dqa[j] += jnp.dot(kt_ref[lanes, rows], ds, preferred_element_type=F32)

    dk_ref[...] = dka[...].astype(BF)
    dv_ref[...] = dva[...].astype(BF)
    for j in range(8):
        split_heads(j, dqa[j] * 0.125, dq_ref)


ANY = pl.BlockSpec(memory_space=pl.ANY)
TOKEN = jax.ShapeDtypeStruct((8, 128), jnp.float32)


def params(mib):
    return pltpu.CompilerParams(vmem_limit_bytes=mib << 20)


def shape(dims, dtype):
    return jax.ShapeDtypeStruct(dims, dtype)


def cost(mults, size, exps=0):
    return pl.CostEstimate(flops=1, bytes_accessed=1, transcendentals=0)


def dot(a, b, dims=((1,), (0,))):
    return lax.dot_general(a, b, (dims, ((), ())), preferred_element_type=F32)


TN = ((0,), (0,))
NTD = ((1,), (1,))


def norm_forward(v, gain, bias):
    centered = v - jnp.mean(v, axis=-1, keepdims=True)
    scale = lax.rsqrt(jnp.mean(centered * centered, axis=-1, keepdims=True) + EPS)
    hat = centered * scale
    return hat * gain + bias, hat, scale


def norm_backward(g, hat, scale, gain):
    gh = g * gain
    out = scale * (gh - jnp.mean(gh, axis=-1, keepdims=True) - hat * jnp.mean(gh * hat, axis=-1, keepdims=True))
    return out, jnp.sum(g * hat, axis=0, keepdims=True), jnp.sum(g, axis=0, keepdims=True)


def gelu_both(x):
    c = 0.7978845608028654
    sq = x * x
    t = jnp.tanh(c * x * (1 + 0.044715 * sq))
    half = 0.5 * (1 + t)
    return x * half, half + 0.5 * x * (1 - t * t) * (c * (1 + 3 * 0.044715 * sq))


def inner_rows(g_refT, o_ref, dl_ref):
    for p in range(4):
        both = []
        for a in range(2):
            rows = slice(128 * p + 64 * a, 128 * p + 64 * a + 64)
            both.append(jnp.sum(g_refT[rows, :].astype(F32) * o_ref[rows, :], axis=0, keepdims=True))
        for h in range(2):
            cols = slice(h * HALF, (h + 1) * HALF)
            dl_ref[2 * p + h] = jnp.concatenate([both[0][:, cols], both[1][:, cols]], 1)


def join_tokens(x, seg):
    def kernel(x_ref, seg_ref, o_ref):
        o_ref[0:BLK, :] = x_ref[...]
        row = jnp.concatenate([seg_ref[...].astype(F32), jnp.zeros((1, 256), F32)], 1)
        o_ref[BLK:, :] = jnp.broadcast_to(row, (16, 512)).astype(BF)

    return pl.pallas_call(
        kernel,
        out_shape=shape((BLK + 16, 512), BF),
        in_specs=[VM, VM],
        out_specs=VM,
        compiler_params=params(60),
        cost_estimate=cost(0, 1 << 19),
        name="join_tokens",
    )(x, seg)


def join_blocks(a, b, *after):
    def kernel(a_ref, b_ref, *refs):
        refs[-1][0:BLK, :] = a_ref[...]
        refs[-1][BLK:, :] = b_ref[...]

    return pl.pallas_call(
        kernel,
        out_shape=shape((2 * BLK, 512), BF),
        in_specs=[VM, VM] + [ANY] * len(after),
        out_specs=VM,
        compiler_params=params(60),
        cost_estimate=cost(0, 1 << 19),
        name="join_blocks",
    )(a, b, *after)


def self_front_kernel(n, me_ref, tag_ref, *refs):
    xs, refs = refs[:n], refs[n:]
    segs = [x[BLK : BLK + 8, 0:BLK].astype(F32)[0:1].astype(jnp.int32) for x in xs]
    (table_ref, w_ref, wT_ref, so_ref, cqwT_ref, gain_ref, bias_ref,
     low_ref, k_ref, v_ref, kt_ref, khot_ref, qhot_ref, qT_ref, oT_ref, lse_ref, hat_ref, scale_ref, first_ref, cqT_ref,
     mixT_ref, slow_ref, low_s, k_s, v_s, kt_s, khot_s, vt_s, start_s, qb, m_s, l_s, acc, sems) = refs
    table = table_ref[...].astype(F32)
    ids = lax.broadcasted_iota(jnp.int32, (NTAGS, 512), 0)
    rows = [jnp.sum(jnp.where(ids == tag_ref[s], table, 0.0), axis=0, keepdims=True) for s in range(SEGS)]
    tag_rows = jnp.concatenate(rows + [jnp.zeros((4, 512), F32)], 0)
    copies = [
        pltpu.make_async_copy(a, b, sems.at[j])
        for j, (a, b) in enumerate(
            [(low_s, low_ref), (k_s, k_ref), (v_s, v_ref), (kt_s, kt_ref), (khot_s, khot_ref)]
        )
    ]
    for r in range(n):
        at = slice(r * BLK, (r + 1) * BLK)
        seg = segs[r]
        hotT = (lax.broadcasted_iota(jnp.int32, (128, BLK), 0) == seg).astype(F32)
        hot = hotT.T
        khot_s[at, :] = hot.astype(BF)
        start = xs[r][0:BLK, :].astype(F32)
        for s in range(SEGS):
            start = start + hot[:, s : s + 1] * tag_rows[s : s + 1, :]
        low = start.astype(BF)
        low_s[at, :] = low
        if r == 0:
            start_s[0:HALF, :] = start[0:HALF]
        if r == n - 1:
            start_s[HALF:, :] = start[HALF:]
        k_s[at, :] = dot(low, w_ref[:, 512:1024]).astype(BF)
        v_s[at, :] = dot(low, w_ref[:, 1024:1536]).astype(BF)
        kt_s[:, at] = dot(wT_ref[512:1024, :], low, NTD).astype(BF)
        vt_s[:, at] = dot(wT_ref[1024:1536, :], low, NTD).astype(BF)
    for copy in copies:
        copy.start()
    seg = jnp.concatenate([segs[0][:, 0:HALF], segs[n - 1][:, HALF:]], 1)
    ids = lax.broadcasted_iota(jnp.int32, (16, BLK), 0)
    qhot_ref[...] = jnp.where((ids != seg) & (ids < SEGS), BIG, 0.0).astype(BF)
    slow = start_s[...].astype(BF)
    slow_ref[...] = slow
    qT_ref[...] = (dot(wT_ref[0:512, :], slow, NTD).astype(BF) * 0.125).astype(BF)
    self_fwd_kernel(n, me_ref, qT_ref, k_s, vt_s, khot_s, qhot_ref, oT_ref, lse_ref, qb, m_s, l_s, acc)
    mixT = oT_ref[...].astype(BF)
    mixT_ref[...] = mixT
    branch = dot(mixT, so_ref[...], TN)
    first, hat, scale = norm_forward(
        start_s[...] + branch, gain_ref[0:1, :].astype(F32), bias_ref[0:1, :].astype(F32)
    )
    hat_ref[...] = hat
    scale_ref[...] = jnp.broadcast_to(scale, (BLK, 128))
    first_ref[...] = first
    cqT_ref[...] = (dot(cqwT_ref[...], first.astype(BF), NTD).astype(BF) * 0.125).astype(BF)
    for copy in copies:
        copy.wait()


def self_front(me, tags, xs, table, w, wT, so, cqwT, gain, bias):
    n = len(xs)
    S = n * BLK
    outs = (
        shape((S, 512), BF), shape((S, 512), BF), shape((S, 512), BF), shape((512, S), BF), shape((S, 128), BF),
        shape((16, BLK), BF), shape((512, BLK), BF), shape((512, BLK), F32), shape((8, 1, BLK), F32),
        shape((BLK, 512), F32), shape((BLK, 128), F32), shape((BLK, 512), F32), shape((512, BLK), BF),
        shape((512, BLK), BF), shape((BLK, 512), BF),
    )
    scratch = [
        pltpu.VMEM((S, 512), BF), pltpu.VMEM((S, 512), BF), pltpu.VMEM((S, 512), BF), pltpu.VMEM((512, S), BF),
        pltpu.VMEM((S, 128), BF), pltpu.VMEM((512, S), BF), pltpu.VMEM((BLK, 512), F32),
        pltpu.VMEM((8, 256, 256), BF), pltpu.VMEM((8, 1, 256), F32), pltpu.VMEM((8, 1, 256), F32),
        pltpu.VMEM((8, 128, 256), F32), pltpu.SemaphoreType.DMA((5,)),
    ]
    work = S * 512 * 512 * 5 + S * 512 * 256 * 4
    return pl.pallas_call(
        lambda *refs: self_front_kernel(n, *refs),
        out_shape=outs,
        in_specs=[SM, SM] + [VM] * (n + 7),
        out_specs=(ANY,) * 5 + (VM,) * 10,
        scratch_shapes=scratch,
        compiler_params=params(60),
        cost_estimate=cost(work, 16 * S * 512, S * 2048),
        name="self_front",
    )(me, tags, *xs, table, w, wT, so, cqwT, gain, bias)


def middle_kernel(n, me_ref, len_ref, *refs):
    encs, refs = refs[: n // 2], refs[n // 2 :]
    (w_ref, wT_ref, cqT_ref, qhot_ref, first_ref, co_ref, fi_ref, fo_ref, bi_ref, bo_ref, gain_ref, bias_ref,
     oga_ref, ogb_ref,
     la_ref, lb_ref, hid_ref, slow_ref, gffn_ref, gpre_ref, gmid_ref, gcT_ref, dl_ref, lse_ref, cmixT_ref, vec_ref,
     dib_ref, khot_ref,
     k_s, vt_s, oT_s, slope_s, qb) = refs
    me = me_ref[0]
    e0 = len_ref[0]
    e1 = e0 + len_ref[1]
    e2 = e1 + len_ref[2]
    for r in range(n):
        at = slice(r * BLK, (r + 1) * BLK)
        pos = lax.broadcasted_iota(jnp.int32, (BLK, 128), 0) + (me ^ r) * BLK
        seg = (pos >= e0).astype(jnp.int32) + (pos >= e1).astype(jnp.int32) + (pos >= e2).astype(jnp.int32)
        khot_ref[at, :] = (lax.broadcasted_iota(jnp.int32, (BLK, 128), 1) == seg).astype(F32).astype(BF)
        enc = encs[r // 2][BLK * (r % 2) : BLK * (r % 2) + BLK, :]
        k_s[at, :] = dot(enc, w_ref[:, 0:512]).astype(BF)
        vt_s[:, at] = dot(wT_ref[512:1024, :], enc, NTD).astype(BF)
    cross_fwd_kernel(me_ref, cqT_ref, k_s, vt_s, khot_ref, qhot_ref, oT_s, lse_ref, qb)
    cmixT = oT_s[...].astype(BF)
    cmixT_ref[...] = cmixT
    gains = [gain_ref[j : j + 1, :].astype(F32) for j in range(3)]
    shifts = [bias_ref[j : j + 1, :].astype(F32) for j in range(3)]
    second, hat2, scale2 = norm_forward(first_ref[...] + dot(cmixT, co_ref[...], TN), gains[1], shifts[1])
    second_low = second.astype(BF)
    slow_ref[...] = second_low
    out = second + bo_ref[...].astype(F32)
    for c in range(4):
        cols = slice(512 * c, 512 * c + 512)
        act, slope = gelu_both(dot(second_low, fi_ref[:, cols]) + bi_ref[:, cols].astype(F32))
        hidden = act.astype(BF)
        hid_ref[:, cols] = hidden
        slope_s[:, cols] = slope
        out = out + dot(hidden, fo_ref[cols, :])
    result, hat3, scale3 = norm_forward(out, gains[2], shifts[2])
    la_ref[...] = result[0:HALF].astype(BF)
    lb_ref[...] = result[HALF:].astype(BF)
    og = jnp.concatenate([oga_ref[...], ogb_ref[...]], 0).astype(F32)
    g3, gg3, gb3 = norm_backward(og, hat3, scale3, gains[2])
    g_ffn = g3.astype(BF)
    gffn_ref[...] = g_ffn
    d_out_bias = jnp.sum(g_ffn.astype(F32), axis=0, keepdims=True)
    g2 = g3
    for c in range(4):
        cols = slice(512 * c, 512 * c + 512)
        g_pre = (dot(g_ffn, fo_ref[cols, :], NTD) * slope_s[:, cols]).astype(BF)
        gpre_ref[:, cols] = g_pre
        dib_ref[:, cols] = jnp.sum(g_pre.astype(F32), axis=0, keepdims=True)
        g2 = g2 + dot(g_pre, fi_ref[:, cols], NTD)
    g_mid, gg2, gb2 = norm_backward(g2, hat2, scale2, gains[1])
    gmid_ref[...] = g_mid
    gcT_ref[...] = dot(co_ref[...], g_mid.astype(BF), NTD).astype(BF)
    inner_rows(gcT_ref, oT_s, dl_ref)
    vec_ref[...] = jnp.concatenate([gg2, gb2, gg3, gb3, d_out_bias, jnp.zeros((3, 512), F32)], 0)


def middle(me, lens, encs, w, wT, cqT, qhotT, first, co, fi, fo, bi, bo, gain, bias, oga, ogb):
    n = 2 * len(encs)
    S = n * BLK
    outs = (
        shape((HALF, 512), BF), shape((HALF, 512), BF), shape((BLK, 2048), BF), shape((BLK, 512), BF),
        shape((BLK, 512), BF), shape((BLK, 2048), BF), shape((BLK, 512), F32), shape((512, BLK), BF),
        shape((8, 1, 256), F32), shape((8, 1, 256), F32), shape((512, BLK), BF), shape((8, 512), F32),
        shape((1, 2048), F32), shape((S, 128), BF),
    )
    scratch = [
        pltpu.VMEM((S, 512), BF), pltpu.VMEM((512, S), BF), pltpu.VMEM((512, BLK), F32),
        pltpu.VMEM((BLK, 2048), F32), pltpu.VMEM((8, 256, 256), BF),
    ]
    work = S * 512 * 512 * 2 + S * 512 * 512 * 4 + 256 * 512 * 2048 * 4
    return pl.pallas_call(
        lambda *refs: middle_kernel(n, *refs),
        out_shape=outs,
        in_specs=[SM, SM] + [VM] * (n // 2 + 14),
        out_specs=(VM,) * len(outs),
        scratch_shapes=scratch,
        compiler_params=params(60),
        cost_estimate=cost(work, 16 * S * 512, S * 2048),
        name="middle",
    )(me, lens, *encs, w, wT, cqT, qhotT, first, co, fi, fo, bi, bo, gain, bias, oga, ogb)


def cross_project_kernel(n, *refs):
    encs, (w_ref, wT_ref, _, k_ref, v_ref, kt_ref, all_ref, token_ref, k_s, v_s, kt_s, sems) = refs[: n // 2], refs[n // 2 :]
    copies = []
    for r in range(n // 2):
        at = slice(2 * r * BLK, 2 * (r + 1) * BLK)
        copies.append(pltpu.make_async_copy(encs[r], all_ref.at[at, :], sems.at[3, r]))
        copies[-1].start()
    for r in range(n):
        at = slice(r * BLK, (r + 1) * BLK)
        enc = encs[r // 2][BLK * (r % 2) : BLK * (r % 2) + BLK, :]
        k, v = dot(enc, w_ref[:, 0:512]).astype(BF), dot(enc, w_ref[:, 512:1024]).astype(BF)
        for p in range(4):
            k_s[r, p] = k[:, 128 * p : 128 * p + 128]
            v_s[r, p] = v[:, 128 * p : 128 * p + 128]
        kt_s[:, at] = dot(wT_ref[0:512, :], enc, NTD).astype(BF)
        for j, (a, b) in enumerate(
            ((k_s.at[r], k_ref.at[r]), (v_s.at[r], v_ref.at[r]), (kt_s.at[:, at], kt_ref.at[:, at]))
        ):
            copies.append(pltpu.make_async_copy(a, b, sems.at[j, r]))
            copies[-1].start()
    token_ref[...] = jnp.zeros(token_ref.shape, F32)
    for copy in copies:
        copy.wait()


def cross_project(encs, w, wT, token):
    n = 2 * len(encs)
    S = n * BLK
    return pl.pallas_call(
        lambda *refs: cross_project_kernel(n, *refs),
        out_shape=(
            shape((n, 4, BLK, 128), BF), shape((n, 4, BLK, 128), BF), shape((512, S), BF), shape((S, 512), BF), TOKEN,
        ),
        in_specs=[VM] * (n // 2 + 2) + [ANY],
        out_specs=(ANY,) * 4 + (VM,),
        scratch_shapes=[
            pltpu.VMEM((n, 4, BLK, 128), BF), pltpu.VMEM((n, 4, BLK, 128), BF), pltpu.VMEM((512, S), BF),
            pltpu.SemaphoreType.DMA((4, n)),
        ],
        compiler_params=params(60),
        cost_estimate=cost(S * 512 * 512 * 3, 12 * S * 512),
        name="cross_project",
    )(*encs, w, wT, token)


def cross_back_kernel(n, me_ref, *refs):
    (k_hbm, v_hbm, kt_hbm, _, w_ref, cqT_ref, khot_ref, qhot_ref, gcT_ref, lse_ref, dl_ref, gmid_ref, cqwT_ref, hat_ref, scale_ref,
     gain_ref, so_ref, oT_ref, *refs) = refs
    half = n // 2
    evens, (odd_ref, dk_ref, dv_ref, dq_ref, gstart_ref, gbr_ref, gmT_ref, dl1_ref, vec_ref,
            k_s, kt_s, v_s, dqT_s, qb, db, sems) = refs[:half], refs[half:]
    copies = []
    for p in range(4):
        lanes = slice(128 * p, 128 * p + 128)
        copies.append([
            pltpu.make_async_copy(k_hbm.at[:, p], k_s.at[p], sems.at[3 * p]),
            pltpu.make_async_copy(v_hbm.at[:, p], v_s.at[p], sems.at[3 * p + 1]),
            pltpu.make_async_copy(kt_hbm.at[lanes, :], kt_s.at[lanes, :], sems.at[3 * p + 2]),
        ])
        for copy in copies[p]:
            copy.start()
    cross_bwd_kernel(
        copies, cqT_ref, k_s, kt_s, v_s, khot_ref, qhot_ref, gcT_ref, lse_ref, dl_ref, dqT_s, dk_ref, dv_ref, qb, db
    )
    for r in range(n):
        at = slice(r * BLK, (r + 1) * BLK)
        part = dot(dk_ref[at, :], w_ref[:, 0:512], NTD) + dot(dv_ref[at, :], w_ref[:, 512:1024], NTD)
        if r % 2:
            odd_ref[r // 2] = part.astype(BF)
        else:
            evens[r // 2][...] = part.astype(BF)
    dqT = dqT_s[...]
    dq_ref[...] = dqT.T.astype(BF)
    g1 = gmid_ref[...] + dot(dqT.astype(BF), cqwT_ref[...], TN)
    g_start, gg1, gb1 = norm_backward(g1, hat_ref[...], scale_ref[:, 0:1], gain_ref[0:1, :].astype(F32))
    gstart_ref[...] = g_start
    g_branch = g_start.astype(BF)
    gbr_ref[...] = g_branch
    gmT_ref[...] = dot(so_ref[...], g_branch, NTD).astype(BF)
    inner_rows(gmT_ref, oT_ref, dl1_ref)
    vec_ref[...] = jnp.concatenate([gg1, gb1, jnp.zeros((6, 512), F32)], 0)


def cross_back(me, k, v, kt, token, w, cqT, khot, qhotT, gcT, lse, dl, gmid, cqwT, hat, scale, gain, so, oT):
    S = khot.shape[0]
    n = S // BLK
    outs = (shape((BLK, 512), BF),) * (n // 2) + (
        shape((n // 2, BLK, 512), BF), shape((S, 512), BF), shape((S, 512), BF), shape((BLK, 512), BF),
        shape((BLK, 512), F32), shape((BLK, 512), BF), shape((512, BLK), BF), shape((8, 1, 256), F32),
        shape((8, 512), F32),
    )
    scratch = [
        pltpu.VMEM((4, n, BLK, 128), BF), pltpu.VMEM((512, S), BF), pltpu.VMEM((4, n, BLK, 128), BF), pltpu.VMEM((512, BLK), F32),
        pltpu.VMEM((8, 256, 256), BF), pltpu.VMEM((8, 128, 256), BF), pltpu.SemaphoreType.DMA((12,)),
    ]
    work = S * 512 * 512 * 2 + S * 512 * 512 * 10
    got = pl.pallas_call(
        lambda *refs: cross_back_kernel(n, *refs),
        out_shape=outs,
        in_specs=[SM] + [ANY] * 4 + [VM] * 14,
        out_specs=(VM,) * len(outs),
        scratch_shapes=scratch,
        compiler_params=params(60),
        cost_estimate=cost(work, 16 * S * 512, S * 2048),
        name="cross_back",
    )(me, k, v, kt, token, w, cqT, khot, qhotT, gcT, lse, dl, gmid, cqwT, hat, scale, gain, so, oT)
    return got[: n // 2], got[n // 2 :]


def self_back_kernel(n, me_ref, *refs):
    (_, qT_ref, k_ref, kt_ref, v_ref, khot_ref, qhot_ref, gmT_ref, lse_ref, dl_ref, w_ref, wT_ref, gstart_ref,
     *refs) = refs
    half = n // 2
    evens, (odd_ref, dk_ref, dv_ref, dq_ref, sums_ref, dqT_s, qb, db, dqa, dka, dva) = refs[:half], refs[half:]
    self_bwd_kernel(
        n, me_ref, qT_ref, k_ref, kt_ref, v_ref, khot_ref, qhot_ref, gmT_ref, lse_ref, dl_ref,
        dqT_s, dk_ref, dv_ref, qb, db, dqa, dka, dva,
    )
    dqT = dqT_s[...]
    dq_ref[...] = dqT.T.astype(BF)
    mine = gstart_ref[...] + dot(dqT.astype(BF), wT_ref[0:512, :], TN)
    sums = jnp.zeros((128, 512), F32)
    for r in range(n):
        at = slice(r * BLK, (r + 1) * BLK)
        part = dot(dk_ref[at, :], w_ref[:, 512:1024], NTD) + dot(dv_ref[at, :], w_ref[:, 1024:1536], NTD)
        if r == 0:
            part = jnp.concatenate([part[:HALF] + mine[:HALF], part[HALF:]], 0)
        if r == n - 1:
            part = jnp.concatenate([part[:HALF], part[HALF:] + mine[HALF:]], 0)
        part = part.astype(BF)
        sums = sums + dot(khot_ref[at, :], part, TN)
        if r % 2:
            odd_ref[r // 2] = part
        else:
            evens[r // 2][...] = part
    sums_ref[...] = sums[0:8, :]


def self_back(me, token, qT, K, KT, V, khot, qhotT, gmT, lse, dl, w, wT, gstart):
    S = K.shape[0]
    n = S // BLK
    outs = (shape((BLK, 512), BF),) * (n // 2) + (
        shape((n // 2, BLK, 512), BF), shape((S, 512), BF), shape((S, 512), BF), shape((BLK, 512), BF),
        shape((8, 512), F32),
    )
    scratch = [
        pltpu.VMEM((512, BLK), F32), pltpu.VMEM((8, 256, 256), BF), pltpu.VMEM((8, 128, 256), BF),
        pltpu.VMEM((8, 128, 256), F32), pltpu.VMEM((S, 512), F32), pltpu.VMEM((S, 512), F32),
    ]
    work = S * 512 * 512 * 2 + S * 512 * 256 * 10
    got = pl.pallas_call(
        lambda *refs: self_back_kernel(n, *refs),
        out_shape=outs,
        in_specs=[SM, ANY] + [VM] * 12,
        out_specs=(VM,) * len(outs),
        scratch_shapes=scratch,
        compiler_params=params(60),
        cost_estimate=cost(work, 16 * S * 512, S * 1024),
        name="self_back",
    )(me, token, qT, K, KT, V, khot, qhotT, gmT, lse, dl, w, wT, gstart)
    return got[: n // 2], got[n // 2 :]


def weight_kernel(specs, zsize, chips, me_ref, *refs):
    count = len(specs)
    pairs = [(refs[2 * j], refs[2 * j + 1]) for j in range(count)]
    refs = refs[2 * count + 1 :]
    evens, odd_ref, token_ref, stage = refs[:chips], refs[chips], refs[chips + 1], refs[chips + 2 :]
    token_ref[...] = jnp.zeros(token_ref.shape, F32)
    me = me_ref[0]
    core, chip = me & 1, me >> 1
    for turn in range(2):
        side = core if turn == 0 else 1 - core
        base = 0
        for (turned, R, C), (left, right), keep in zip(specs, pairs, stage):
            half = C // 2
            cols = pl.ds(pl.multiple_of(side * half, half), half)
            for at in range(0, R, 512):
                a = left[at : at + 512, :] if turned else left[:, at : at + 512]
                keep[at : at + 512, :] = dot(a, right[:, cols], ((1,) if turned else (0,), (0,))).astype(BF)
            size = R // (zsize * chips)
            for j in range(chips):
                for z in range(zsize):
                    row = pl.multiple_of(z * (R // zsize) + (chip ^ j) * size, size)
                    for c in range(half // 256):
                        piece = keep[pl.ds(row, size), 256 * c : 256 * c + 256]
                        to = slice(base + c * size, base + (c + 1) * size)
                        if turn == 0:
                            evens[j][z, to, :] = piece
                        else:
                            odd_ref[j, z, to, :] = piece
            base += size * (half // 256)


def weight_terms(me, zsize, chips, pairs, token):
    specs, rows, work = [], 0, 0
    for left, right, turned in pairs:
        R, C = left.shape[0 if turned else 1], right.shape[1]
        specs.append((turned, R, C))
        rows += R * C // (zsize * chips * 512)
        work += R * C * right.shape[0]
    got = pl.pallas_call(
        lambda *refs: weight_kernel(specs, zsize, chips, *refs),
        out_shape=(shape((zsize, rows, 256), BF),) * chips + (shape((chips, zsize, rows, 256), BF), TOKEN),
        in_specs=[SM] + [VM] * (2 * len(pairs)) + [ANY],
        out_specs=(VM,) * (chips + 2),
        scratch_shapes=[pltpu.VMEM((R, C // 2), BF) for _, R, C in specs],
        compiler_params=params(60),
        cost_estimate=cost(work, 2 * rows * 256 * zsize * chips * 4),
        name="weight_terms",
    )(me, *[x for left, right, _ in pairs for x in (left, right)], token)
    return got[:chips], got[chips], got[chips + 1]


def add_core(groups, token):
    count = len(groups[0][0])
    flat = [x for even, got in groups for x in (*even, got)]
    rows = sum(even[0].size // 256 for even, _ in groups)

    def kernel(*refs):
        outs, token_ref = refs[len(flat) + 1 : -1], refs[-1]
        token_ref[...] = jnp.zeros(token_ref.shape, F32)
        for j in range(count):
            base = 0
            for g in range(len(groups)):
                even, got = refs[g * (count + 1) + j], refs[g * (count + 1) + count]
                if len(even.shape) == 2:
                    both = (even[...].astype(F32) + got[j].astype(F32)).astype(BF)
                    for c in range(even.shape[1] // 256):
                        outs[j][base : base + even.shape[0], :] = both[:, 256 * c : 256 * c + 256]
                        base += even.shape[0]
                else:
                    for z in range(even.shape[0]):
                        both = (even[z].astype(F32) + got[j, z].astype(F32)).astype(BF)
                        outs[j][base : base + even.shape[1], :] = both
                        base += even.shape[1]

    got = pl.pallas_call(
        kernel,
        out_shape=(shape((rows, 256), BF),) * count + (TOKEN,),
        in_specs=[VM] * len(flat) + [ANY],
        out_specs=(VM,) * (count + 1),
        compiler_params=params(60),
        cost_estimate=cost(0, 6 * rows * 256 * count),
        name="add_core",
    )(*flat, token)
    return got[:count], got[count]


def add_chips(zme, terms, zsize, tokens, after):
    rows = terms[0].shape[0]
    first = 512 if tokens else 0
    size = (rows - first) // zsize
    count = len(terms)

    def kernel(z_ref, *refs):
        outs = refs[count + 1 :]
        outs[-1][...] = jnp.zeros(outs[-1].shape, F32)
        for k in range(zsize):
            row = pl.multiple_of(first + (z_ref[0] ^ k) * size, 16)
            outs[k][...] = total([refs[j][pl.ds(row, size), :] for j in range(count)]).astype(BF)
        if tokens:
            for c in range(2):
                part = total([refs[j][BLK * c : BLK * c + BLK, :] for j in range(count)])
                outs[zsize][:, 256 * c : 256 * c + 256] = part

    got = pl.pallas_call(
        kernel,
        out_shape=(shape((size, 256), BF),) * zsize + (shape((BLK, 512), F32),) * tokens + (TOKEN,),
        in_specs=[SM] + [VM] * count + [ANY],
        out_specs=(VM,) * (zsize + tokens + 1),
        compiler_params=params(60),
        cost_estimate=cost(0, 10 * terms[0].size),
        name="add_chips",
    )(zme, *terms, after)
    return got[:zsize], got[zsize], got[-1]


def unpack_kernel(layout, n, me_ref, *refs):
    shards, outs = refs[:n], refs[n:]
    me = me_ref[0]
    chips = n // 2
    for k in range(n):
        chip, core = (me >> 1) ^ (k >> 1), (me & 1) ^ (k & 1)
        for out, R, left, C, at in layout:
            size, half = R // chips, C // 2
            row = pl.multiple_of(chip * size, size)
            for c in range(half // 256):
                col = pl.multiple_of(left + core * half + 256 * c, 256)
                value = shards[k][at + c * size : at + (c + 1) * size, :].astype(F32)
                outs[out][pl.ds(row, size), pl.ds(col, 256)] = value


def unpack_shards(me, shards, shapes, layout):
    n = len(shards)
    return pl.pallas_call(
        lambda *refs: unpack_kernel(layout, n, *refs),
        out_shape=tuple(shape(s, F32) for s in shapes),
        in_specs=[SM] + [VM] * n,
        out_specs=(VM,) * len(shapes),
        compiler_params=params(60),
        cost_estimate=cost(0, 3 * n * shards[0].size * 2),
        name="unpack_shards",
    )(me, *shards)


def exchange(x, axis, k):
    size = lax.axis_size(axis)
    return lax.ppermute(x, axis, [(i, i ^ k) for i in range(size)])


def gather(x):
    n = lax.axis_size("seq")
    parts = {0: x}
    for k in range(2, n, 2):
        parts[k] = exchange(x, "seq", k)
    for k in range(0, n, 2):
        parts[k + 1] = exchange(parts[k], "seq", 1)
    return [parts[k] for k in range(n)]


def total(terms):
    out = terms[0].astype(F32)
    for term in terms[1:]:
        out = out + term.astype(F32)
    return out


def across_chips(mine):
    return [mine[0]] + [exchange(mine[j], "seq", 2 * j) for j in range(1, len(mine))]


def plain_weights(pairs, small):
    zsize = lax.axis_size("rows")
    zme = lax.axis_index("rows")
    outs = []
    for left, right, turned in pairs:
        whole = lax.psum(dot(left, right, ((1,) if turned else (0,), (0,))), ("seq", "rows"))
        size = whole.shape[0] // zsize
        outs.append(lax.dynamic_slice_in_dim(whole, zme * size, size, 0))
    small = lax.psum(small, ("seq", "rows"))
    return outs, lax.dynamic_index_in_dim(small, zme, 0, keepdims=False).reshape(-1)


def local(
    dec_input, encoded, segment_ids, pair_tags, enc_lengths, out_grad, tag_table, self_qkv, self_out, cross_query,
    cross_kv, cross_out, ffn_in, ffn_in_bias, ffn_out, ffn_out_bias, norm_gain, norm_bias,
):
    n, zsize = lax.axis_size("seq"), lax.axis_size("rows")
    chips = n // 2
    me, zme = lax.axis_index("seq").astype(jnp.int32)[None], lax.axis_index("rows").astype(jnp.int32)[None]
    mirror = n - 1
    cut = 512 // (zsize * chips) >= 16

    xs = gather(join_tokens(dec_input[0], segment_ids))
    both = join_blocks(encoded[0], exchange(encoded[0], "seq", 1), *xs[2::2])
    encs = [both] + [exchange(both, "seq", k) for k in range(2, n, 2)]
    oga, ogb = out_grad[0, :HALF], exchange(out_grad[0, HALF:], "seq", mirror)
    qkvT, ckvT, cqwT = self_qkv.T, cross_kv.T, cross_query.T

    (low_all, K, V, KT, khot, qhotT, qT, oT, lse, hat1, scale1, first, cqT, mixT, start_low) = self_front(
        me, pair_tags[0], xs, tag_table, self_qkv, qkvT, self_out, cqwT, norm_gain, norm_bias
    )
    (la, lb, hidden, second_low, g_ffn, g_pre, g_mid, gcT, cdelta, clse, cmixT, vec2, d_in_bias, ehot) = middle(
        me, enc_lengths[0], encs, cross_kv, ckvT, cqT, qhotT, first, cross_out, ffn_in, ffn_out,
        ffn_in_bias[None], ffn_out_bias[None], norm_gain, norm_bias, oga, ogb,
    )
    layer_out = jnp.concatenate([la, exchange(lb, "seq", mirror)])[None]
    ffn_pairs = [(second_low, g_pre, False), (hidden, g_ffn, False)]
    token = clse
    if cut:
        even1, odd1, token = weight_terms(me, zsize, chips, ffn_pairs, token)
    ek, ev, ekt, enc_all, token = cross_project(encs, cross_kv, ckvT, token)
    if cut:
        sum1, token = add_core([(even1, exchange(odd1, "seq", 1))], token)
        sum1 = across_chips(sum1)
    enc_even, (enc_odd, edk, edv, dcq, g_start, g_branch, gmT, delta, vec1) = cross_back(
        me, ek, ev, ekt, token, cross_kv, cqT, ehot, qhotT, gcT, clse, cdelta, g_mid, cqwT, hat1, scale1, norm_gain,
        self_out, oT,
    )
    groups2 = [(enc_even, exchange(enc_odd, "seq", 1))]
    cross_pairs = [
        (enc_all, edk, False),
        (enc_all, edv, False),
        (cmixT, g_mid.astype(BF), True),
        (first.astype(BF), dcq, False),
        (mixT, g_branch, True),
    ]
    token = g_start
    if cut:
        parts1, _, token = add_chips(zme, sum1, zsize, 0, g_start)
        even2, odd2, token = weight_terms(me, zsize, chips, cross_pairs, token)
        groups2.append((even2, exchange(odd2, "seq", 1)))
    sum2, token = add_core(groups2, token)
    sum2 = across_chips(sum2)
    dec_even, (dec_odd, dk, dv, dq, seg_sums) = self_back(
        me, token, qT, K, KT, V, khot, qhotT, gmT, lse, delta, self_qkv, qkvT, g_start
    )
    groups3 = [(dec_even, exchange(dec_odd, "seq", 1))]
    self_pairs = [(start_low, dq, False), (low_all, dk, False), (low_all, dv, False)]

    tag_hot = (pair_tags[0][:, None] == jnp.arange(NTAGS, dtype=jnp.int32)[None]).astype(F32)
    d_table = lax.dot_general(tag_hot, seg_sums[:SEGS], (TN, ((), ())), precision=lax.Precision.HIGHEST)
    vectors = jnp.stack([vec1[0], vec2[0], vec2[2], vec1[1], vec2[1], vec2[3], vec2[4]])
    lanes = 512 // zsize
    small = jnp.concatenate(
        [
            d_table.reshape(zsize, -1),
            d_in_bias.reshape(zsize, -1),
            vectors.reshape(7, zsize, lanes).transpose(1, 0, 2).reshape(zsize, -1),
        ],
        axis=1,
    )
    small = jnp.pad(small, ((0, 0), (0, 4096 - small.shape[1]))).reshape(zsize, 16, 256)
    if cut:
        even3, odd3, token = weight_terms(me, zsize, chips, self_pairs, token)
        small = small.astype(BF)
        even3 = [jnp.concatenate([e, small], axis=1) for e in even3]
        odd3 = jnp.concatenate([odd3, jnp.broadcast_to(small[None], (chips,) + small.shape)], axis=2)
        groups3.append((even3, exchange(odd3, "seq", 1)))
        sum3, token = add_core(groups3, token)
        sum3 = across_chips(sum3)
        parts2, encoded_grad, _ = add_chips(zme, sum2, zsize, 1, token)
        parts3, input_grad, _ = add_chips(zme, sum3, zsize, 1, token)
        shares = []
        for parts in (parts1, parts2, parts3):
            shares.append(total([parts[0]] + [exchange(parts[k], "rows", k) for k in range(1, zsize)]))
        small = shares[2][-16:].reshape(-1)
        shards = gather(jnp.concatenate([shares[0], shares[1], shares[2][:-16]]).astype(BF))
        ins = 512 // zsize
        shapes = [(ins, 2048), (2048 // zsize, 512), (ins, 1024), (ins, 512), (ins, 512), (ins, 512), (ins, 1536)]
        places = [(0, ins, 0, 2048), (1, 2048 // zsize, 0, 512), (2, ins, 0, 512), (2, ins, 512, 512)]
        places += [(j, ins, 0, 512) for j in (3, 4, 5)] + [(6, ins, 512 * j, 512) for j in range(3)]
        layout, at = [], 0
        for out, R, left, C in places:
            layout.append((out, R, left, C, at))
            at += R // chips * (C // 512)
        d_fi, d_fo, d_ckv, d_co, d_cq, d_so, d_qkv = unpack_shards(me, shards, shapes, layout)
    else:
        (d_fi, d_fo, ck, cv, d_co, d_cq, d_so, dq, dk, dv), small = plain_weights(
            ffn_pairs + cross_pairs + self_pairs, small
        )
        d_ckv, d_qkv = jnp.concatenate([ck, cv], axis=1), jnp.concatenate([dq, dk, dv], axis=1)
        sum3 = across_chips(add_core(groups3, token)[0])
        encoded_grad, input_grad = (
            total([jnp.concatenate([t[:BLK], t[BLK:]], axis=1) for t in terms]) for terms in (sum2, sum3)
        )
    tags, inner = NTAGS // zsize * 512, 2048 // zsize
    vectors = small[tags + inner : tags + inner + 7 * lanes].reshape(7, lanes)
    return (
        layer_out, input_grad[None], encoded_grad[None], small[:tags].reshape(-1, 512), d_qkv, d_so, d_cq, d_ckv, d_co, d_fi,
        small[tags : tags + inner], d_fo, vectors[6], vectors[0:3], vectors[3:6],
    )


def solution(mesh):
    tokens = P("rows", "seq", None)
    placed = (tokens, tokens, P("rows", "seq"), P("rows", None), P("rows", None), tokens) + (P(),) * 12
    rows = P("rows", None)
    return jax.shard_map(
        local,
        mesh=mesh,
        in_specs=placed,
        out_specs=(tokens, tokens, tokens)
        + (rows,) * 7
        + (P("rows"), rows, P("rows"), P(None, "rows"), P(None, "rows")),
        check_vma=False,
    )
```

```python
import jax
import jax.numpy as jnp
from jax import lax
from jax.experimental import pallas as pl
from jax.experimental.pallas import tpu as pltpu
from jax.sharding import PartitionSpec as P

F32 = jnp.float32
BF = jnp.bfloat16
SEGS = 4
NTAGS = 16
BLK = 256
HALF = 128
TILE = 512
BIG = -1e30
EPS = 1e-5
TN = ((0,), (0,))
NT = ((1,), (1,))
VM = pl.BlockSpec(memory_space=pltpu.VMEM)
SM = pl.BlockSpec(memory_space=pltpu.SMEM)
ANY = pl.BlockSpec(memory_space=pl.ANY)
TOKEN = jax.ShapeDtypeStruct((8, 128), F32)


def shape(dims, dtype=BF):
    return jax.ShapeDtypeStruct(dims, dtype)


def call(kernel, name, ins, specs, outs, out_specs=None, scratch=(), work=1):
    return pl.pallas_call(
        kernel,
        out_shape=tuple(outs),
        in_specs=list(specs),
        out_specs=tuple(out_specs or (VM,) * len(outs)),
        scratch_shapes=list(scratch),
        compiler_params=pltpu.CompilerParams(vmem_limit_bytes=60 << 20),
        cost_estimate=pl.CostEstimate(flops=work, bytes_accessed=1, transcendentals=0),
        name=name,
    )(*ins)


def dot(a, b, dims=((1,), (0,))):
    return lax.dot_general(a, b, (dims, ((), ())), preferred_element_type=F32)


def total(terms):
    out = terms[0].astype(F32)
    for term in terms[1:]:
        out = out + term.astype(F32)
    return out


def build_blocks(src_ref, extra_ref, dst_ref):
    z = jnp.zeros((64, HALF), BF)
    for p in range(4):
        for h in range(2):
            c = slice(h * HALF, (h + 1) * HALF)
            dst_ref[2 * p + h, 0:64, :] = jnp.concatenate([src_ref[128 * p : 128 * p + 64, c], z], 1)
            dst_ref[2 * p + h, 64:128, :] = jnp.concatenate([z, src_ref[128 * p + 64 : 128 * p + 128, c]], 1)
            if extra_ref is not None:
                e = extra_ref[:, c]
                dst_ref[2 * p + h, 128:144, :] = jnp.concatenate([e, e], 1)
                dst_ref[2 * p + h, 144:256, :] = jnp.zeros((112, 256), BF)


def split_heads(j, a, o_ref):
    p, h = j // 2, j % 2
    o_ref[128 * p : 128 * p + 64, h * HALF : (h + 1) * HALF] = a[0:64, 0:HALF]
    o_ref[128 * p + 64 : 128 * p + 128, h * HALF : (h + 1) * HALF] = a[64:128, HALF:]


def cross_forward(q_ref, k_ref, vt_ref, khot_ref, qhot_ref, o_ref, lse_ref, qb):
    build_blocks(q_ref, qhot_ref, qb)
    tiles = k_ref.shape[0] // TILE
    for j in range(8):
        p = j // 2

        def scores(t):
            rows = pl.ds(t * TILE, TILE)
            kt = jnp.concatenate([k_ref[rows, 128 * p : 128 * p + 128], khot_ref[rows, :]], 1)
            return dot(kt, qb[j])

        top = jnp.max(scores(0), axis=0, keepdims=True)
        for t in range(1, tiles):
            top = jnp.maximum(top, jnp.max(scores(t), axis=0, keepdims=True))
        whole = jnp.zeros((1, 256), F32)
        acc = jnp.zeros((128, 256), F32)
        for t in range(tiles):
            e = jnp.exp(scores(t) - top)
            whole = whole + jnp.sum(e, axis=0, keepdims=True)
            acc = acc + dot(vt_ref[128 * p : 128 * p + 128, t * TILE : (t + 1) * TILE], e.astype(BF))
        lse_ref[j] = top + jnp.log(whole)
        split_heads(j, acc * (1.0 / whole), o_ref)


def cross_backward(copies, q_ref, k_ref, v_ref, khot_ref, qhot_ref, do_ref, lse_ref, dl_ref, dq_ref, dkv_ref, qb, db):
    build_blocks(q_ref, qhot_ref, qb)
    build_blocks(do_ref, None, db)
    size = min(2048, k_ref.shape[1])
    for p in range(4):
        lanes = slice(128 * p, 128 * p + 128)
        dq = [0.0, 0.0]
        for copy in copies[p]:
            copy.wait()
        for t in range(k_ref.shape[1] // size):
            rows = slice(t * size, (t + 1) * size)
            k = k_ref[p, rows, :]
            k_turned = k.T
            kt = jnp.concatenate([k, khot_ref[rows, :]], 1)
            dk = dv = 0.0
            for h in range(2):
                j = 2 * p + h
                pr = jnp.exp(dot(kt, qb[j]) - lse_ref[j])
                dp = dot(v_ref[p, rows, :], db[j])
                ds = (pr * (dp - dl_ref[j])).astype(BF)
                dv += dot(pr.astype(BF), db[j], NT)
                dk += dot(ds, qb[j, 0:128, :], NT)
                dq[h] += dot(k_turned, ds)
            dkv_ref[rows, lanes] = dk.astype(BF)
            dkv_ref[rows, 512 + 128 * p : 640 + 128 * p] = dv.astype(BF)
        for h in range(2):
            split_heads(2 * p + h, dq[h] * 0.125, dq_ref)


def work_item(t, i, blocks):
    first = (i + 2) // 2
    second = (t >= first).astype(jnp.int32)
    tile = t - second * first
    start = jnp.where(second == 1, (blocks - 1 - i) * BLK + HALF, i * BLK)
    return second, tile, start - tile * TILE


def relative_positions(swap):
    k = lax.broadcasted_iota(jnp.int32, (TILE, 2 * HALF), 0)
    q = lax.broadcasted_iota(jnp.int32, (TILE, 2 * HALF), 1) & (HALF - 1)
    return (k ^ swap) - q


def self_forward(blocks, i, q_ref, k_ref, vt_ref, khot_ref, qhot_ref, o_ref, lse_ref, qb, m_s, l_s, acc):
    build_blocks(q_ref, qhot_ref, qb)
    swap = (i & 1) * BLK
    items = blocks // 2 + 1
    m_s[...] = jnp.full(m_s.shape, -3e38, F32)
    l_s[...] = jnp.zeros(l_s.shape, F32)
    acc[...] = jnp.zeros(acc.shape, F32)

    def scores(t, p):
        h, tile, offset = work_item(t, i, blocks)
        r0 = pl.multiple_of((tile ^ (i >> 1)) * TILE, TILE)
        kt = jnp.concatenate([k_ref[pl.ds(r0, TILE), 128 * p : 128 * p + 128], khot_ref[pl.ds(r0, TILE), :]], 1)
        return jnp.where(relative_positions(swap) <= offset, dot(kt, qb[2 * p + h]), BIG), 2 * p + h, r0

    @pl.loop(0, items)
    def _(t):
        for p in range(4):
            s, j, _ = scores(t, p)
            m_s[j] = jnp.maximum(m_s[j], jnp.max(s, axis=0, keepdims=True))

    @pl.loop(0, items)
    def _(t):
        for p in range(4):
            s, j, r0 = scores(t, p)
            e = jnp.exp(s - m_s[j])
            l_s[j] += jnp.sum(e, axis=0, keepdims=True)
            acc[j] += dot(vt_ref[128 * p : 128 * p + 128, pl.ds(r0, TILE)], e.astype(BF))

    for j in range(8):
        lse_ref[j] = m_s[j] + jnp.log(l_s[j])
        split_heads(j, acc[j] * (1.0 / l_s[j]), o_ref)


def self_backward(
    blocks, i, q_ref, k_ref, kt_ref, v_ref, khot_ref, qhot_ref, do_ref, lse_ref, dl_ref, dq_ref, dkv_ref,
    qb, db, dqa, dka, dva,
):
    build_blocks(q_ref, qhot_ref, qb)
    build_blocks(do_ref, None, db)
    swap = (i & 1) * BLK
    dqa[...] = jnp.zeros(dqa.shape, F32)
    dka[...] = jnp.zeros(dka.shape, F32)
    dva[...] = jnp.zeros(dva.shape, F32)

    @pl.loop(0, blocks // 2 + 1)
    def _(t):
        h, tile, offset = work_item(t, i, blocks)
        rows = pl.ds(pl.multiple_of((tile ^ (i >> 1)) * TILE, TILE), TILE)
        hot = khot_ref[rows, :]
        for p in range(4):
            j = 2 * p + h
            lanes = slice(128 * p, 128 * p + 128)
            s = dot(jnp.concatenate([k_ref[rows, lanes], hot], 1), qb[j])
            pr = jnp.exp(jnp.where(relative_positions(swap) <= offset, s, BIG) - lse_ref[j])
            dp = dot(v_ref[rows, lanes], db[j])
            ds = (pr * (dp - dl_ref[j])).astype(BF)
            dva[rows, lanes] += dot(pr.astype(BF), db[j], NT)
            dka[rows, lanes] += dot(ds, qb[j, 0:128, :], NT)
            dqa[j] += dot(kt_ref[lanes, rows], ds)

    dkv_ref[:, 0:512] = dka[...].astype(BF)
    dkv_ref[:, 512:1024] = dva[...].astype(BF)
    for j in range(8):
        split_heads(j, dqa[j] * 0.125, dq_ref)


def norm_forward(v, gain, bias):
    centered = v - jnp.mean(v, axis=-1, keepdims=True)
    scale = lax.rsqrt(jnp.mean(centered * centered, axis=-1, keepdims=True) + EPS)
    hat = centered * scale
    return hat * gain + bias, hat, scale


def norm_backward(g, hat, scale, gain):
    gh = g * gain
    out = scale * (gh - jnp.mean(gh, axis=-1, keepdims=True) - hat * jnp.mean(gh * hat, axis=-1, keepdims=True))
    return out, jnp.sum(g * hat, axis=0, keepdims=True), jnp.sum(g, axis=0, keepdims=True)


def gelu_both(x):
    c = 0.7978845608028654
    sq = x * x
    t = jnp.tanh(c * x * (1 + 0.044715 * sq))
    half = 0.5 * (1 + t)
    return x * half, half + 0.5 * x * (1 - t * t) * (c * (1 + 3 * 0.044715 * sq))


def inner_rows(g_refT, o_ref, dl_ref):
    for p in range(4):
        both = []
        for a in range(2):
            rows = slice(128 * p + 64 * a, 128 * p + 64 * a + 64)
            both.append(jnp.sum(g_refT[rows, :].astype(F32) * o_ref[rows, :], axis=0, keepdims=True))
        for h in range(2):
            cols = slice(h * HALF, (h + 1) * HALF)
            dl_ref[2 * p + h] = jnp.concatenate([both[0][:, cols], both[1][:, cols]], 1)


class Cut:
    def __init__(self, chips, zsize, tokens, sizes, extra=0):
        self.chips, self.zsize, self.tokens, self.extra = chips, zsize, tokens, extra
        self.at, rows = [], 0
        for R, C in sizes:
            self.at.append(rows)
            rows += R // (zsize * chips) * (C // 512)
        self.per_z = rows + extra
        self.rows = tokens + zsize * self.per_z

    def write(self, index, keep, me, evens, odd_ref):
        R, C = keep.shape
        core, chip = me & 1, me >> 1
        size, half = R // (self.zsize * self.chips), C // 2
        for turn in range(2):
            side = core if turn == 0 else 1 - core
            for j in range(self.chips):
                for z in range(self.zsize):
                    row = pl.multiple_of(z * (R // self.zsize) + (chip ^ j) * size, size)
                    for c in range(half // 256):
                        left = pl.multiple_of(side * half + 256 * c, 256)
                        at = self.tokens + z * self.per_z + self.at[index] + c * size
                        piece = keep[pl.ds(row, size), pl.ds(left, 256)]
                        if turn == 0:
                            evens[j][at : at + size, :] = piece
                        else:
                            odd_ref[j, at : at + size, :] = piece

    def write_tokens(self, r, part, evens, odd_ref):
        for c in range(2):
            piece = part[:, 256 * c : 256 * c + 256]
            if r % 2:
                odd_ref[r // 2, BLK * c : BLK * c + BLK, :] = piece
            else:
                evens[r // 2][BLK * c : BLK * c + BLK, :] = piece

    def write_extra(self, z, part, evens, odd_ref):
        at = self.tokens + z * self.per_z + self.per_z - self.extra
        for j in range(self.chips):
            evens[j][at : at + self.extra, :] = part
            odd_ref[j, at : at + self.extra, :] = part

    def outs(self):
        return [shape((self.rows, 256))] * self.chips + [shape((self.chips, self.rows, 256))]


def join_tokens(x, seg):
    def kernel(x_ref, seg_ref, o_ref):
        o_ref[0:BLK, :] = x_ref[...]
        row = jnp.concatenate([seg_ref[...].astype(F32), jnp.zeros((1, 256), F32)], 1)
        o_ref[BLK:, :] = jnp.broadcast_to(row, (16, 512)).astype(BF)

    return call(kernel, "join_tokens", (x, seg), [VM] * 2, [shape((BLK + 16, 512))])[0]


def prepare(after, grad, mine, other, *rest):
    def kernel(g_ref, a_ref, b_ref, *refs):
        ga_ref, gb_ref, both_ref = refs[-3:]
        ga_ref[...] = g_ref[0:HALF, :]
        gb_ref[...] = g_ref[HALF:, :]
        both_ref[0:BLK, :] = a_ref[...]
        both_ref[BLK:, :] = b_ref[...]

    outs = [shape((HALF, 512)), shape((HALF, 512)), shape((2 * BLK, 512))]
    ins = (grad, mine, other, after, *rest)
    return call(kernel, "prepare", ins, [VM] * 3 + [ANY] * (len(ins) - 3), outs)


def self_front_kernel(n, me_ref, tag_ref, *refs):
    xs, refs = refs[:n], refs[n:]
    (table_ref, w_ref, so_ref, cqw_ref, gain_ref, bias_ref,
     low_ref, k_ref, v_ref, khot_ref, qhot_ref, qT_ref, oT_ref, lse_ref, hat_ref, scale_ref, first_ref,
     flow_ref, cqT_ref, mixT_ref, slow_ref,
     low_s, k_s, v_s, khot_s, vt_s, start_s, qb, m_s, l_s, acc, sems) = refs
    segs = [x[BLK : BLK + 8, 0:BLK].astype(F32)[0:1].astype(jnp.int32) for x in xs]
    table = table_ref[...].astype(F32)
    ids = lax.broadcasted_iota(jnp.int32, (NTAGS, 512), 0)
    rows = [jnp.sum(jnp.where(ids == tag_ref[s], table, 0.0), axis=0, keepdims=True) for s in range(SEGS)]
    tag_rows = jnp.concatenate(rows + [jnp.zeros((128 - SEGS, 512), F32)], 0).astype(BF)
    for r in range(n):
        at = slice(r * BLK, (r + 1) * BLK)
        hotT = (lax.broadcasted_iota(jnp.int32, (128, BLK), 0) == segs[r]).astype(F32)
        hot = hotT.T
        khot_s[at, :] = hot.astype(BF)
        start = xs[r][0:BLK, :].astype(F32) + dot(hot.astype(BF), tag_rows)
        low = start.astype(BF)
        low_s[at, :] = low
        if r == 0:
            start_s[0:HALF, :] = start[0:HALF]
        if r == n - 1:
            start_s[HALF:, :] = start[HALF:]
        k_s[at, :] = dot(low, w_ref[:, 512:1024]).astype(BF)
        v = dot(low, w_ref[:, 1024:1536]).astype(BF)
        v_s[at, :] = v
        vt_s[:, at] = v.T
    pairs = [(low_s, low_ref), (k_s, k_ref), (v_s, v_ref), (khot_s, khot_ref)]
    copies = [pltpu.make_async_copy(a, b, sems.at[j]) for j, (a, b) in enumerate(pairs)]
    for copy in copies:
        copy.start()
    seg = jnp.concatenate([segs[0][:, 0:HALF], segs[n - 1][:, HALF:]], 1)
    ids = lax.broadcasted_iota(jnp.int32, (16, BLK), 0)
    qhot_ref[...] = jnp.where((ids != seg) & (ids < SEGS), BIG, 0.0).astype(BF)
    slow = start_s[...].astype(BF)
    slow_ref[...] = slow
    qT_ref[...] = (dot(slow, w_ref[:, 0:512]) * 0.125).astype(BF).T
    self_forward(n, me_ref[0], qT_ref, k_s, vt_s, khot_s, qhot_ref, oT_ref, lse_ref, qb, m_s, l_s, acc)
    mixT = oT_ref[...].astype(BF)
    mixT_ref[...] = mixT
    first, hat, scale = norm_forward(
        start_s[...] + dot(mixT, so_ref[...], TN), gain_ref[0:1, :].astype(F32), bias_ref[0:1, :].astype(F32)
    )
    hat_ref[...] = hat
    scale_ref[...] = jnp.broadcast_to(scale, (BLK, 128))
    first_ref[...] = first
    first_low = first.astype(BF)
    flow_ref[...] = first_low
    cqT_ref[...] = (dot(first_low, cqw_ref[...]) * 0.125).astype(BF).T
    for copy in copies:
        copy.wait()


def self_front(me, tags, xs, table, w, so, cqw, gain, bias):
    n = len(xs)
    S = n * BLK
    big = [shape((S, 512)), shape((S, 512)), shape((S, 512)), shape((S, 128))]
    outs = big + [
        shape((16, BLK)), shape((512, BLK)), shape((512, BLK), F32), shape((8, 1, BLK), F32), shape((BLK, 512), F32),
        shape((BLK, 128), F32), shape((BLK, 512), F32), shape((BLK, 512)), shape((512, BLK)), shape((512, BLK)),
        shape((BLK, 512)),
    ]
    scratch = [pltpu.VMEM(s.shape, BF) for s in big] + [
        pltpu.VMEM((512, S), BF), pltpu.VMEM((BLK, 512), F32), pltpu.VMEM((8, 256, 256), BF),
        pltpu.VMEM((8, 1, 256), F32), pltpu.VMEM((8, 1, 256), F32), pltpu.VMEM((8, 128, 256), F32),
        pltpu.SemaphoreType.DMA((4,)),
    ]
    return call(
        lambda *refs: self_front_kernel(n, *refs), "self_front", (me, tags, *xs, table, w, so, cqw, gain, bias),
        [SM, SM] + [VM] * (n + 6), outs, [ANY] * 4 + [VM] * 11, scratch,
    )


def middle_kernel(n, cut, me_ref, len_ref, *refs):
    encs, refs = refs[: n // 2], refs[n // 2 :]
    (w_ref, cqT_ref, qhot_ref, first_ref, co_ref, fi_ref, fo_ref, bi_ref, bo_ref, gain_ref, bias_ref,
     oga_ref, ogb_ref, *refs) = refs
    if cut:
        evens, (odd_ref, *refs) = refs[: cut.chips], refs[cut.chips :]
    (la_ref, lb_ref, hid_ref, slow_ref, gffn_ref, gpre_ref, gmid_ref, gcb_ref, gcT_ref, dl_ref, lse_ref, cmixT_ref,
     vec_ref, dib_ref, khot_ref, k_ref, v_ref, k_s, v_s, vt_s, oT_s, slope_s, qb, fi_s, fo_s, sems) = refs
    me = me_ref[0]
    e0 = len_ref[0]
    e1 = e0 + len_ref[1]
    e2 = e1 + len_ref[2]
    for r in range(n):
        at = slice(r * BLK, (r + 1) * BLK)
        pos = lax.broadcasted_iota(jnp.int32, (BLK, 128), 0) + (me ^ r) * BLK
        seg = (pos >= e0).astype(jnp.int32) + (pos >= e1).astype(jnp.int32) + (pos >= e2).astype(jnp.int32)
        khot_ref[at, :] = (lax.broadcasted_iota(jnp.int32, (BLK, 128), 1) == seg).astype(F32).astype(BF)
        enc = encs[r // 2][BLK * (r % 2) : BLK * (r % 2) + BLK, :]
        k_s[at, :] = dot(enc, w_ref[:, 0:512]).astype(BF)
        v = dot(enc, w_ref[:, 512:1024]).astype(BF)
        v_s[at, :] = v
        vt_s[:, at] = v.T
    copies = [pltpu.make_async_copy(k_s, k_ref, sems.at[0]), pltpu.make_async_copy(v_s, v_ref, sems.at[1])]
    for copy in copies:
        copy.start()
    cross_forward(cqT_ref, k_s, vt_s, khot_ref, qhot_ref, oT_s, lse_ref, qb)
    cmixT = oT_s[...].astype(BF)
    cmixT_ref[...] = cmixT
    gains = [gain_ref[j : j + 1, :].astype(F32) for j in range(3)]
    shifts = [bias_ref[j : j + 1, :].astype(F32) for j in range(3)]
    second, hat2, scale2 = norm_forward(first_ref[...] + dot(cmixT, co_ref[...], TN), gains[1], shifts[1])
    second_low = second.astype(BF)
    slow_ref[...] = second_low
    out = second + bo_ref[...].astype(F32)
    for c in range(4):
        cols = slice(512 * c, 512 * c + 512)
        act, slope = gelu_both(dot(second_low, fi_ref[:, cols]) + bi_ref[:, cols].astype(F32))
        hidden = act.astype(BF)
        hid_ref[:, cols] = hidden
        slope_s[:, cols] = slope
        out = out + dot(hidden, fo_ref[cols, :])
    result, hat3, scale3 = norm_forward(out, gains[2], shifts[2])
    la_ref[...] = result[0:HALF].astype(BF)
    lb_ref[...] = result[HALF:].astype(BF)
    og = jnp.concatenate([oga_ref[...], ogb_ref[...]], 0).astype(F32)
    g3, gg3, gb3 = norm_backward(og, hat3, scale3, gains[2])
    g_ffn = g3.astype(BF)
    gffn_ref[...] = g_ffn
    d_out_bias = jnp.sum(g_ffn.astype(F32), axis=0, keepdims=True)
    g2 = g3
    for c in range(4):
        cols = slice(512 * c, 512 * c + 512)
        g_pre = (dot(g_ffn, fo_ref[cols, :], NT) * slope_s[:, cols]).astype(BF)
        gpre_ref[:, cols] = g_pre
        dib_ref[:, cols] = jnp.sum(g_pre.astype(F32), axis=0, keepdims=True)
        g2 = g2 + dot(g_pre, fi_ref[:, cols], NT)
        if cut:
            fi_s[:, cols] = dot(second_low, g_pre, TN).astype(BF)
            fo_s[cols, :] = dot(hid_ref[:, cols], g_ffn, TN).astype(BF)
    g_mid, gg2, gb2 = norm_backward(g2, hat2, scale2, gains[1])
    gmid_ref[...] = g_mid
    g_cb = g_mid.astype(BF)
    gcb_ref[...] = g_cb
    gcT_ref[...] = dot(co_ref[...], g_cb, NT).astype(BF)
    inner_rows(gcT_ref, oT_s, dl_ref)
    vec_ref[...] = jnp.concatenate([gg2, gb2, gg3, gb3, d_out_bias, jnp.zeros((3, 512), F32)], 0)
    if cut:
        cut.write(0, fi_s, me, evens, odd_ref)
        cut.write(1, fo_s, me, evens, odd_ref)
    for copy in copies:
        copy.wait()


def middle(cut, me, lens, encs, *rest):
    n = 2 * len(encs)
    S = n * BLK
    outs = (cut.outs() if cut else []) + [
        shape((HALF, 512)), shape((HALF, 512)), shape((BLK, 2048)), shape((BLK, 512)), shape((BLK, 512)),
        shape((BLK, 2048)), shape((BLK, 512), F32), shape((BLK, 512)), shape((512, BLK)), shape((8, 1, 256), F32),
        shape((8, 1, 256), F32), shape((512, BLK)), shape((8, 512), F32), shape((1, 2048), F32), shape((S, 128)),
        shape((S, 512)), shape((S, 512)),
    ]
    scratch = [
        pltpu.VMEM((S, 512), BF), pltpu.VMEM((S, 512), BF), pltpu.VMEM((512, S), BF), pltpu.VMEM((512, BLK), F32),
        pltpu.VMEM((BLK, 2048), F32), pltpu.VMEM((8, 256, 256), BF), pltpu.VMEM((512, 2048), BF),
        pltpu.VMEM((2048, 512), BF), pltpu.SemaphoreType.DMA((2,)),
    ]
    got = call(
        lambda *refs: middle_kernel(n, cut, *refs), "middle", (me, lens, *encs, *rest),
        [SM, SM] + [VM] * (n // 2 + 13), outs, [VM] * (len(outs) - 2) + [ANY] * 2, scratch,
    )
    return got[:-17], got[-17:]


def cross_back_kernel(n, cut, weights, me_ref, *refs):
    half = n // 2
    (k_hbm, v_hbm, _, *refs) = refs
    encs, refs = refs[:half], refs[half:]
    (w_ref, cqT_ref, khot_ref, qhot_ref, gcT_ref, lse_ref, dl_ref, gmid_ref, cqw_ref, hat_ref, scale_ref, gain_ref,
     so_ref, oT_ref, cmixT_ref, gcb_ref, flow_ref, mixT_ref, *refs) = refs
    evens, (odd_ref, gstart_ref, gmT_ref, dl1_ref, vec_ref, *refs) = refs[:half], refs[half:]
    dkv_ref, dq_ref, gbr_ref, k_s, v_s, dqT_s, qb, db, enc_s, keep, kv_keep, sems = refs
    copies, late = [], []
    for p in range(4):
        lanes = slice(128 * p, 128 * p + 128)
        copies.append([
            pltpu.make_async_copy(k_hbm.at[:, lanes], k_s.at[p], sems.at[2 * p]),
            pltpu.make_async_copy(v_hbm.at[:, lanes], v_s.at[p], sems.at[2 * p + 1]),
        ])
    if weights:
        for j in range(half):
            rows = slice(2 * BLK * j, 2 * BLK * (j + 1))
            late.append(pltpu.make_async_copy(encs[j], enc_s.at[rows, :], sems.at[12 + j]))
    for copy in sum(copies, []) + late:
        copy.start()
    cross_backward(
        copies, cqT_ref, k_s, v_s, khot_ref, qhot_ref, gcT_ref, lse_ref, dl_ref, dqT_s, dkv_ref, qb, db
    )
    me = me_ref[0]
    for r in range(n):
        at = slice(r * BLK, (r + 1) * BLK)
        part = dot(dkv_ref[at, :], w_ref[...], NT)
        cut.write_tokens(r, part.astype(BF), evens, odd_ref)
    dq = dqT_s[...].astype(BF).T
    dq_ref[...] = dq
    g1 = gmid_ref[...] + dot(dq, cqw_ref[...], NT)
    g_start, gg1, gb1 = norm_backward(g1, hat_ref[...], scale_ref[:, 0:1], gain_ref[0:1, :].astype(F32))
    gstart_ref[...] = g_start
    g_branch = g_start.astype(BF)
    gbr_ref[...] = g_branch
    gmT_ref[...] = dot(so_ref[...], g_branch, NT).astype(BF)
    inner_rows(gmT_ref, oT_ref, dl1_ref)
    vec_ref[...] = jnp.concatenate([gg1, gb1, jnp.zeros((6, 512), F32)], 0)
    if weights:
        keep[0] = dot(cmixT_ref[...], gcb_ref[...]).astype(BF)
        keep[1] = dot(flow_ref[...], dq_ref[...], TN).astype(BF)
        keep[2] = dot(mixT_ref[...], g_branch).astype(BF)
        for j in range(3):
            cut.write(1 + j, keep.at[j], me, evens, odd_ref)
        for copy in late:
            copy.wait()
        kv_keep[...] = dot(enc_s[...], dkv_ref[...], TN).astype(BF)
        cut.write(0, kv_keep, me, evens, odd_ref)


def cross_back(cut, weights, me, k, v, after, encs, *rest):
    n = 2 * len(encs)
    S = n * BLK
    more = [shape((S, 1024)), shape((BLK, 512)), shape((BLK, 512))]
    outs = cut.outs() + [
        shape((BLK, 512), F32), shape((512, BLK)), shape((8, 1, 256), F32), shape((8, 512), F32)
    ] + ([] if weights else more)
    scratch = ([pltpu.VMEM(s.shape, s.dtype) for s in more] if weights else []) + [
        pltpu.VMEM((4, S, 128), BF), pltpu.VMEM((4, S, 128), BF),
        pltpu.VMEM((512, BLK), F32), pltpu.VMEM((8, 256, 256), BF), pltpu.VMEM((8, 128, 256), BF),
        pltpu.VMEM((S if weights else 16, 512), BF), pltpu.VMEM((3, 512, 512), BF), pltpu.VMEM((512, 1024), BF),
        pltpu.SemaphoreType.DMA((12 + n // 2,)),
    ]
    got = call(
        lambda *refs: cross_back_kernel(n, cut, weights, *refs), "cross_back", (me, k, v, after, *encs, *rest),
        [SM] + [ANY] * (3 + n // 2) + [VM] * 18, outs, None, scratch,
    )
    return got[: n // 2 + 1], got[n // 2 + 1 :]


def self_back_kernel(n, cut, weights, me_ref, tag_ref, *refs):
    half = n // 2
    (_, low_hbm, k_hbm, v_hbm, khot_hbm, qT_ref, qhot_ref, gmT_ref, lse_ref, dl_ref, w_ref,
     gstart_ref, slow_ref, vec1_ref, vec2_ref, dib_ref, *refs) = refs
    evens, (odd_ref, small_ref, *refs) = refs[:half], refs[half:]
    (dkv_ref, dq_ref, low_s, k_s, v_s, kt_s, khot_s, dqT_s, qb, db, dqa, dka, dva, keep, sems) = refs
    pairs = [(k_hbm, k_s), (v_hbm, v_s), (khot_hbm, khot_s)]
    if weights:
        pairs.append((low_hbm, low_s))
    copies = [pltpu.make_async_copy(a, b, sems.at[j]) for j, (a, b) in enumerate(pairs)]
    for copy in copies:
        copy.start()
    for copy in copies[:3]:
        copy.wait()
    for r in range(n):
        at = slice(r * BLK, (r + 1) * BLK)
        kt_s[:, at] = k_s[at, :].T
    me = me_ref[0]
    self_backward(
        n, me, qT_ref, k_s, kt_s, v_s, khot_s, qhot_ref, gmT_ref, lse_ref, dl_ref, dqT_s, dkv_ref,
        qb, db, dqa, dka, dva,
    )
    dq = dqT_s[...].astype(BF).T
    dq_ref[...] = dq
    mine = gstart_ref[...] + dot(dq, w_ref[:, 0:512], NT)
    sums = jnp.zeros((128, 512), F32)
    for r in range(n):
        at = slice(r * BLK, (r + 1) * BLK)
        part = dot(dkv_ref[at, :], w_ref[:, 512:1536], NT)
        if r == 0:
            part = jnp.concatenate([part[:HALF] + mine[:HALF], part[HALF:]], 0)
        if r == n - 1:
            part = jnp.concatenate([part[:HALF], part[HALF:] + mine[HALF:]], 0)
        part = part.astype(BF)
        sums = sums + dot(khot_s[at, :], part, TN)
        cut.write_tokens(r, part, evens, odd_ref)
    ids = lax.broadcasted_iota(jnp.int32, (NTAGS, 512), 0)
    table = jnp.zeros((NTAGS, 512), F32)
    for s in range(SEGS):
        table = table + jnp.where(ids == tag_ref[s], sums[s : s + 1, :], 0.0)
    v1, v2 = vec1_ref[...], vec2_ref[...]
    vectors = [v1[0:1], v2[0:1], v2[2:3], v1[1:2], v2[1:2], v2[3:4], v2[4:5], jnp.zeros((1, 512), F32)]
    if weights:
        zs = cut.zsize
        wide, lanes, tags = 2048 // zs, 512 // zs, NTAGS // zs
        for z in range(zs):
            rows = []
            for c in range(2):
                rows.append(table[tags * z : tags * (z + 1), 256 * c : 256 * c + 256])
            rows += [dib_ref[:, wide * z + 256 * c : wide * z + 256 * (c + 1)] for c in range(wide // 256)]
            cut_rows = [v[:, lanes * z : lanes * (z + 1)] for v in vectors]
            rows += [jnp.concatenate(cut_rows[2 * c : 2 * c + 2], 1) for c in range(4)]
            used = 2 * tags + wide // 256 + 4
            rows.append(jnp.zeros((16 - used, 256), F32))
            cut.write_extra(z, jnp.concatenate(rows, 0).astype(BF), evens, odd_ref)
        small_ref[...] = jnp.zeros(small_ref.shape, F32)
        keep[:, 0:512] = dot(slow_ref[...], dq_ref[...], TN).astype(BF)
        copies[3].wait()
        keep[:, 512:1536] = dot(low_s[...], dkv_ref[...], TN).astype(BF)
        for j in range(3):
            cut.write(j, keep.at[:, 512 * j : 512 * j + 512], me, evens, odd_ref)
    else:
        small_ref[...] = jnp.concatenate([table] + vectors, 0)


def self_back(cut, weights, me, tags, after, low, k, v, khot, *rest):
    S = k.shape[0]
    n = S // BLK
    more = [shape((S, 1024)), shape((BLK, 512))]
    outs = cut.outs() + [shape((24, 512), F32)] + ([] if weights else more)
    scratch = ([pltpu.VMEM(s.shape, s.dtype) for s in more] if weights else []) + [
        pltpu.VMEM((S if weights else 16, 512), BF), pltpu.VMEM((S, 512), BF), pltpu.VMEM((S, 512), BF),
        pltpu.VMEM((512, S), BF), pltpu.VMEM((S, 128), BF),
        pltpu.VMEM((512, BLK), F32), pltpu.VMEM((8, 256, 256), BF), pltpu.VMEM((8, 128, 256), BF),
        pltpu.VMEM((8, 128, 256), F32), pltpu.VMEM((S, 512), F32), pltpu.VMEM((S, 512), F32),
        pltpu.VMEM((512, 1536), BF), pltpu.SemaphoreType.DMA((4,)),
    ]
    got = call(
        lambda *refs: self_back_kernel(n, cut, weights, *refs), "self_back",
        (me, tags, after, low, k, v, khot, *rest), [SM, SM] + [ANY] * 5 + [VM] * 11, outs, None, scratch,
    )
    return got[: n // 2 + 1], got[n // 2 + 1 :]


def add_core(evens, got, after):
    count = len(evens)

    def kernel(*refs):
        ins, got_ref, outs, (e_s, g_s, sems) = refs[:count], refs[count], refs[count + 2 : 2 * count + 2], refs[-3:]
        loads, stores = [], []
        for j in range(count):
            loads.append((
                pltpu.make_async_copy(ins[j], e_s.at[j], sems.at[0, j]),
                pltpu.make_async_copy(got_ref.at[j], g_s.at[j], sems.at[1, j]),
            ))
            for copy in loads[j]:
                copy.start()
        for j in range(count):
            for copy in loads[j]:
                copy.wait()
            e_s[j] = (e_s[j].astype(F32) + g_s[j].astype(F32)).astype(BF)
            stores.append(pltpu.make_async_copy(e_s.at[j], outs[j], sems.at[2, j]))
            stores[j].start()
        for copy in stores:
            copy.wait()

    dims = (count,) + evens[0].shape
    return call(
        kernel, "add_core", (*evens, got, after), [ANY] * (count + 2), [shape(e.shape) for e in evens], [ANY] * count,
        [pltpu.VMEM(dims, BF), pltpu.VMEM(dims, BF), pltpu.SemaphoreType.DMA((3, count))],
    )


def add_chips(cut, zme, terms, after, more=None):
    count, per = len(terms), cut.per_z
    extra = list(more or [])

    def kernel(z_ref, *refs):
        ins, (near_ref, far_ref, *outs) = refs[:count], refs[count + 1 + len(extra) :]
        s, sems = outs[-2:]
        loads = []
        for j in range(count):
            rows = slice(cut.tokens, cut.rows)
            loads.append(pltpu.make_async_copy(ins[j].at[rows, :], s.at[j, rows, :], sems.at[0, j]))
        for j in range(count if cut.tokens else 0):
            rows = slice(0, cut.tokens)
            loads.append(pltpu.make_async_copy(ins[j].at[rows, :], s.at[j, rows, :], sems.at[1, j]))
        for copy in loads:
            copy.start()
        for copy in loads[:count]:
            copy.wait()
        for k in range(4):
            row = pl.multiple_of(cut.tokens + (z_ref[0] ^ k) * per, 16)
            value = total([s[j, pl.ds(row, per), :] for j in range(count)]).astype(BF)
            (near_ref if k < 2 else far_ref)[k % 2] = value
        for copy in loads[count:]:
            copy.wait()
        for c in range(2 if cut.tokens else 0):
            part = total([s[j, BLK * c : BLK * c + BLK, :] for j in range(count)])
            outs[0][:, 256 * c : 256 * c + 256] = part
        if extra:
            near, got = refs[count + 1 : count + 3]
            send_ref, keep_ref = outs[-4:-2]
            send_ref[...] = (near[1].astype(F32) + got[1].astype(F32)).astype(BF)
            keep_ref[...] = near[0].astype(F32) + got[0].astype(F32)

    outs = [shape((2, per, 256)), shape((2, per, 256))] + [shape((BLK, 512), F32)] * (cut.tokens > 0)
    if extra:
        outs += [shape(extra[0].shape[1:]), shape(extra[0].shape[1:], F32)]
    return call(
        kernel, "add_chips", (zme, *terms, after, *extra), [SM] + [ANY] * (count + 1) + [VM] * len(extra), outs, None,
        [pltpu.VMEM((count, cut.rows, 256), BF), pltpu.SemaphoreType.DMA((2, count))], 1 << 40,
    )


def add_far(near, got, kept=None, sent=None):
    extra = [] if kept is None else [kept, sent]

    def kernel(near_ref, got_ref, *refs):
        outs = refs[len(extra) :]
        outs[0][...] = (near_ref[1].astype(F32) + got_ref[1].astype(F32)).astype(BF)
        outs[1][...] = near_ref[0].astype(F32) + got_ref[0].astype(F32)
        if extra:
            outs[2][...] = (refs[0][...] + refs[1][...].astype(F32)).astype(BF)

    outs = [shape(near.shape[1:]), shape(near.shape[1:], F32)] + [shape(x.shape) for x in extra[:1]]
    return call(kernel, "add_far", (near, got, *extra), [VM] * (2 + len(extra)), outs)


def add_near(first, kept, sent):
    top, rows = first.shape[0], first.shape[0] + kept.shape[0]

    def kernel(first_ref, kept_ref, sent_ref, out_ref):
        out_ref[0:top, :] = first_ref[...]
        out_ref[top:, :] = (kept_ref[...] + sent_ref[...].astype(F32)).astype(BF)

    return call(kernel, "add_near", (first, kept, sent), [VM] * 3, [shape((rows, 256))])[0]


def add_last(kept, sent, extra, after):
    rows = kept.shape[0] - extra

    def kernel(kept_ref, sent_ref, *refs):
        out_ref, small_ref = refs[-2:]
        value = kept_ref[...] + sent_ref[...].astype(F32)
        out_ref[...] = value[:rows].astype(BF)
        small_ref[...] = value[rows:]

    return call(kernel, "add_last", (kept, sent, *after), [VM] * 2 + [ANY] * len(after), [shape((rows, 256)), shape((extra, 256), F32)])


def unpack_shards(me, shards, shapes, layout):
    n = len(shards)
    chips = n // 2

    def kernel(me_ref, *refs):
        parts, outs = refs[:n], refs[n:]
        me = me_ref[0]
        for k in range(n):
            chip, core = (me >> 1) ^ (k >> 1), (me & 1) ^ (k & 1)
            for out, R, left, C, at in layout:
                size, half = R // chips, C // 2
                row = pl.multiple_of(chip * size, size)
                for c in range(half // 256):
                    col = pl.multiple_of(left + core * half + 256 * c, 256)
                    value = parts[k][at + c * size : at + (c + 1) * size, :].astype(F32)
                    outs[out][pl.ds(row, size), pl.ds(col, 256)] = value

    return call(kernel, "unpack_shards", (me, *shards), [SM] + [VM] * n, [shape(s, F32) for s in shapes])


def exchange(x, axis, k):
    size = lax.axis_size(axis)
    return lax.ppermute(x, axis, [(i, i ^ k) for i in range(size)])


def once(x, after):
    return lax.optimization_barrier((x, after))[0]


def gather(x, after=None):
    n = lax.axis_size("seq")
    parts = {0: x}
    for k in range(2, n, 2):
        parts[k] = exchange(x, "seq", k)
    for k in range(0, n, 2):
        held = parts[k] if after is None or k == 0 else once(parts[k], after)
        parts[k + 1] = exchange(held, "seq", 1)
    return [parts[k] for k in range(n)]


def across_chips(mine):
    return [mine[0]] + [exchange(mine[j], "seq", 2 * j) for j in range(1, len(mine))]


def plain_weights(pairs, small):
    zsize, zme = lax.axis_size("rows"), lax.axis_index("rows")
    outs = []
    for left, right, turned in pairs:
        whole = lax.psum(dot(left, right, ((1,) if turned else (0,), (0,))), ("seq", "rows"))
        size = whole.shape[0] // zsize
        outs.append(lax.dynamic_slice_in_dim(whole, zme * size, size, 0))
    whole = lax.psum(small, ("seq", "rows"))
    parts = []
    for x, dim in ((whole[:NTAGS], 0), (whole[NTAGS : NTAGS + 4].reshape(-1), 0), (whole[NTAGS + 4 :], 1)):
        size = x.shape[dim] // zsize
        parts.append(lax.dynamic_slice_in_dim(x, zme * size, size, dim))
    return outs, parts


def local(
    dec_input, encoded, segment_ids, pair_tags, enc_lengths, out_grad, tag_table, self_qkv, self_out, cross_query,
    cross_kv, cross_out, ffn_in, ffn_in_bias, ffn_out, ffn_out_bias, norm_gain, norm_bias,
):
    n, zsize = lax.axis_size("seq"), lax.axis_size("rows")
    chips = n // 2
    me, zme = lax.axis_index("seq").astype(jnp.int32)[None], lax.axis_index("rows").astype(jnp.int32)[None]
    mirror = n - 1
    weights = zsize == 4 and 512 // (zsize * chips) >= 16
    square = (512, 512)
    cut1 = Cut(chips, zsize, 0, [(512, 2048), (2048, 512)]) if weights else None
    cut2 = Cut(chips, zsize, 512, [(512, 1024), square, square, square] if weights else [])
    cut3 = Cut(chips, zsize, 512, [square] * 3 if weights else [], 16 if weights else 0)

    message = join_tokens(dec_input[0], segment_ids)
    b_in, b_out = ffn_in_bias[None], ffn_out_bias[None]
    oga, ogb, both = prepare(message, out_grad[0], encoded[0], exchange(encoded[0], "seq", 1), b_in, b_out)
    xs = gather(message, oga)
    both = once(both, xs[2::2])
    encs = [both] + [exchange(both, "seq", k) for k in range(2, n, 2)]
    ogb = exchange(once(ogb, xs[2::2]), "seq", mirror)
    (low_all, K, V, khot, qhotT, qT, oT, lse, hat1, scale1, first, first_low, cqT, mixT, start_low) = self_front(
        me, pair_tags[0], xs, tag_table, self_qkv, self_out, cross_query, norm_gain, norm_bias
    )
    terms1, (la, lb, hidden, second_low, g_ffn, g_pre, g_mid, g_cb, gcT, cdelta, clse, cmixT, vec2, dib, ehot, ek, ev) = middle(
        cut1, me, enc_lengths[0], encs, cross_kv, cqT, qhotT, first, cross_out, ffn_in, ffn_out,
        b_in, b_out, norm_gain, norm_bias, oga, ogb,
    )
    layer_out = jnp.concatenate([la, exchange(lb, "seq", mirror)])[None]
    token = g_mid
    if weights:
        sums1 = add_core(terms1[:-1], exchange(terms1[-1], "seq", 1), token)
        token = sums1[0]
        sums1 = across_chips(sums1)
    terms2, (g_start, gmT, delta, vec1, *back2) = cross_back(
        cut2, weights, me, ek, ev, token, encs, cross_kv, cqT, ehot, qhotT, gcT, clse, cdelta, g_mid, cross_query,
        hat1, scale1, norm_gain, self_out, oT, cmixT, g_cb, first_low, mixT,
    )
    token = g_start
    if weights:
        near1, far1 = add_chips(cut1, zme, sums1, g_start)
        token = near1
    sums2 = add_core(terms2[:-1], exchange(terms2[-1], "seq", 1), token)
    token = sums2[0]
    sums2 = across_chips(sums2)
    if weights:
        got1 = exchange(once(far1, token), "rows", 2)
    terms3, (small, *back3) = self_back(
        cut3, weights, me, pair_tags[0], token, low_all, K, V, khot, qT, qhotT, gmT, lse, delta, self_qkv,
        g_start, start_low, vec1, vec2, dib,
    )
    if weights:
        near2, far2, encoded_grad, send1, kept1 = add_chips(cut2, zme, sums2, terms3[0], (near1, got1))
        sums3 = add_core(terms3[:-1], exchange(terms3[-1], "seq", 1), near2)
        got2 = exchange(once(far2, sums3[0]), "rows", 2)
        sent1 = exchange(once(send1, sums3[0]), "rows", 1)
        sums3 = across_chips(sums3)
        send2, kept2, share1 = add_far(near2, got2, kept1, sent1)
        share12 = add_near(share1, kept2, exchange(send2, "rows", 1))
        near3, far3, input_grad = add_chips(cut3, zme, sums3, share12)
        got3 = exchange(far3, "rows", 2)
        shards12 = gather(once(share12, near3))
        send3, kept3 = add_far(near3, got3)
        share3, small = add_last(kept3, exchange(send3, "rows", 1), 16, shards12[2::2])
        ins, outs = 512 // zsize, 2048 // zsize

        def layout(places):
            found, at = [], 0
            for out, R, left, C in places:
                found.append((out, R, left, C, at))
                at += R // chips * (C // 512)
            return found

        places = [(0, ins, 0, 2048), (1, outs, 0, 512), (2, ins, 0, 1024)] + [(j, ins, 0, 512) for j in (3, 4, 5)]
        shapes = [(ins, 2048), (outs, 512), (ins, 1024), (ins, 512), (ins, 512), (ins, 512)]
        d_fi, d_fo, d_ckv, d_co, d_cq, d_so = unpack_shards(me, shards12, shapes, layout(places))
        shards3 = gather(share3, d_fi)
        places = [(0, ins, 512 * j, 512) for j in range(3)]
        d_qkv = unpack_shards(me, shards3, [(ins, 1536)], layout(places))[0]
        tags, wide, lanes = NTAGS // zsize, outs // 256, 512 // zsize
        d_table = jnp.concatenate([small[0:tags], small[tags : 2 * tags]], axis=1)
        d_inner = small[2 * tags : 2 * tags + wide].reshape(-1)
        vectors = small[2 * tags + wide : 2 * tags + wide + 4].reshape(8, lanes)
    else:
        encoded_grad, input_grad = (
            total([jnp.concatenate([t[:BLK], t[BLK:]], axis=1) for t in terms])
            for terms in (sums2, across_chips(add_core(terms3[:-1], exchange(terms3[-1], "seq", 1), small)))
        )
        (edkv, dcq, g_branch), (dkv, dq) = back2, back3
        enc_all = jnp.concatenate(encs)
        pairs = [
            (second_low, g_pre, False), (hidden, g_ffn, False), (enc_all, edkv, False), (cmixT, g_cb, True),
            (first_low, dcq, False), (mixT, g_branch, True), (start_low, dq, False), (low_all, dkv, False),
        ]
        small = jnp.concatenate([small[:NTAGS], dib.reshape(4, 512), small[NTAGS:]])
        (d_fi, d_fo, d_ckv, d_co, d_cq, d_so, dq, dkv), (d_table, d_inner, vectors) = plain_weights(pairs, small)
        d_qkv = jnp.concatenate([dq, dkv], axis=1)
    return (
        layer_out, input_grad[None], encoded_grad[None], d_table, d_qkv, d_so, d_cq, d_ckv, d_co, d_fi, d_inner, d_fo,
        vectors[6], vectors[0:3], vectors[3:6],
    )


def solution(mesh):
    tokens = P("rows", "seq", None)
    placed = (tokens, tokens, P("rows", "seq"), P("rows", None), P("rows", None), tokens) + (P(),) * 12
    rows = P("rows", None)
    return jax.shard_map(
        local,
        mesh=mesh,
        in_specs=placed,
        out_specs=(tokens, tokens, tokens)
        + (rows,) * 7
        + (P("rows"), rows, P("rows"), P(None, "rows"), P(None, "rows")),
        check_vma=False,
    )
```

```python
import jax
import jax.numpy as jnp
from jax import lax
from jax.experimental import pallas as pl
from jax.experimental.pallas import tpu as pltpu
from jax.sharding import PartitionSpec as P

F32 = jnp.float32
BF = jnp.bfloat16
SEGS = 4
NTAGS = 16
BLK = 256
HALF = 128
TILE = 512
BIG = -1e30
EPS = 1e-5
TN = ((0,), (0,))
NT = ((1,), (1,))
VM = pl.BlockSpec(memory_space=pltpu.VMEM)
SM = pl.BlockSpec(memory_space=pltpu.SMEM)
ANY = pl.BlockSpec(memory_space=pl.ANY)
HB = pl.BlockSpec(memory_space=pltpu.HBM)
SENT = "sent"
TOKEN = jax.ShapeDtypeStruct((8, 128), F32)


def shape(dims, dtype=BF):
    return jax.ShapeDtypeStruct(dims, dtype)


TIMES = {
    "self_front": 16, "middle": 20, "cross_back": 18, "self_back": 18, "add_core": 3, "add_chips": 20, "prepare": 2,
    "join_tokens": 2, "add_far": 2, "add_near": 2, "add_last": 2, "unpack_shards": 3,
}


LIMITS = {
    "self_front": 20, "middle": 32, "cross_back": 28, "self_back": 34, "add_core": 8, "add_chips": 10, "prepare": 4,
    "join_tokens": 4, "add_far": 4, "add_near": 4, "add_last": 4, "unpack_shards": 12,
}


class Outgoing:
    def __init__(self, ref, target, sems):
        self.ref, self.target, self.sems, self.copies = ref, target, sems, []

    def send(self, *index):
        pair = (self.ref.at[index], self.target.at[index]) if index else (self.ref, self.target)
        self.copies.append(pltpu.make_async_copy(*pair, self.sems.at[len(self.copies)]))
        self.copies[-1].start()


def call(kernel, name, ins, specs, outs, out_specs=None, scratch=(), blocks=8):
    outs, out_specs = list(outs), list(out_specs or (VM,) * len(outs))
    ins = [pltpu.with_memory_space_constraint(x, pltpu.HBM) if spec is HB else x for x, spec in zip(ins, specs)]
    sent = [j for j, spec in enumerate(out_specs) if spec is SENT]
    more = [pltpu.VMEM(outs[j].shape, outs[j].dtype) for j in sent]
    more += [pltpu.SemaphoreType.DMA((len(sent), 2))] if sent else []

    def body(*refs):
        if not sent:
            return kernel(*refs)
        refs, mine, sems = list(refs[: -len(more)]), refs[-len(more) : -1], refs[-1]
        going = []
        for at, j in enumerate(sent):
            going.append(Outgoing(mine[at], refs[len(ins) + j], sems.at[at]))
            refs[len(ins) + j] = going[-1]
        kernel(*refs)
        for out in going:
            if not out.copies:
                out.send()
        for out in going:
            for copy in out.copies:
                copy.wait()

    return pl.pallas_call(
        body,
        out_shape=tuple(pltpu.HBM(o.shape, o.dtype) if s in (SENT, HB) else o for o, s in zip(outs, out_specs)),
        in_specs=list(specs),
        out_specs=tuple(HB if spec is SENT else spec for spec in out_specs),
        scratch_shapes=list(scratch) + more,
        compiler_params=pltpu.CompilerParams(vmem_limit_bytes=min(60, LIMITS[name] * blocks // 8) << 20),
        cost_estimate=pl.CostEstimate(flops=TIMES[name] * 10**9, bytes_accessed=1, transcendentals=0),
        name=name,
    )(*ins)


def dot(a, b, dims=((1,), (0,))):
    return lax.dot_general(a, b, (dims, ((), ())), preferred_element_type=F32)


def total(terms):
    out = terms[0].astype(F32)
    for term in terms[1:]:
        out = out + term.astype(F32)
    return out


def build_blocks(src_ref, extra_ref, dst_ref):
    z = jnp.zeros((64, HALF), BF)
    for p in range(4):
        for h in range(2):
            c = slice(h * HALF, (h + 1) * HALF)
            dst_ref[2 * p + h, 0:64, :] = jnp.concatenate([src_ref[128 * p : 128 * p + 64, c], z], 1)
            dst_ref[2 * p + h, 64:128, :] = jnp.concatenate([z, src_ref[128 * p + 64 : 128 * p + 128, c]], 1)
            if extra_ref is not None:
                e = extra_ref[:, c]
                dst_ref[2 * p + h, 128:144, :] = jnp.concatenate([e, e], 1)
                dst_ref[2 * p + h, 144:256, :] = jnp.zeros((112, 256), BF)


def split_heads(j, a, o_ref):
    p, h = j // 2, j % 2
    o_ref[128 * p : 128 * p + 64, h * HALF : (h + 1) * HALF] = a[0:64, 0:HALF]
    o_ref[128 * p + 64 : 128 * p + 128, h * HALF : (h + 1) * HALF] = a[64:128, HALF:]


def cross_forward(q_ref, k_ref, vt_ref, khot_ref, qhot_ref, o_ref, lse_ref, qb):
    build_blocks(q_ref, qhot_ref, qb)
    tiles = k_ref.shape[0] // TILE
    for j in range(8):
        p = j // 2

        def scores(t):
            rows = pl.ds(t * TILE, TILE)
            kt = jnp.concatenate([k_ref[rows, 128 * p : 128 * p + 128], khot_ref[rows, :]], 1)
            return dot(kt, qb[j])

        top = jnp.max(scores(0), axis=0, keepdims=True)
        for t in range(1, tiles):
            top = jnp.maximum(top, jnp.max(scores(t), axis=0, keepdims=True))
        whole = jnp.zeros((1, 256), F32)
        acc = jnp.zeros((128, 256), F32)
        for t in range(tiles):
            e = jnp.exp(scores(t) - top)
            whole = whole + jnp.sum(e, axis=0, keepdims=True)
            acc = acc + dot(vt_ref[128 * p : 128 * p + 128, t * TILE : (t + 1) * TILE], e.astype(BF))
        lse_ref[j] = top + jnp.log(whole)
        split_heads(j, acc * (1.0 / whole), o_ref)


def cross_backward(copies, q_ref, k_ref, v_ref, khot_ref, qhot_ref, do_ref, lse_ref, dl_ref, dq_ref, dkv_ref, qb, db):
    build_blocks(q_ref, qhot_ref, qb)
    build_blocks(do_ref, None, db)
    size = min(2048, k_ref.shape[1])
    for p in range(4):
        lanes = slice(128 * p, 128 * p + 128)
        dq = [0.0, 0.0]
        for copy in copies[p]:
            copy.wait()
        for t in range(k_ref.shape[1] // size):
            rows = slice(t * size, (t + 1) * size)
            k = k_ref[p, rows, :]
            k_turned = k.T
            kt = jnp.concatenate([k, khot_ref[rows, :]], 1)
            dk = dv = 0.0
            for h in range(2):
                j = 2 * p + h
                pr = jnp.exp(dot(kt, qb[j]) - lse_ref[j])
                dp = dot(v_ref[p, rows, :], db[j])
                ds = (pr * (dp - dl_ref[j])).astype(BF)
                dv += dot(pr.astype(BF), db[j], NT)
                dk += dot(ds, qb[j, 0:128, :], NT)
                dq[h] += dot(k_turned, ds)
            dkv_ref[rows, lanes] = dk.astype(BF)
            dkv_ref[rows, 512 + 128 * p : 640 + 128 * p] = dv.astype(BF)
        for h in range(2):
            split_heads(2 * p + h, dq[h] * 0.125, dq_ref)


def work_item(t, i, blocks):
    first = (i + 2) // 2
    second = (t >= first).astype(jnp.int32)
    tile = t - second * first
    start = jnp.where(second == 1, (blocks - 1 - i) * BLK + HALF, i * BLK)
    return second, tile, start - tile * TILE


def relative_positions(swap):
    k = lax.broadcasted_iota(jnp.int32, (TILE, 2 * HALF), 0)
    q = lax.broadcasted_iota(jnp.int32, (TILE, 2 * HALF), 1) & (HALF - 1)
    return (k ^ swap) - q


def self_forward(blocks, i, q_ref, k_ref, vt_ref, khot_ref, qhot_ref, o_ref, lse_ref, qb, m_s, l_s, acc):
    build_blocks(q_ref, qhot_ref, qb)
    swap = (i & 1) * BLK
    items = blocks // 2 + 1
    m_s[...] = jnp.full(m_s.shape, -3e38, F32)
    l_s[...] = jnp.zeros(l_s.shape, F32)
    acc[...] = jnp.zeros(acc.shape, F32)

    def scores(t, p):
        h, tile, offset = work_item(t, i, blocks)
        r0 = pl.multiple_of((tile ^ (i >> 1)) * TILE, TILE)
        kt = jnp.concatenate([k_ref[pl.ds(r0, TILE), 128 * p : 128 * p + 128], khot_ref[pl.ds(r0, TILE), :]], 1)
        return jnp.where(relative_positions(swap) <= offset, dot(kt, qb[2 * p + h]), BIG), 2 * p + h, r0

    @pl.loop(0, items)
    def _(t):
        for p in range(4):
            s, j, _ = scores(t, p)
            m_s[j] = jnp.maximum(m_s[j], jnp.max(s, axis=0, keepdims=True))

    @pl.loop(0, items)
    def _(t):
        for p in range(4):
            s, j, r0 = scores(t, p)
            e = jnp.exp(s - m_s[j])
            l_s[j] += jnp.sum(e, axis=0, keepdims=True)
            acc[j] += dot(vt_ref[128 * p : 128 * p + 128, pl.ds(r0, TILE)], e.astype(BF))

    for j in range(8):
        lse_ref[j] = m_s[j] + jnp.log(l_s[j])
        split_heads(j, acc[j] * (1.0 / l_s[j]), o_ref)


def self_backward(
    blocks, i, q_ref, k_ref, kt_ref, v_ref, khot_ref, qhot_ref, do_ref, lse_ref, dl_ref, dq_ref, dkv_ref,
    qb, db, dqa, dka, dva,
):
    build_blocks(q_ref, qhot_ref, qb)
    build_blocks(do_ref, None, db)
    swap = (i & 1) * BLK
    dqa[...] = jnp.zeros(dqa.shape, F32)
    dka[...] = jnp.zeros(dka.shape, F32)
    dva[...] = jnp.zeros(dva.shape, F32)

    @pl.loop(0, blocks // 2 + 1)
    def _(t):
        h, tile, offset = work_item(t, i, blocks)
        rows = pl.ds(pl.multiple_of((tile ^ (i >> 1)) * TILE, TILE), TILE)
        hot = khot_ref[rows, :]
        for p in range(4):
            j = 2 * p + h
            lanes = slice(128 * p, 128 * p + 128)
            s = dot(jnp.concatenate([k_ref[rows, lanes], hot], 1), qb[j])
            pr = jnp.exp(jnp.where(relative_positions(swap) <= offset, s, BIG) - lse_ref[j])
            dp = dot(v_ref[rows, lanes], db[j])
            ds = (pr * (dp - dl_ref[j])).astype(BF)
            dva[rows, lanes] += dot(pr.astype(BF), db[j], NT)
            dka[rows, lanes] += dot(ds, qb[j, 0:128, :], NT)
            dqa[j] += dot(kt_ref[lanes, rows], ds)

    dkv_ref[:, 0:512] = dka[...].astype(BF)
    dkv_ref[:, 512:1024] = dva[...].astype(BF)
    for j in range(8):
        split_heads(j, dqa[j] * 0.125, dq_ref)


def norm_forward(v, gain, bias):
    centered = v - jnp.mean(v, axis=-1, keepdims=True)
    scale = lax.rsqrt(jnp.mean(centered * centered, axis=-1, keepdims=True) + EPS)
    hat = centered * scale
    return hat * gain + bias, hat, scale


def norm_backward(g, hat, scale, gain):
    gh = g * gain
    out = scale * (gh - jnp.mean(gh, axis=-1, keepdims=True) - hat * jnp.mean(gh * hat, axis=-1, keepdims=True))
    return out, jnp.sum(g * hat, axis=0, keepdims=True), jnp.sum(g, axis=0, keepdims=True)


def gelu_both(x):
    c = 0.7978845608028654
    sq = x * x
    t = jnp.tanh(c * x * (1 + 0.044715 * sq))
    half = 0.5 * (1 + t)
    return x * half, half + 0.5 * x * (1 - t * t) * (c * (1 + 3 * 0.044715 * sq))


def inner_rows(g_refT, o_ref, dl_ref):
    for p in range(4):
        both = []
        for a in range(2):
            rows = slice(128 * p + 64 * a, 128 * p + 64 * a + 64)
            both.append(jnp.sum(g_refT[rows, :].astype(F32) * o_ref[rows, :], axis=0, keepdims=True))
        for h in range(2):
            cols = slice(h * HALF, (h + 1) * HALF)
            dl_ref[2 * p + h] = jnp.concatenate([both[0][:, cols], both[1][:, cols]], 1)


class Cut:
    def __init__(self, chips, zsize, tokens, sizes, extra=0):
        self.chips, self.zsize, self.tokens, self.extra = chips, zsize, tokens, extra
        self.at, rows = [], 0
        for R, C in sizes:
            self.at.append(rows)
            rows += R // (zsize * chips) * (C // 512)
        self.per_z = rows + extra
        self.rows = tokens + zsize * self.per_z

    def write(self, index, keep, me, evens, odd_ref):
        R, C = keep.shape
        core, chip = me & 1, me >> 1
        size, half = R // (self.zsize * self.chips), C // 2
        for turn in range(2):
            side = core if turn == 0 else 1 - core
            for j in range(self.chips):
                for z in range(self.zsize):
                    row = pl.multiple_of(z * (R // self.zsize) + (chip ^ j) * size, size)
                    for c in range(half // 256):
                        left = pl.multiple_of(side * half + 256 * c, 256)
                        at = self.tokens + z * self.per_z + self.at[index] + c * size
                        piece = keep[pl.ds(row, size), pl.ds(left, 256)]
                        if turn == 0:
                            evens[j][at : at + size, :] = piece
                        else:
                            odd_ref[j, at : at + size, :] = piece

    def write_tokens(self, r, part, evens, odd_ref):
        for c in range(2):
            piece = part[:, 256 * c : 256 * c + 256]
            if r % 2:
                odd_ref[r // 2, BLK * c : BLK * c + BLK, :] = piece
            else:
                evens[r // 2][BLK * c : BLK * c + BLK, :] = piece

    def write_extra(self, z, part, evens, odd_ref):
        at = self.tokens + z * self.per_z + self.per_z - self.extra
        for j in range(self.chips):
            evens[j][at : at + self.extra, :] = part
            odd_ref[j, at : at + self.extra, :] = part

    def outs(self):
        return [shape((self.rows, 256))] * self.chips + [shape((self.chips, self.rows, 256))]


def join_tokens(x, seg):
    def kernel(x_hbm, seg_hbm, out, seg_s, sems):
        loads = [
            pltpu.make_async_copy(x_hbm, out.ref.at[0:BLK, :], sems.at[0]),
            pltpu.make_async_copy(seg_hbm, seg_s, sems.at[1]),
        ]
        for copy in loads:
            copy.start()
        for copy in loads[::-1]:
            copy.wait()
            if copy is loads[1]:
                row = jnp.concatenate([seg_s[...].astype(F32), jnp.zeros((1, 256), F32)], 1)
                out.ref[BLK:, :] = jnp.broadcast_to(row, (16, 512)).astype(BF)

    scratch = [pltpu.VMEM((1, 256), jnp.int32), pltpu.SemaphoreType.DMA((2,))]
    return call(kernel, "join_tokens", (x, seg), [HB] * 2, [shape((BLK + 16, 512))], [SENT], scratch)[0]


def prepare(after, grad, *rest):
    def kernel(g_ref, *refs):
        ga_ref, gb_ref = refs[-2:]
        ga_ref[...] = g_ref[0:HALF, :]
        gb_ref[...] = g_ref[HALF:, :]

    ins = (grad, after, *rest)
    return call(
        kernel, "prepare", ins, [VM, HB] + [ANY] * (len(ins) - 2), [shape((HALF, 512)), shape((HALF, 512))], [VM, VM]
    )


def self_front_kernel(n, me_ref, tag_ref, *refs):
    xs, refs = refs[:n], refs[n:]
    (table_ref, w_ref, so_ref, cqw_ref, gain_ref, bias_ref,
     low_o, k_o, v_o, khot_o, qhot_ref, qT_o, oT_ref, lse_o, hat_ref, scale_ref, first_ref,
     flow_ref, cqT_ref, mixT_ref, slow_o, vt_s, start_s, qb, m_s, l_s, acc) = refs
    low_s, k_s, v_s, khot_s, qT_ref, lse_ref = (out.ref for out in (low_o, k_o, v_o, khot_o, qT_o, lse_o))
    segs = [x[BLK : BLK + 8, 0:BLK].astype(F32)[0:1].astype(jnp.int32) for x in xs]
    table = table_ref[...].astype(F32)
    ids = lax.broadcasted_iota(jnp.int32, (NTAGS, 512), 0)
    rows = [jnp.sum(jnp.where(ids == tag_ref[s], table, 0.0), axis=0, keepdims=True) for s in range(SEGS)]
    tag_rows = jnp.concatenate(rows + [jnp.zeros((128 - SEGS, 512), F32)], 0).astype(BF)
    for r in range(n):
        at = slice(r * BLK, (r + 1) * BLK)
        hotT = (lax.broadcasted_iota(jnp.int32, (128, BLK), 0) == segs[r]).astype(F32)
        hot = hotT.T
        khot_s[at, :] = hot.astype(BF)
        start = xs[r][0:BLK, :].astype(F32) + dot(hot.astype(BF), tag_rows)
        low = start.astype(BF)
        low_s[at, :] = low
        if r == 0:
            start_s[0:HALF, :] = start[0:HALF]
        if r == n - 1:
            start_s[HALF:, :] = start[HALF:]
        k_s[at, :] = dot(low, w_ref[:, 512:1024]).astype(BF)
        v = dot(low, w_ref[:, 1024:1536]).astype(BF)
        v_s[at, :] = v
        vt_s[:, at] = v.T
    for out in (low_o, k_o, v_o, khot_o):
        out.send()
    seg = jnp.concatenate([segs[0][:, 0:HALF], segs[n - 1][:, HALF:]], 1)
    ids = lax.broadcasted_iota(jnp.int32, (16, BLK), 0)
    qhot_ref[...] = jnp.where((ids != seg) & (ids < SEGS), BIG, 0.0).astype(BF)
    slow = start_s[...].astype(BF)
    slow_o.ref[...] = slow
    qT_ref[...] = (dot(slow, w_ref[:, 0:512]) * 0.125).astype(BF).T
    slow_o.send()
    qT_o.send()
    self_forward(n, me_ref[0], qT_ref, k_s, vt_s, khot_s, qhot_ref, oT_ref, lse_ref, qb, m_s, l_s, acc)
    mixT = oT_ref[...].astype(BF)
    mixT_ref[...] = mixT
    first, hat, scale = norm_forward(
        start_s[...] + dot(mixT, so_ref[...], TN), gain_ref[0:1, :].astype(F32), bias_ref[0:1, :].astype(F32)
    )
    hat_ref[...] = hat
    scale_ref[...] = jnp.broadcast_to(scale, (BLK, 128))
    first_ref[...] = first
    first_low = first.astype(BF)
    flow_ref[...] = first_low
    cqT_ref[...] = (dot(first_low, cqw_ref[...]) * 0.125).astype(BF).T


def self_front(me, tags, xs, table, w, so, cqw, gain, bias):
    n = len(xs)
    S = n * BLK
    big = [shape((S, 512)), shape((S, 512)), shape((S, 512)), shape((S, 128))]
    outs = big + [
        shape((16, BLK)), shape((512, BLK)), shape((512, BLK), F32), shape((8, 1, BLK), F32), shape((BLK, 512), F32),
        shape((BLK, 128), F32), shape((BLK, 512), F32), shape((BLK, 512)), shape((512, BLK)), shape((512, BLK)),
        shape((BLK, 512)),
    ]
    scratch = [
        pltpu.VMEM((512, S), BF), pltpu.VMEM((BLK, 512), F32), pltpu.VMEM((8, 256, 256), BF),
        pltpu.VMEM((8, 1, 256), F32), pltpu.VMEM((8, 1, 256), F32), pltpu.VMEM((8, 128, 256), F32),
    ]
    kinds = [SENT] * 4 + [VM, SENT, VM, SENT] + [VM] * 6 + [SENT]
    return call(
        lambda *refs: self_front_kernel(n, *refs), "self_front", (me, tags, *xs, table, w, so, cqw, gain, bias),
        [SM, SM] + [VM] * (n + 6), outs, kinds, scratch, n,
    )


def middle_kernel(n, cut, me_ref, len_ref, *refs):
    encs, refs = refs[:n], refs[n:]
    (w_ref, cqT_ref, qhot_ref, first_ref, co_ref, fi_ref, fo_ref, bi_ref, bo_ref, gain_ref, bias_ref,
     oga_ref, ogb_ref, *refs) = refs
    if cut:
        evens, (odd_ref, *refs) = refs[: cut.chips], refs[cut.chips :]
    (la_ref, lb_ref, gmid_ref, gcb_ref, gcT_ref, dl_ref, lse_ref, cmixT_ref, vec_o, dib_o, khot_ref, k_ref, v_ref,
     hid_ref, slow_ref, gffn_ref, gpre_ref, k_s, v_s, vt_s, oT_s, slope_s, qb, fi_s, fo_s, sems) = refs
    me, vec_ref, dib_ref = me_ref[0], vec_o.ref, dib_o.ref
    e0 = len_ref[0]
    e1 = e0 + len_ref[1]
    e2 = e1 + len_ref[2]
    for r in range(n):
        at = slice(r * BLK, (r + 1) * BLK)
        pos = lax.broadcasted_iota(jnp.int32, (BLK, 128), 0) + (me ^ r) * BLK
        seg = (pos >= e0).astype(jnp.int32) + (pos >= e1).astype(jnp.int32) + (pos >= e2).astype(jnp.int32)
        khot_ref[at, :] = (lax.broadcasted_iota(jnp.int32, (BLK, 128), 1) == seg).astype(F32).astype(BF)
        enc = encs[r][...]
        k_s[at, :] = dot(enc, w_ref[:, 0:512]).astype(BF)
        v = dot(enc, w_ref[:, 512:1024]).astype(BF)
        v_s[at, :] = v
        vt_s[:, at] = v.T
    copies = [pltpu.make_async_copy(k_s, k_ref, sems.at[0]), pltpu.make_async_copy(v_s, v_ref, sems.at[1])]
    for copy in copies:
        copy.start()
    cross_forward(cqT_ref, k_s, vt_s, khot_ref, qhot_ref, oT_s, lse_ref, qb)
    cmixT = oT_s[...].astype(BF)
    cmixT_ref[...] = cmixT
    gains = [gain_ref[j : j + 1, :].astype(F32) for j in range(3)]
    shifts = [bias_ref[j : j + 1, :].astype(F32) for j in range(3)]
    second, hat2, scale2 = norm_forward(first_ref[...] + dot(cmixT, co_ref[...], TN), gains[1], shifts[1])
    second_low = second.astype(BF)
    slow_ref[...] = second_low
    out = second + bo_ref[...].astype(F32)
    for c in range(4):
        cols = slice(512 * c, 512 * c + 512)
        act, slope = gelu_both(dot(second_low, fi_ref[:, cols]) + bi_ref[:, cols].astype(F32))
        hidden = act.astype(BF)
        hid_ref[:, cols] = hidden
        slope_s[:, cols] = slope
        out = out + dot(hidden, fo_ref[cols, :])
    result, hat3, scale3 = norm_forward(out, gains[2], shifts[2])
    la_ref[...] = result[0:HALF].astype(BF)
    lb_ref[...] = result[HALF:].astype(BF)
    og = jnp.concatenate([oga_ref[...], ogb_ref[...]], 0).astype(F32)
    g3, gg3, gb3 = norm_backward(og, hat3, scale3, gains[2])
    g_ffn = g3.astype(BF)
    gffn_ref[...] = g_ffn
    d_out_bias = jnp.sum(g_ffn.astype(F32), axis=0, keepdims=True)
    g2 = g3
    for c in range(4):
        cols = slice(512 * c, 512 * c + 512)
        g_pre = (dot(g_ffn, fo_ref[cols, :], NT) * slope_s[:, cols]).astype(BF)
        gpre_ref[:, cols] = g_pre
        dib_ref[:, cols] = jnp.sum(g_pre.astype(F32), axis=0, keepdims=True)
        g2 = g2 + dot(g_pre, fi_ref[:, cols], NT)
        if cut:
            fi_s[:, cols] = dot(second_low, g_pre, TN).astype(BF)
            fo_s[cols, :] = dot(hid_ref[:, cols], g_ffn, TN).astype(BF)
    g_mid, gg2, gb2 = norm_backward(g2, hat2, scale2, gains[1])
    gmid_ref[...] = g_mid
    g_cb = g_mid.astype(BF)
    gcb_ref[...] = g_cb
    gcT_ref[...] = dot(co_ref[...], g_cb, NT).astype(BF)
    inner_rows(gcT_ref, oT_s, dl_ref)
    vec_ref[...] = jnp.concatenate([gg2, gb2, gg3, gb3, d_out_bias, jnp.zeros((3, 512), F32)], 0)
    if cut:
        cut.write(0, fi_s, me, evens, odd_ref)
        cut.write(1, fo_s, me, evens, odd_ref)
    for copy in copies:
        copy.wait()


def middle(cut, me, lens, encs, *rest):
    n = len(encs)
    S = n * BLK
    outs = (cut.outs() if cut else []) + [
        shape((HALF, 512)), shape((HALF, 512)), shape((BLK, 512), F32), shape((BLK, 512)), shape((512, BLK)),
        shape((8, 1, 256), F32), shape((8, 1, 256), F32), shape((512, BLK)), shape((8, 512), F32),
        shape((1, 2048), F32), shape((S, 128)), shape((S, 512)), shape((S, 512)),
    ]
    hold = [shape((BLK, 2048)), shape((BLK, 512)), shape((BLK, 512)), shape((BLK, 2048))]
    kinds = [VM] * (len(outs) - 5) + [SENT] * 2 + [VM] + [HB] * 2
    plain = [] if cut else hold
    outs += plain
    kinds += [VM] * len(plain)
    scratch = ([pltpu.VMEM(x.shape, BF) for x in hold] if cut else []) + [
        pltpu.VMEM((S, 512), BF), pltpu.VMEM((S, 512), BF), pltpu.VMEM((512, S), BF), pltpu.VMEM((512, BLK), F32),
        pltpu.VMEM((BLK, 2048), F32), pltpu.VMEM((8, 256, 256), BF), pltpu.VMEM((512, 2048), BF),
        pltpu.VMEM((2048, 512), BF), pltpu.SemaphoreType.DMA((2,)),
    ]
    got = call(
        lambda *refs: middle_kernel(n, cut, *refs), "middle", (me, lens, *encs, *rest),
        [SM, SM] + [VM] * (n + 13), outs, kinds, scratch, n,
    )
    first = len(cut.outs()) if cut else 0
    return got[:first], got[first:]


def cross_back_kernel(n, cut, weights, me_ref, *refs):
    half = n // 2
    (k_hbm, v_hbm, _, *refs) = refs
    encs, refs = refs[:n], refs[n:]
    (w_ref, cqT_ref, khot_ref, qhot_ref, gcT_ref, lse_ref, dl_ref, gmid_ref, cqw_ref, hat_ref, scale_ref, gain_ref,
     so_ref, oT_ref, cmixT_ref, gcb_ref, flow_ref, mixT_ref, *refs) = refs
    going, (odd_ref, gstart, gmT, dl1, vec, *refs) = refs[:half], refs[half:]
    evens = [out.ref for out in going]
    gstart_ref, gmT_ref, dl1_ref, vec_ref = gstart.ref, gmT.ref, dl1.ref, vec.ref
    dkv_ref, dq_ref, gbr_ref, k_s, v_s, dqT_s, qb, db, enc_s, keep, kv_keep, sems = refs
    copies, late = [], []
    for p in range(4):
        lanes = slice(128 * p, 128 * p + 128)
        copies.append([
            pltpu.make_async_copy(k_hbm.at[:, lanes], k_s.at[p], sems.at[2 * p]),
            pltpu.make_async_copy(v_hbm.at[:, lanes], v_s.at[p], sems.at[2 * p + 1]),
        ])
    if weights:
        for j in range(n):
            rows = slice(BLK * j, BLK * (j + 1))
            late.append(pltpu.make_async_copy(encs[j], enc_s.at[rows, :], sems.at[12 + j]))
    for copy in sum(copies, []) + late:
        copy.start()
    cross_backward(
        copies, cqT_ref, k_s, v_s, khot_ref, qhot_ref, gcT_ref, lse_ref, dl_ref, dqT_s, dkv_ref, qb, db
    )
    me = me_ref[0]
    for r in range(n):
        at = slice(r * BLK, (r + 1) * BLK)
        part = dot(dkv_ref[at, :], w_ref[...], NT)
        cut.write_tokens(r, part.astype(BF), evens, odd_ref)
    if weights:
        for out in going:
            out.send(slice(0, 512))
    dq = dqT_s[...].astype(BF).T
    dq_ref[...] = dq
    g1 = gmid_ref[...] + dot(dq, cqw_ref[...], NT)
    g_start, gg1, gb1 = norm_backward(g1, hat_ref[...], scale_ref[:, 0:1], gain_ref[0:1, :].astype(F32))
    gstart_ref[...] = g_start
    g_branch = g_start.astype(BF)
    gbr_ref[...] = g_branch
    gmT_ref[...] = dot(so_ref[...], g_branch, NT).astype(BF)
    inner_rows(gmT_ref, oT_ref, dl1_ref)
    vec_ref[...] = jnp.concatenate([gg1, gb1, jnp.zeros((6, 512), F32)], 0)
    for out in (gstart, gmT, dl1, vec):
        out.send()
    if weights:
        keep[0] = dot(cmixT_ref[...], gcb_ref[...]).astype(BF)
        keep[1] = dot(flow_ref[...], dq_ref[...], TN).astype(BF)
        keep[2] = dot(mixT_ref[...], g_branch).astype(BF)
        for j in range(3):
            cut.write(1 + j, keep.at[j], me, evens, odd_ref)
        for copy in late:
            copy.wait()
        kv_keep[...] = dot(enc_s[...], dkv_ref[...], TN).astype(BF)
        cut.write(0, kv_keep, me, evens, odd_ref)
        for out in going:
            out.send(slice(512, cut.rows))


def cross_back(cut, weights, me, k, v, after, encs, *rest):
    n = len(encs)
    S = n * BLK
    more = [shape((S, 1024)), shape((BLK, 512)), shape((BLK, 512))]
    outs = cut.outs() + [
        shape((BLK, 512), F32), shape((512, BLK)), shape((8, 1, 256), F32), shape((8, 512), F32)
    ] + ([] if weights else more)
    scratch = ([pltpu.VMEM(s.shape, s.dtype) for s in more] if weights else []) + [
        pltpu.VMEM((4, S, 128), BF), pltpu.VMEM((4, S, 128), BF),
        pltpu.VMEM((512, BLK), F32), pltpu.VMEM((8, 256, 256), BF), pltpu.VMEM((8, 128, 256), BF),
        pltpu.VMEM((S if weights else 16, 512), BF), pltpu.VMEM((3, 512, 512), BF), pltpu.VMEM((512, 1024), BF),
        pltpu.SemaphoreType.DMA((12 + n,)),
    ]
    got = call(
        lambda *refs: cross_back_kernel(n, cut, weights, *refs), "cross_back", (me, k, v, after, *encs, *rest),
        [SM] + [HB] * (3 if weights else 2) + [ANY] * (n if weights else n + 1) + [VM] * 18,
        outs, [SENT] * (n // 2) + [VM] + [SENT] * 4 + [VM] * (len(outs) - n // 2 - 5), scratch, n,
    )
    return got[: n // 2 + 1], got[n // 2 + 1 :]


def self_back_kernel(n, cut, weights, me_ref, tag_ref, *refs):
    half = n // 2
    (_, low_hbm, k_s, v_s, khot_s, qT_ref, qhot_ref, gmT_ref, lse_ref, dl_ref, w_ref,
     gstart_ref, slow_ref, vec1_ref, vec2_ref, dib_ref, *refs) = refs
    evens, (odd_ref, small_ref, *refs) = refs[:half], refs[half:]
    (dkv_ref, dq_ref, low_s, kt_s, dqT_s, qb, db, dqa, dka, dva, keep, sems) = refs
    if weights:
        low_copy = pltpu.make_async_copy(low_hbm, low_s, sems.at[0])
        low_copy.start()
    for r in range(n):
        at = slice(r * BLK, (r + 1) * BLK)
        kt_s[:, at] = k_s[at, :].T
    me = me_ref[0]
    self_backward(
        n, me, qT_ref, k_s, kt_s, v_s, khot_s, qhot_ref, gmT_ref, lse_ref, dl_ref, dqT_s, dkv_ref,
        qb, db, dqa, dka, dva,
    )
    dq = dqT_s[...].astype(BF).T
    dq_ref[...] = dq
    mine = gstart_ref[...] + dot(dq, w_ref[:, 0:512], NT)
    sums = jnp.zeros((128, 512), F32)
    for r in range(n):
        at = slice(r * BLK, (r + 1) * BLK)
        part = dot(dkv_ref[at, :], w_ref[:, 512:1536], NT)
        if r == 0:
            part = jnp.concatenate([part[:HALF] + mine[:HALF], part[HALF:]], 0)
        if r == n - 1:
            part = jnp.concatenate([part[:HALF], part[HALF:] + mine[HALF:]], 0)
        part = part.astype(BF)
        sums = sums + dot(khot_s[at, :], part, TN)
        cut.write_tokens(r, part, evens, odd_ref)
    ids = lax.broadcasted_iota(jnp.int32, (NTAGS, 512), 0)
    table = jnp.zeros((NTAGS, 512), F32)
    for s in range(SEGS):
        table = table + jnp.where(ids == tag_ref[s], sums[s : s + 1, :], 0.0)
    v1, v2 = vec1_ref[...], vec2_ref[...]
    vectors = [v1[0:1], v2[0:1], v2[2:3], v1[1:2], v2[1:2], v2[3:4], v2[4:5], jnp.zeros((1, 512), F32)]
    if weights:
        zs = cut.zsize
        wide, lanes, tags = 2048 // zs, 512 // zs, NTAGS // zs
        for z in range(zs):
            rows = []
            for c in range(2):
                rows.append(table[tags * z : tags * (z + 1), 256 * c : 256 * c + 256])
            rows += [dib_ref[:, wide * z + 256 * c : wide * z + 256 * (c + 1)] for c in range(wide // 256)]
            cut_rows = [v[:, lanes * z : lanes * (z + 1)] for v in vectors]
            rows += [jnp.concatenate(cut_rows[2 * c : 2 * c + 2], 1) for c in range(4)]
            used = 2 * tags + wide // 256 + 4
            rows.append(jnp.zeros((16 - used, 256), F32))
            cut.write_extra(z, jnp.concatenate(rows, 0).astype(BF), evens, odd_ref)
        small_ref[...] = jnp.zeros(small_ref.shape, F32)
        keep[:, 0:512] = dot(slow_ref[...], dq_ref[...], TN).astype(BF)
        low_copy.wait()
        keep[:, 512:1536] = dot(low_s[...], dkv_ref[...], TN).astype(BF)
        for j in range(3):
            cut.write(j, keep.at[:, 512 * j : 512 * j + 512], me, evens, odd_ref)
    else:
        small_ref[...] = jnp.concatenate([table] + vectors, 0)


def self_back(cut, weights, me, tags, after, low, k, v, khot, *rest):
    S = k.shape[0]
    n = S // BLK
    more = [shape((S, 1024)), shape((BLK, 512))]
    outs = cut.outs() + [shape((24, 512), F32)] + ([] if weights else more)
    scratch = ([pltpu.VMEM(s.shape, s.dtype) for s in more] if weights else []) + [
        pltpu.VMEM((S if weights else 16, 512), BF), pltpu.VMEM((512, S), BF),
        pltpu.VMEM((512, BLK), F32), pltpu.VMEM((8, 256, 256), BF), pltpu.VMEM((8, 128, 256), BF),
        pltpu.VMEM((8, 128, 256), F32), pltpu.VMEM((S, 512), F32), pltpu.VMEM((S, 512), F32),
        pltpu.VMEM((512, 1536), BF), pltpu.SemaphoreType.DMA((1,)),
    ]
    got = call(
        lambda *refs: self_back_kernel(n, cut, weights, *refs), "self_back",
        (me, tags, after, low, k, v, khot, *rest), [SM, SM, HB, HB] + [VM] * 14, outs, None, scratch, n,
    )
    return got[: n // 2 + 1], got[n // 2 + 1 :]


def add_core(evens, got, after):
    count = len(evens)

    def kernel(*refs):
        ins, got_ref, (first, *outs) = refs[:count], refs[count], refs[count + 2 :]
        for j, out_ref in enumerate([first.ref] + outs):
            out_ref[...] = (ins[j][...].astype(F32) + got_ref[j].astype(F32)).astype(BF)
            if j == 0:
                first.send()

    return call(
        kernel, "add_core", (*evens, got, after), [VM] * (count + 1) + [ANY], [shape(e.shape) for e in evens],
        [SENT] + [VM] * (count - 1),
    )


def add_chips(cut, zme, terms, after, near=None, far=None, pinned=False):
    count, per = len(terms), cut.per_z
    extra = [] if near is None else [near, far]
    base = extra[0].shape[1] if extra else 0

    def kernel(z_ref, *refs):
        ins, (near_ref, far_ref, *outs) = refs[:count], refs[count + len(after) + len(extra) :]
        s, sems = outs[-2:]
        loads = []
        for j in range(count):
            rows = slice(cut.tokens, cut.rows)
            loads.append(pltpu.make_async_copy(ins[j].at[rows, :], s.at[j, rows, :], sems.at[0, j]))
        for j in range(count if cut.tokens else 0):
            rows = slice(0, cut.tokens)
            loads.append(pltpu.make_async_copy(ins[j].at[rows, :], s.at[j, rows, :], sems.at[1, j]))
        for copy in loads:
            copy.start()
        if extra:
            early = refs[count + len(after) : count + len(after) + 2]
            near_ref[:, 0:base, :] = early[0][...]
            far_ref[:, 0:base, :] = early[1][...]
        for copy in loads[:count]:
            copy.wait()
        for k in range(4):
            row = pl.multiple_of(cut.tokens + (z_ref[0] ^ k) * per, 16)
            value = total([s[j, pl.ds(row, per), :] for j in range(count)]).astype(BF)
            (near_ref if k < 2 else far_ref)[k % 2, base : base + per, :] = value
        for copy in loads[count:]:
            copy.wait()
        for c in range(2 if cut.tokens else 0):
            part = total([s[j, BLK * c : BLK * c + BLK, :] for j in range(count)])
            outs[0][:, 256 * c : 256 * c + 256] = part

    outs = [shape((2, base + per, 256)), shape((2, base + per, 256))] + [shape((BLK, 512), F32)] * (cut.tokens > 0)
    return call(
        kernel, "add_chips", (zme, *terms, *after, *extra),
        [SM, HB] + [ANY] * (count - 1) + [HB if pinned else ANY] * len(after) + [VM] * len(extra), outs, None,
        [pltpu.VMEM((count, cut.rows, 256), BF), pltpu.SemaphoreType.DMA((2, count))],
    )


def add_far(near, got):
    def kernel(near_ref, got_ref, send_ref, keep_ref):
        send_ref[...] = (near_ref[1].astype(F32) + got_ref[1].astype(F32)).astype(BF)
        keep_ref[...] = near_ref[0].astype(F32) + got_ref[0].astype(F32)

    outs = [shape(near.shape[1:]), shape(near.shape[1:], F32)]
    return call(kernel, "add_far", (near, got), [VM] * 2, outs)


def add_near(kept, sent):
    def kernel(kept_ref, sent_ref, out_ref):
        out_ref[...] = (kept_ref[...] + sent_ref[...].astype(F32)).astype(BF)

    return call(kernel, "add_near", (kept, sent), [VM] * 2, [shape(kept.shape)])[0]


def add_last(kept, sent, extra, after):
    rows = kept.shape[0] - extra

    def kernel(kept_ref, sent_ref, *refs):
        out_ref, small_ref = refs[-2:]
        value = kept_ref[...] + sent_ref[...].astype(F32)
        out_ref[...] = value[:rows].astype(BF)
        small_ref[...] = value[rows:]

    return call(kernel, "add_last", (kept, sent, *after), [VM] * 2 + [ANY] * len(after), [shape((rows, 256)), shape((extra, 256), F32)])


def unpack_shards(me, shards, shapes, layout):
    n = len(shards)
    chips = n // 2

    def kernel(me_ref, *refs):
        parts, outs = refs[:n], refs[n:]
        me = me_ref[0]
        for k in range(n):
            chip, core = (me >> 1) ^ (k >> 1), (me & 1) ^ (k & 1)
            for out, R, left, C, at in layout:
                size, half = R // chips, C // 2
                row = pl.multiple_of(chip * size, size)
                for c in range(half // 256):
                    col = pl.multiple_of(left + core * half + 256 * c, 256)
                    value = parts[k][at + c * size : at + (c + 1) * size, :].astype(F32)
                    outs[out][pl.ds(row, size), pl.ds(col, 256)] = value

    return call(kernel, "unpack_shards", (me, *shards), [SM] + [VM] * n, [shape(s, F32) for s in shapes])


def exchange(x, axis, k):
    size = lax.axis_size(axis)
    return lax.ppermute(x, axis, [(i, i ^ k) for i in range(size)])


def once(x, after):
    return lax.optimization_barrier((x, after))[0]


def gather(x, after=None):
    n = lax.axis_size("seq")
    parts = {0: x}
    for k in range(2, n, 2):
        parts[k] = exchange(x, "seq", k)
    for k in range(0, n, 2):
        held = parts[k] if after is None or k == 0 else once(parts[k], after)
        parts[k + 1] = exchange(held, "seq", 1)
    return [parts[k] for k in range(n)]


def across_chips(mine):
    return [mine[0]] + [exchange(mine[j], "seq", 2 * j) for j in range(1, len(mine))]


def plain_weights(pairs, small):
    zsize, zme = lax.axis_size("rows"), lax.axis_index("rows")
    outs = []
    for left, right, turned in pairs:
        whole = lax.psum(dot(left, right, ((1,) if turned else (0,), (0,))), ("seq", "rows"))
        size = whole.shape[0] // zsize
        outs.append(lax.dynamic_slice_in_dim(whole, zme * size, size, 0))
    whole = lax.psum(small, ("seq", "rows"))
    parts = []
    for x, dim in ((whole[:NTAGS], 0), (whole[NTAGS : NTAGS + 4].reshape(-1), 0), (whole[NTAGS + 4 :], 1)):
        size = x.shape[dim] // zsize
        parts.append(lax.dynamic_slice_in_dim(x, zme * size, size, dim))
    return outs, parts


def local(
    dec_input, encoded, segment_ids, pair_tags, enc_lengths, out_grad, tag_table, self_qkv, self_out, cross_query,
    cross_kv, cross_out, ffn_in, ffn_in_bias, ffn_out, ffn_out_bias, norm_gain, norm_bias,
):
    n, zsize = lax.axis_size("seq"), lax.axis_size("rows")
    chips = n // 2
    me, zme = lax.axis_index("seq").astype(jnp.int32)[None], lax.axis_index("rows").astype(jnp.int32)[None]
    mirror = n - 1
    weights = zsize == 4 and 512 // (zsize * chips) >= 16
    square = (512, 512)
    cut1 = Cut(chips, zsize, 0, [(512, 2048), (2048, 512)]) if weights else None
    cut2 = Cut(chips, zsize, 512, [(512, 1024), square, square, square] if weights else [])
    cut3 = Cut(chips, zsize, 512, [square] * 3 if weights else [], 16 if weights else 0)

    message = join_tokens(dec_input[0], segment_ids)
    b_in, b_out = ffn_in_bias[None], ffn_out_bias[None]
    oga, ogb = prepare(message, out_grad[0], b_in, b_out)
    xs = gather(message, oga)
    mine = once(encoded[0], xs[2::2])
    enc_parts = {0: encoded[0]} | {k: exchange(mine, "seq", k) for k in range(2, n, 2)}
    ogb = exchange(once(ogb, xs[2::2]), "seq", mirror)
    (low_all, K, V, khot, qhotT, qT, oT, lse, hat1, scale1, first, first_low, cqT, mixT, start_low) = self_front(
        me, pair_tags[0], xs, tag_table, self_qkv, self_out, cross_query, norm_gain, norm_bias
    )
    for k in range(0, n, 2):
        enc_parts[k + 1] = exchange(once(enc_parts[k], (cqT, ogb)) if k else encoded[0], "seq", 1)
    encs = [enc_parts[k] for k in range(n)]
    terms1, (la, lb, g_mid, g_cb, gcT, cdelta, clse, cmixT, vec2, dib, ehot, ek, ev, *back1) = middle(
        cut1, me, enc_lengths[0], encs, cross_kv, cqT, qhotT, first, cross_out, ffn_in, ffn_out,
        b_in, b_out, norm_gain, norm_bias, oga, ogb,
    )
    lb = exchange(lb, "seq", mirror)
    layer_out = jnp.concatenate([la, lb])[None]
    token = g_mid
    if weights:
        sums1 = add_core(terms1[:-1], exchange(terms1[-1], "seq", 1), token)
        token = sums1[0]
        sums1 = across_chips(sums1)
    terms2, (g_start, gmT, delta, vec1, *back2) = cross_back(
        cut2, weights, me, ek, ev, token, encs, cross_kv, cqT, ehot, qhotT, gcT, clse, cdelta, g_mid, cross_query,
        hat1, scale1, norm_gain, self_out, oT, cmixT, g_cb, first_low, mixT,
    )
    token = g_start
    if weights:
        near1, far1 = add_chips(cut1, zme, sums1, (terms2[0],), pinned=True)
        token = near1
    sums2 = add_core(terms2[:-1], exchange(terms2[-1], "seq", 1), token)
    token = sums2[0]
    sums2 = across_chips(sums2)
    terms3, (small, *back3) = self_back(
        cut3, weights, me, pair_tags[0], token, low_all, K, V, khot, qT, qhotT, gmT, lse, delta, self_qkv,
        g_start, start_low, vec1, vec2, dib,
    )
    if weights:
        near12, far12, encoded_grad = add_chips(cut2, zme, sums2, (terms3[0], lb), near1, far1)
        sums3 = add_core(terms3[:-1], exchange(terms3[-1], "seq", 1), near12)
        got12 = exchange(once(far12, sums3[0]), "rows", 2)
        sums3 = across_chips(sums3)
        send12, kept12 = add_far(near12, got12)
        near3, far3, input_grad = add_chips(cut3, zme, sums3, (kept12,))
        got3 = exchange(far3, "rows", 2)
        share12 = add_near(kept12, exchange(send12, "rows", 1))
        shards12 = gather(once(share12, near3))
        send3, kept3 = add_far(near3, got3)
        share3, small = add_last(kept3, exchange(send3, "rows", 1), 16, shards12[2::2])
        ins, outs = 512 // zsize, 2048 // zsize

        def layout(places):
            found, at = [], 0
            for out, R, left, C in places:
                found.append((out, R, left, C, at))
                at += R // chips * (C // 512)
            return found

        places = [(0, ins, 0, 2048), (1, outs, 0, 512), (2, ins, 0, 1024)] + [(j, ins, 0, 512) for j in (3, 4, 5)]
        shapes = [(ins, 2048), (outs, 512), (ins, 1024), (ins, 512), (ins, 512), (ins, 512)]
        d_fi, d_fo, d_ckv, d_co, d_cq, d_so = unpack_shards(me, shards12, shapes, layout(places))
        shards3 = gather(share3, d_fi)
        places = [(0, ins, 512 * j, 512) for j in range(3)]
        d_qkv = unpack_shards(me, shards3, [(ins, 1536)], layout(places))[0]
        tags, wide, lanes = NTAGS // zsize, outs // 256, 512 // zsize
        d_table = jnp.concatenate([small[0:tags], small[tags : 2 * tags]], axis=1)
        d_inner = small[2 * tags : 2 * tags + wide].reshape(-1)
        vectors = small[2 * tags + wide : 2 * tags + wide + 4].reshape(8, lanes)
    else:
        encoded_grad, input_grad = (
            total([jnp.concatenate([t[:BLK], t[BLK:]], axis=1) for t in terms])
            for terms in (sums2, across_chips(add_core(terms3[:-1], exchange(terms3[-1], "seq", 1), small)))
        )
        (hidden, second_low, g_ffn, g_pre), (edkv, dcq, g_branch), (dkv, dq) = back1, back2, back3
        enc_all = jnp.concatenate(encs)
        pairs = [
            (second_low, g_pre, False), (hidden, g_ffn, False), (enc_all, edkv, False), (cmixT, g_cb, True),
            (first_low, dcq, False), (mixT, g_branch, True), (start_low, dq, False), (low_all, dkv, False),
        ]
        small = jnp.concatenate([small[:NTAGS], dib.reshape(4, 512), small[NTAGS:]])
        (d_fi, d_fo, d_ckv, d_co, d_cq, d_so, dq, dkv), (d_table, d_inner, vectors) = plain_weights(pairs, small)
        d_qkv = jnp.concatenate([dq, dkv], axis=1)
    return (
        layer_out, input_grad[None], encoded_grad[None], d_table, d_qkv, d_so, d_cq, d_ckv, d_co, d_fi, d_inner, d_fo,
        vectors[6], vectors[0:3], vectors[3:6],
    )


def solution(mesh):
    tokens = P("rows", "seq", None)
    placed = (tokens, tokens, P("rows", "seq"), P("rows", None), P("rows", None), tokens) + (P(),) * 12
    rows = P("rows", None)
    return jax.shard_map(
        local,
        mesh=mesh,
        in_specs=placed,
        out_specs=(tokens, tokens, tokens)
        + (rows,) * 7
        + (P("rows"), rows, P("rows"), P(None, "rows"), P(None, "rows")),
        check_vma=False,
    )
```

```python
import jax
import jax.numpy as jnp
from jax import lax
from jax.experimental import pallas as pl
from jax.experimental.pallas import tpu as pltpu
from jax.sharding import PartitionSpec as P

F32 = jnp.float32
BF = jnp.bfloat16
SEGS = 4
NTAGS = 16
BLK = 256
HALF = 128
TILE = 512
BIG = -1e30
LEAST = 1e-25
EPS = 1e-5
TN = ((0,), (0,))
NT = ((1,), (1,))
VM = pl.BlockSpec(memory_space=pltpu.VMEM)
SM = pl.BlockSpec(memory_space=pltpu.SMEM)
ANY = pl.BlockSpec(memory_space=pl.ANY)
HB = pl.BlockSpec(memory_space=pltpu.HBM)
SENT = "sent"
TOKEN = jax.ShapeDtypeStruct((8, 128), F32)


def shape(dims, dtype=BF):
    return jax.ShapeDtypeStruct(dims, dtype)


TIMES = {
    "self_front": 16, "middle": 20, "cross_back": 18, "self_back": 18, "add_core": 3, "add_chips": 20, "prepare": 2,
    "join_tokens": 2, "add_far": 2, "add_near": 2, "add_last": 2, "unpack_shards": 3,
}


LIMITS = {
    "self_front": 20, "middle": 32, "cross_back": 28, "self_back": 34, "add_core": 8, "add_chips": 10, "prepare": 4,
    "join_tokens": 4, "add_far": 4, "add_near": 4, "add_last": 4, "unpack_shards": 12,
}


class Outgoing:
    def __init__(self, ref, target, sems):
        self.ref, self.target, self.sems, self.copies = ref, target, sems, []

    def send(self, *index):
        pair = (self.ref.at[index], self.target.at[index]) if index else (self.ref, self.target)
        self.copies.append(pltpu.make_async_copy(*pair, self.sems.at[len(self.copies)]))
        self.copies[-1].start()


def call(kernel, name, ins, specs, outs, out_specs=None, scratch=(), blocks=8):
    outs, out_specs = list(outs), list(out_specs or (VM,) * len(outs))
    ins = [pltpu.with_memory_space_constraint(x, pltpu.HBM) if spec is HB else x for x, spec in zip(ins, specs)]
    sent = [j for j, spec in enumerate(out_specs) if spec is SENT]
    more = [pltpu.VMEM(outs[j].shape, outs[j].dtype) for j in sent]
    more += [pltpu.SemaphoreType.DMA((len(sent), 2))] if sent else []

    def body(*refs):
        if not sent:
            return kernel(*refs)
        refs, mine, sems = list(refs[: -len(more)]), refs[-len(more) : -1], refs[-1]
        going = []
        for at, j in enumerate(sent):
            going.append(Outgoing(mine[at], refs[len(ins) + j], sems.at[at]))
            refs[len(ins) + j] = going[-1]
        kernel(*refs)
        for out in going:
            if not out.copies:
                out.send()
        for out in going:
            for copy in out.copies:
                copy.wait()

    return pl.pallas_call(
        body,
        out_shape=tuple(pltpu.HBM(o.shape, o.dtype) if s in (SENT, HB) else o for o, s in zip(outs, out_specs)),
        in_specs=list(specs),
        out_specs=tuple(HB if spec is SENT else spec for spec in out_specs),
        scratch_shapes=list(scratch) + more,
        compiler_params=pltpu.CompilerParams(vmem_limit_bytes=min(60, LIMITS[name] * blocks // 8) << 20),
        cost_estimate=pl.CostEstimate(flops=TIMES[name] * 10**9, bytes_accessed=1, transcendentals=0),
        name=name,
    )(*ins)


def dot(a, b, dims=((1,), (0,))):
    return lax.dot_general(a, b, (dims, ((), ())), preferred_element_type=F32)


def total(terms):
    out = terms[0].astype(F32)
    for term in terms[1:]:
        out = out + term.astype(F32)
    return out


def build_blocks(src_ref, extra_ref, dst_ref):
    z = jnp.zeros((64, HALF), BF)
    for p in range(4):
        for h in range(2):
            c = slice(h * HALF, (h + 1) * HALF)
            dst_ref[2 * p + h, 0:64, :] = jnp.concatenate([src_ref[128 * p : 128 * p + 64, c], z], 1)
            dst_ref[2 * p + h, 64:128, :] = jnp.concatenate([z, src_ref[128 * p + 64 : 128 * p + 128, c]], 1)
            if extra_ref is not None:
                e = extra_ref[:, c]
                dst_ref[2 * p + h, 128:144, :] = jnp.concatenate([e, e], 1)
                dst_ref[2 * p + h, 144:256, :] = jnp.zeros((112, 256), BF)


def bound_scores(q_ref, k_ref, qhot_ref, qb):
    S = k_ref.shape[0]
    top = jnp.zeros((1, 512), F32)
    for r in range(S // 512):
        rows = jnp.abs(k_ref[512 * r : 512 * r + 512, :].astype(F32))
        top = jnp.maximum(top, jnp.max(rows, axis=0, keepdims=True))
    head = lax.broadcasted_iota(jnp.int32, (16, 512), 1) // 64
    table = jnp.where(head == lax.broadcasted_iota(jnp.int32, (16, 512), 0), top * 1.02, 0.0).astype(BF)
    bound = (dot(table, jnp.abs(q_ref[...])) * 1.02).astype(BF).astype(F32)
    shift = []
    row = lax.broadcasted_iota(jnp.int32, (16, 256), 0)
    for p in range(4):
        for h in range(2):
            c = slice(h * HALF, (h + 1) * HALF)
            shift.append(jnp.concatenate([bound[2 * p : 2 * p + 1, c], bound[2 * p + 1 : 2 * p + 2, c]], 1))
            extra = jnp.concatenate([qhot_ref[:, c], qhot_ref[:, c]], 1).astype(F32)
            qb[2 * p + h, 128:144, :] = jnp.where(row == SEGS, -shift[-1], extra).astype(BF)
    return shift


def split_heads(j, a, o_ref):
    p, h = j // 2, j % 2
    if not isinstance(j, int):
        p, h = pl.multiple_of(128 * p, 128), pl.multiple_of(h * HALF, HALF)
    else:
        p, h = 128 * p, h * HALF
    o_ref[pl.ds(p, 64), pl.ds(h, HALF)] = a[0:64, 0:HALF]
    o_ref[pl.ds(p + 64, 64), pl.ds(h, HALF)] = a[64:128, HALF:]


def pair_of(p):
    return pl.ds(pl.multiple_of(128 * p, 128), 128)


def cross_forward(q_ref, k_ref, vt_ref, khot_ref, qhot_ref, o_ref, lse_ref, qb, least_ref):
    build_blocks(q_ref, qhot_ref, qb)
    shift = bound_scores(q_ref, k_ref, qhot_ref, qb)
    for j in range(8):
        lse_ref[j] = shift[j]

    @pl.loop(0, 4)
    def _(p):
        pair = pair_of(p)
        for h in range(2):
            j = 2 * p + h
            whole = jnp.zeros((1, 256), F32)
            acc = jnp.zeros((128, 256), F32)
            for t in range(k_ref.shape[0] // TILE):
                rows = slice(t * TILE, (t + 1) * TILE)
                kt = jnp.concatenate([k_ref[rows, pair], khot_ref[rows, :]], 1)
                e = jnp.exp(dot(kt, qb[j]))
                whole = whole + jnp.sum(e, axis=0, keepdims=True)
                acc = acc + dot(vt_ref[pair, rows], e.astype(BF))
            least_ref[j] = whole
            lse_ref[j] = lse_ref[j] + jnp.log(whole)
            split_heads(j, acc * (1.0 / whole), o_ref)

    @pl.when(jnp.min(least_ref[...]) < LEAST)
    def _():
        cross_forward_exact(q_ref, k_ref, vt_ref, khot_ref, qhot_ref, o_ref, lse_ref, qb)


def cross_forward_exact(q_ref, k_ref, vt_ref, khot_ref, qhot_ref, o_ref, lse_ref, qb):
    build_blocks(q_ref, qhot_ref, qb)
    tiles = k_ref.shape[0] // TILE

    @pl.loop(0, 8)
    def _(j):
        pair = pair_of(j // 2)

        def scores(t):
            rows = pl.ds(t * TILE, TILE)
            return dot(jnp.concatenate([k_ref[rows, pair], khot_ref[rows, :]], 1), qb[j])

        top = jnp.max(scores(0), axis=0, keepdims=True)
        for t in range(1, tiles):
            top = jnp.maximum(top, jnp.max(scores(t), axis=0, keepdims=True))
        whole = jnp.zeros((1, 256), F32)
        acc = jnp.zeros((128, 256), F32)
        for t in range(tiles):
            e = jnp.exp(scores(t) - top)
            whole = whole + jnp.sum(e, axis=0, keepdims=True)
            acc = acc + dot(vt_ref[pair, t * TILE : (t + 1) * TILE], e.astype(BF))
        lse_ref[j] = top + jnp.log(whole)
        split_heads(j, acc * (1.0 / whole), o_ref)


def cross_backward(q_ref, k_ref, v_ref, khot_ref, qhot_ref, do_ref, lse_ref, dl_ref, dq_ref, dkv_ref, qb, db):
    build_blocks(q_ref, qhot_ref, qb)
    build_blocks(do_ref, None, db)
    size = min(2048, k_ref.shape[0])

    @pl.loop(0, 4)
    def _(p):
        pair = pair_of(p)
        dq = [0.0, 0.0]
        for t in range(k_ref.shape[0] // size):
            rows = slice(t * size, (t + 1) * size)
            k, v = k_ref[rows, pair], v_ref[rows, pair]
            k_turned = k.T
            kt = jnp.concatenate([k, khot_ref[rows, :]], 1)
            dk = dv = 0.0
            for h in range(2):
                j = 2 * p + h
                pr = jnp.exp(dot(kt, qb[j]) - lse_ref[j])
                dp = dot(v, db[j])
                ds = (pr * (dp - dl_ref[j])).astype(BF)
                dv += dot(pr.astype(BF), db[j], NT)
                dk += dot(ds, qb[j, 0:128, :], NT)
                dq[h] += dot(k_turned, ds)
            dkv_ref[rows, pair] = dk.astype(BF)
            dkv_ref[rows, pl.ds(pl.multiple_of(512 + 128 * p, 128), 128)] = dv.astype(BF)
        for h in range(2):
            split_heads(2 * p + h, dq[h] * 0.125, dq_ref)


def work_item(t, i, blocks):
    first = (i + 2) // 2
    second = (t >= first).astype(jnp.int32)
    tile = t - second * first
    start = jnp.where(second == 1, (blocks - 1 - i) * BLK + HALF, i * BLK)
    return second, tile, start - tile * TILE


def relative_positions(swap):
    k = lax.broadcasted_iota(jnp.int32, (TILE, 2 * HALF), 0)
    q = lax.broadcasted_iota(jnp.int32, (TILE, 2 * HALF), 1) & (HALF - 1)
    return (k ^ swap) - q


def self_tiles(blocks, i, full, masked):
    for h, block in ((0, i), (1, blocks - 1 - i)):
        last = block >> 1
        place = lambda tile: pl.multiple_of((tile ^ (i >> 1)) * TILE, TILE)
        pl.loop(0, last)(lambda tile, h=h: full(h, place(tile)))
        masked(h, place(last), (block & 1) * BLK + h * HALF)


def self_forward(blocks, i, q_ref, k_ref, vt_ref, khot_ref, qhot_ref, o_ref, lse_ref, qb, m_s, l_s, acc):
    build_blocks(q_ref, qhot_ref, qb)
    shift = bound_scores(q_ref, k_ref, qhot_ref, qb)
    l_s[...] = jnp.zeros(l_s.shape, F32)
    acc[...] = jnp.zeros(acc.shape, F32)

    def visit(h, r0, offset=None):
        rows = pl.ds(r0, TILE)
        hot = khot_ref[rows, :]
        for p in range(4):
            j = 2 * p + h
            s = dot(jnp.concatenate([k_ref[rows, 128 * p : 128 * p + 128], hot], 1), qb[j])
            if offset is not None:
                s = jnp.where(relative_positions((i & 1) * BLK) <= offset, s, BIG)
            e = jnp.exp(s)
            l_s[j] += jnp.sum(e, axis=0, keepdims=True)
            acc[j] += dot(vt_ref[128 * p : 128 * p + 128, rows], e.astype(BF))

    self_tiles(blocks, i, visit, visit)
    for j in range(8):
        lse_ref[j] = shift[j] + jnp.log(l_s[j])
        split_heads(j, acc[j] * (1.0 / l_s[j]), o_ref)

    @pl.when(jnp.min(l_s[...]) < LEAST)
    def _():
        self_forward_exact(blocks, i, q_ref, k_ref, vt_ref, khot_ref, qhot_ref, o_ref, lse_ref, qb, m_s, l_s, acc)


def self_forward_exact(blocks, i, q_ref, k_ref, vt_ref, khot_ref, qhot_ref, o_ref, lse_ref, qb, m_s, l_s, acc):
    build_blocks(q_ref, qhot_ref, qb)
    swap = (i & 1) * BLK
    items = blocks // 2 + 1
    m_s[...] = jnp.full(m_s.shape, -3e38, F32)
    l_s[...] = jnp.zeros(l_s.shape, F32)
    acc[...] = jnp.zeros(acc.shape, F32)

    def scores(t, p):
        h, tile, offset = work_item(t, i, blocks)
        r0 = pl.multiple_of((tile ^ (i >> 1)) * TILE, TILE)
        kt = jnp.concatenate([k_ref[pl.ds(r0, TILE), pair_of(p)], khot_ref[pl.ds(r0, TILE), :]], 1)
        return jnp.where(relative_positions(swap) <= offset, dot(kt, qb[2 * p + h]), BIG), 2 * p + h, r0

    @pl.loop(0, 4 * items)
    def _(step):
        s, j, _ = scores(step // 4, step % 4)
        m_s[j] = jnp.maximum(m_s[j], jnp.max(s, axis=0, keepdims=True))

    @pl.loop(0, 4 * items)
    def _(step):
        s, j, r0 = scores(step // 4, step % 4)
        e = jnp.exp(s - m_s[j])
        l_s[j] += jnp.sum(e, axis=0, keepdims=True)
        acc[j] += dot(vt_ref[pair_of(step % 4), pl.ds(r0, TILE)], e.astype(BF))

    for j in range(8):
        lse_ref[j] = m_s[j] + jnp.log(l_s[j])
        split_heads(j, acc[j] * (1.0 / l_s[j]), o_ref)


def self_backward(
    blocks, i, q_ref, k_ref, kt_ref, v_ref, khot_ref, qhot_ref, do_ref, lse_ref, dl_ref, dq_ref, dkv_ref,
    qb, db, dqa, dka, dva,
):
    build_blocks(q_ref, qhot_ref, qb)
    build_blocks(do_ref, None, db)
    dqa[...] = jnp.zeros(dqa.shape, F32)
    dka[...] = jnp.zeros(dka.shape, F32)
    dva[...] = jnp.zeros(dva.shape, F32)

    def visit(h, r0, offset=None):
        rows = pl.ds(r0, TILE)
        hot = khot_ref[rows, :]
        for p in range(4):
            j = 2 * p + h
            lanes = slice(128 * p, 128 * p + 128)
            s = dot(jnp.concatenate([k_ref[rows, lanes], hot], 1), qb[j])
            if offset is not None:
                s = jnp.where(relative_positions((i & 1) * BLK) <= offset, s, BIG)
            pr = jnp.exp(s - lse_ref[j])
            dp = dot(v_ref[rows, lanes], db[j])
            ds = (pr * (dp - dl_ref[j])).astype(BF)
            dva[rows, lanes] += dot(pr.astype(BF), db[j], NT)
            dka[rows, lanes] += dot(ds, qb[j, 0:128, :], NT)
            dqa[j] += dot(kt_ref[lanes, rows], ds)

    self_tiles(blocks, i, visit, visit)
    dkv_ref[:, 0:512] = dka[...].astype(BF)
    dkv_ref[:, 512:1024] = dva[...].astype(BF)
    for j in range(8):
        split_heads(j, dqa[j] * 0.125, dq_ref)


def norm_forward(v, gain, bias):
    centered = v - jnp.mean(v, axis=-1, keepdims=True)
    scale = lax.rsqrt(jnp.mean(centered * centered, axis=-1, keepdims=True) + EPS)
    hat = centered * scale
    return hat * gain + bias, hat, scale


def norm_backward(g, hat, scale, gain):
    gh = g * gain
    out = scale * (gh - jnp.mean(gh, axis=-1, keepdims=True) - hat * jnp.mean(gh * hat, axis=-1, keepdims=True))
    return out, jnp.sum(g * hat, axis=0, keepdims=True), jnp.sum(g, axis=0, keepdims=True)


def gelu_both(x):
    c = 0.7978845608028654
    sq = x * x
    t = jnp.tanh(c * x * (1 + 0.044715 * sq))
    half = 0.5 * (1 + t)
    return x * half, half + 0.5 * x * (1 - t * t) * (c * (1 + 3 * 0.044715 * sq))


def inner_rows(g_refT, o_ref, dl_ref):
    for p in range(4):
        both = []
        for a in range(2):
            rows = slice(128 * p + 64 * a, 128 * p + 64 * a + 64)
            both.append(jnp.sum(g_refT[rows, :].astype(F32) * o_ref[rows, :], axis=0, keepdims=True))
        for h in range(2):
            cols = slice(h * HALF, (h + 1) * HALF)
            dl_ref[2 * p + h] = jnp.concatenate([both[0][:, cols], both[1][:, cols]], 1)


class Cut:
    def __init__(self, chips, zsize, tokens, sizes, extra=0):
        self.chips, self.zsize, self.tokens, self.extra = chips, zsize, tokens, extra
        self.at, rows = [], 0
        for R, C in sizes:
            self.at.append(rows)
            rows += R // (zsize * chips) * (C // 512)
        self.per_z = rows + extra
        self.rows = tokens + zsize * self.per_z

    def write(self, index, keep, me, evens, odd_ref):
        R, C = keep.shape
        core, chip = me & 1, me >> 1
        size, half = R // (self.zsize * self.chips), C // 2
        for turn in range(2):
            side = core if turn == 0 else 1 - core
            for j in range(self.chips):
                for z in range(self.zsize):
                    row = pl.multiple_of(z * (R // self.zsize) + (chip ^ j) * size, size)
                    for c in range(half // 256):
                        left = pl.multiple_of(side * half + 256 * c, 256)
                        at = self.tokens + z * self.per_z + self.at[index] + c * size
                        piece = keep[pl.ds(row, size), pl.ds(left, 256)]
                        if turn == 0:
                            evens[j][at : at + size, :] = piece
                        else:
                            odd_ref[j, at : at + size, :] = piece

    def write_tokens(self, r, part, evens, odd_ref):
        for c in range(2):
            piece = part[:, 256 * c : 256 * c + 256]
            if r % 2:
                odd_ref[r // 2, BLK * c : BLK * c + BLK, :] = piece
            else:
                evens[r // 2][BLK * c : BLK * c + BLK, :] = piece

    def write_extra(self, z, part, evens, odd_ref):
        at = self.tokens + z * self.per_z + self.per_z - self.extra
        for j in range(self.chips):
            evens[j][at : at + self.extra, :] = part
            odd_ref[j, at : at + self.extra, :] = part

    def outs(self):
        return [shape((self.rows, 256))] * self.chips + [shape((self.chips, self.rows, 256))]


def join_tokens(x, seg):
    def kernel(x_hbm, seg_hbm, out, seg_s, sems):
        loads = [
            pltpu.make_async_copy(x_hbm, out.ref.at[0:BLK, :], sems.at[0]),
            pltpu.make_async_copy(seg_hbm, seg_s, sems.at[1]),
        ]
        for copy in loads:
            copy.start()
        for copy in loads[::-1]:
            copy.wait()
            if copy is loads[1]:
                row = jnp.concatenate([seg_s[...].astype(F32), jnp.zeros((1, 256), F32)], 1)
                out.ref[BLK:, :] = jnp.broadcast_to(row, (16, 512)).astype(BF)

    scratch = [pltpu.VMEM((1, 256), jnp.int32), pltpu.SemaphoreType.DMA((2,))]
    return call(kernel, "join_tokens", (x, seg), [HB] * 2, [shape((BLK + 16, 512))], [SENT], scratch)[0]


def prepare(after, grad, *rest):
    def kernel(g_ref, *refs):
        ga_ref, gb_ref = refs[-2:]
        ga_ref[...] = g_ref[0:HALF, :]
        gb_ref[...] = g_ref[HALF:, :]

    ins = (grad, after, *rest)
    return call(
        kernel, "prepare", ins, [VM, HB] + [ANY] * (len(ins) - 2), [shape((HALF, 512)), shape((HALF, 512))], [VM, VM]
    )


def self_front_kernel(n, me_ref, tag_ref, *refs):
    xs, refs = refs[:n], refs[n:]
    (table_ref, w_ref, so_ref, cqw_ref, gain_ref, bias_ref,
     low_o, k_o, v_o, khot_o, qhot_ref, qT_o, oT_ref, lse_o, hat_ref, scale_ref, first_ref,
     flow_ref, cqT_ref, mixT_ref, slow_o, vt_s, start_s, qb, m_s, l_s, acc) = refs
    low_s, k_s, v_s, khot_s, qT_ref, lse_ref = (out.ref for out in (low_o, k_o, v_o, khot_o, qT_o, lse_o))
    segs = [x[BLK : BLK + 8, 0:BLK].astype(F32)[0:1].astype(jnp.int32) for x in xs]
    table = table_ref[...].astype(F32)
    ids = lax.broadcasted_iota(jnp.int32, (NTAGS, 512), 0)
    rows = [jnp.sum(jnp.where(ids == tag_ref[s], table, 0.0), axis=0, keepdims=True) for s in range(SEGS)]
    tag_rows = jnp.concatenate(rows + [jnp.zeros((128 - SEGS, 512), F32)], 0).astype(BF)
    for r in range(n):
        at = slice(r * BLK, (r + 1) * BLK)
        ids = lax.broadcasted_iota(jnp.int32, (128, BLK), 0)
        hot = (ids == segs[r]).astype(F32).T
        khot_s[at, :] = ((ids == segs[r]) | (ids == SEGS)).astype(F32).T.astype(BF)
        start = xs[r][0:BLK, :].astype(F32) + dot(hot.astype(BF), tag_rows)
        low = start.astype(BF)
        low_s[at, :] = low
        if r == 0:
            start_s[0:HALF, :] = start[0:HALF]
        if r == n - 1:
            start_s[HALF:, :] = start[HALF:]
        k_s[at, :] = dot(low, w_ref[:, 512:1024]).astype(BF)
        v = dot(low, w_ref[:, 1024:1536]).astype(BF)
        v_s[at, :] = v
        vt_s[:, at] = v.T
    for out in (low_o, k_o, v_o, khot_o):
        out.send()
    seg = jnp.concatenate([segs[0][:, 0:HALF], segs[n - 1][:, HALF:]], 1)
    ids = lax.broadcasted_iota(jnp.int32, (16, BLK), 0)
    qhot_ref[...] = jnp.where((ids != seg) & (ids < SEGS), BIG, 0.0).astype(BF)
    slow = start_s[...].astype(BF)
    slow_o.ref[...] = slow
    qT_ref[...] = (dot(slow, w_ref[:, 0:512]) * 0.125).astype(BF).T
    slow_o.send()
    qT_o.send()
    self_forward(n, me_ref[0], qT_ref, k_s, vt_s, khot_s, qhot_ref, oT_ref, lse_ref, qb, m_s, l_s, acc)
    mixT = oT_ref[...].astype(BF)
    mixT_ref[...] = mixT
    first, hat, scale = norm_forward(
        start_s[...] + dot(mixT, so_ref[...], TN), gain_ref[0:1, :].astype(F32), bias_ref[0:1, :].astype(F32)
    )
    hat_ref[...] = hat
    scale_ref[...] = jnp.broadcast_to(scale, (BLK, 128))
    first_ref[...] = first
    first_low = first.astype(BF)
    flow_ref[...] = first_low
    cqT_ref[...] = (dot(first_low, cqw_ref[...]) * 0.125).astype(BF).T


def self_front(me, tags, xs, table, w, so, cqw, gain, bias):
    n = len(xs)
    S = n * BLK
    big = [shape((S, 512)), shape((S, 512)), shape((S, 512)), shape((S, 128))]
    outs = big + [
        shape((16, BLK)), shape((512, BLK)), shape((512, BLK), F32), shape((8, 1, BLK), F32), shape((BLK, 512), F32),
        shape((BLK, 128), F32), shape((BLK, 512), F32), shape((BLK, 512)), shape((512, BLK)), shape((512, BLK)),
        shape((BLK, 512)),
    ]
    scratch = [
        pltpu.VMEM((512, S), BF), pltpu.VMEM((BLK, 512), F32), pltpu.VMEM((8, 256, 256), BF),
        pltpu.VMEM((8, 1, 256), F32), pltpu.VMEM((8, 1, 256), F32), pltpu.VMEM((8, 128, 256), F32),
    ]
    kinds = [SENT] * 4 + [VM, SENT, VM, SENT] + [VM] * 6 + [SENT]
    return call(
        lambda *refs: self_front_kernel(n, *refs), "self_front", (me, tags, *xs, table, w, so, cqw, gain, bias),
        [SM, SM] + [VM] * (n + 6), outs, kinds, scratch, n,
    )


def middle_kernel(n, cut, me_ref, len_ref, *refs):
    encs, refs = refs[:n], refs[n:]
    (w_ref, cqT_ref, qhot_ref, first_ref, co_ref, fi_ref, fo_ref, bi_ref, bo_ref, gain_ref, bias_ref,
     oga_ref, ogb_ref, *refs) = refs
    if cut:
        evens, (odd_ref, *refs) = refs[: cut.chips], refs[cut.chips :]
    (la_ref, lb_ref, gmid_ref, gcb_ref, gcT_ref, dl_ref, lse_ref, cmixT_ref, vec_o, dib_o, khot_ref, k_ref, v_ref,
     hid_ref, slow_ref, gffn_ref, gpre_ref, k_s, v_s, vt_s, oT_s, slope_s, qb, least_s, fi_s, fo_s, sems) = refs
    me, vec_ref, dib_ref = me_ref[0], vec_o.ref, dib_o.ref
    e0 = len_ref[0]
    e1 = e0 + len_ref[1]
    e2 = e1 + len_ref[2]
    for r in range(n):
        at = slice(r * BLK, (r + 1) * BLK)
        pos = lax.broadcasted_iota(jnp.int32, (BLK, 128), 0) + (me ^ r) * BLK
        seg = (pos >= e0).astype(jnp.int32) + (pos >= e1).astype(jnp.int32) + (pos >= e2).astype(jnp.int32)
        lane = lax.broadcasted_iota(jnp.int32, (BLK, 128), 1)
        khot_ref[at, :] = ((lane == seg) | (lane == SEGS)).astype(F32).astype(BF)
        enc = encs[r][...]
        k_s[at, :] = dot(enc, w_ref[:, 0:512]).astype(BF)
        v = dot(enc, w_ref[:, 512:1024]).astype(BF)
        v_s[at, :] = v
        vt_s[:, at] = v.T
    copies = [pltpu.make_async_copy(k_s, k_ref, sems.at[0]), pltpu.make_async_copy(v_s, v_ref, sems.at[1])]
    for copy in copies:
        copy.start()
    cross_forward(cqT_ref, k_s, vt_s, khot_ref, qhot_ref, oT_s, lse_ref, qb, least_s)
    cmixT = oT_s[...].astype(BF)
    cmixT_ref[...] = cmixT
    gains = [gain_ref[j : j + 1, :].astype(F32) for j in range(3)]
    shifts = [bias_ref[j : j + 1, :].astype(F32) for j in range(3)]
    second, hat2, scale2 = norm_forward(first_ref[...] + dot(cmixT, co_ref[...], TN), gains[1], shifts[1])
    second_low = second.astype(BF)
    slow_ref[...] = second_low
    out = second + bo_ref[...].astype(F32)
    for c in range(4):
        cols = slice(512 * c, 512 * c + 512)
        act, slope = gelu_both(dot(second_low, fi_ref[:, cols]) + bi_ref[:, cols].astype(F32))
        hidden = act.astype(BF)
        hid_ref[:, cols] = hidden
        slope_s[:, cols] = slope
        out = out + dot(hidden, fo_ref[cols, :])
    result, hat3, scale3 = norm_forward(out, gains[2], shifts[2])
    la_ref[...] = result[0:HALF].astype(BF)
    lb_ref[...] = result[HALF:].astype(BF)
    og = jnp.concatenate([oga_ref[...], ogb_ref[...]], 0).astype(F32)
    g3, gg3, gb3 = norm_backward(og, hat3, scale3, gains[2])
    g_ffn = g3.astype(BF)
    gffn_ref[...] = g_ffn
    d_out_bias = jnp.sum(g_ffn.astype(F32), axis=0, keepdims=True)
    g2 = g3
    for c in range(4):
        cols = slice(512 * c, 512 * c + 512)
        g_pre = (dot(g_ffn, fo_ref[cols, :], NT) * slope_s[:, cols]).astype(BF)
        gpre_ref[:, cols] = g_pre
        dib_ref[:, cols] = jnp.sum(g_pre.astype(F32), axis=0, keepdims=True)
        g2 = g2 + dot(g_pre, fi_ref[:, cols], NT)
        if cut:
            fi_s[:, cols] = dot(second_low, g_pre, TN).astype(BF)
            fo_s[cols, :] = dot(hid_ref[:, cols], g_ffn, TN).astype(BF)
    g_mid, gg2, gb2 = norm_backward(g2, hat2, scale2, gains[1])
    gmid_ref[...] = g_mid
    g_cb = g_mid.astype(BF)
    gcb_ref[...] = g_cb
    gcT_ref[...] = dot(co_ref[...], g_cb, NT).astype(BF)
    inner_rows(gcT_ref, oT_s, dl_ref)
    vec_ref[...] = jnp.concatenate([gg2, gb2, gg3, gb3, d_out_bias, jnp.zeros((3, 512), F32)], 0)
    if cut:
        cut.write(0, fi_s, me, evens, odd_ref)
        cut.write(1, fo_s, me, evens, odd_ref)
    for copy in copies:
        copy.wait()


def middle(cut, me, lens, encs, *rest):
    n = len(encs)
    S = n * BLK
    outs = (cut.outs() if cut else []) + [
        shape((HALF, 512)), shape((HALF, 512)), shape((BLK, 512), F32), shape((BLK, 512)), shape((512, BLK)),
        shape((8, 1, 256), F32), shape((8, 1, 256), F32), shape((512, BLK)), shape((8, 512), F32),
        shape((1, 2048), F32), shape((S, 128)), shape((S, 512)), shape((S, 512)),
    ]
    hold = [shape((BLK, 2048)), shape((BLK, 512)), shape((BLK, 512)), shape((BLK, 2048))]
    kinds = [VM] * (len(outs) - 5) + [SENT] * 2 + [VM] + [HB] * 2
    plain = [] if cut else hold
    outs += plain
    kinds += [VM] * len(plain)
    scratch = ([pltpu.VMEM(x.shape, BF) for x in hold] if cut else []) + [
        pltpu.VMEM((S, 512), BF), pltpu.VMEM((S, 512), BF), pltpu.VMEM((512, S), BF), pltpu.VMEM((512, BLK), F32),
        pltpu.VMEM((BLK, 2048), F32), pltpu.VMEM((8, 256, 256), BF), pltpu.VMEM((8, 1, 256), F32), pltpu.VMEM((512, 2048), BF),
        pltpu.VMEM((2048, 512), BF), pltpu.SemaphoreType.DMA((2,)),
    ]
    got = call(
        lambda *refs: middle_kernel(n, cut, *refs), "middle", (me, lens, *encs, *rest),
        [SM, SM] + [VM] * (n + 13), outs, kinds, scratch, n,
    )
    first = len(cut.outs()) if cut else 0
    return got[:first], got[first:]


def cross_back_kernel(n, cut, weights, me_ref, *refs):
    half = n // 2
    (k_s, v_s, _, *refs) = refs
    encs, refs = refs[:n], refs[n:]
    (w_ref, cqT_ref, khot_ref, qhot_ref, gcT_ref, lse_ref, dl_ref, gmid_ref, cqw_ref, hat_ref, scale_ref, gain_ref,
     so_ref, oT_ref, cmixT_ref, gcb_ref, flow_ref, mixT_ref, *refs) = refs
    going, (odd_ref, gstart, gmT, dl1, vec, *refs) = refs[:half], refs[half:]
    evens = [out.ref for out in going]
    gstart_ref, gmT_ref, dl1_ref, vec_ref = gstart.ref, gmT.ref, dl1.ref, vec.ref
    dkv_ref, dq_ref, gbr_ref, dqT_s, qb, db, enc_s, keep, kv_keep, sems = refs
    late = []
    if weights:
        for j in range(n):
            rows = slice(BLK * j, BLK * (j + 1))
            late.append(pltpu.make_async_copy(encs[j], enc_s.at[rows, :], sems.at[j]))
    for copy in late:
        copy.start()
    cross_backward(
        cqT_ref, k_s, v_s, khot_ref, qhot_ref, gcT_ref, lse_ref, dl_ref, dqT_s, dkv_ref, qb, db
    )
    me = me_ref[0]
    for r in range(n):
        at = slice(r * BLK, (r + 1) * BLK)
        part = dot(dkv_ref[at, :], w_ref[...], NT)
        cut.write_tokens(r, part.astype(BF), evens, odd_ref)
    if weights:
        for out in going:
            out.send(slice(0, 512))
    dq = dqT_s[...].astype(BF).T
    dq_ref[...] = dq
    g1 = gmid_ref[...] + dot(dq, cqw_ref[...], NT)
    g_start, gg1, gb1 = norm_backward(g1, hat_ref[...], scale_ref[:, 0:1], gain_ref[0:1, :].astype(F32))
    gstart_ref[...] = g_start
    g_branch = g_start.astype(BF)
    gbr_ref[...] = g_branch
    gmT_ref[...] = dot(so_ref[...], g_branch, NT).astype(BF)
    inner_rows(gmT_ref, oT_ref, dl1_ref)
    vec_ref[...] = jnp.concatenate([gg1, gb1, jnp.zeros((6, 512), F32)], 0)
    for out in (gstart, gmT, dl1, vec):
        out.send()
    if weights:
        keep[0] = dot(cmixT_ref[...], gcb_ref[...]).astype(BF)
        keep[1] = dot(flow_ref[...], dq_ref[...], TN).astype(BF)
        keep[2] = dot(mixT_ref[...], g_branch).astype(BF)
        for j in range(3):
            cut.write(1 + j, keep.at[j], me, evens, odd_ref)
        for copy in late:
            copy.wait()
        kv_keep[...] = dot(enc_s[...], dkv_ref[...], TN).astype(BF)
        cut.write(0, kv_keep, me, evens, odd_ref)
        for out in going:
            out.send(slice(512, cut.rows))


def cross_back(cut, weights, me, k, v, after, encs, *rest):
    n = len(encs)
    S = n * BLK
    more = [shape((S, 1024)), shape((BLK, 512)), shape((BLK, 512))]
    outs = cut.outs() + [
        shape((BLK, 512), F32), shape((512, BLK)), shape((8, 1, 256), F32), shape((8, 512), F32)
    ] + ([] if weights else more)
    scratch = ([pltpu.VMEM(s.shape, s.dtype) for s in more] if weights else []) + [
        pltpu.VMEM((512, BLK), F32), pltpu.VMEM((8, 256, 256), BF), pltpu.VMEM((8, 128, 256), BF),
        pltpu.VMEM((S if weights else 16, 512), BF), pltpu.VMEM((3, 512, 512), BF), pltpu.VMEM((512, 1024), BF),
        pltpu.SemaphoreType.DMA((n,)),
    ]
    got = call(
        lambda *refs: cross_back_kernel(n, cut, weights, *refs), "cross_back", (me, k, v, after, *encs, *rest),
        [SM, VM, VM, HB if weights else ANY] + [ANY] * n + [VM] * 18,
        outs, [SENT] * (n // 2) + [VM] + [SENT] * 4 + [VM] * (len(outs) - n // 2 - 5), scratch, n,
    )
    return got[: n // 2 + 1], got[n // 2 + 1 :]


def self_back_kernel(n, cut, weights, me_ref, tag_ref, *refs):
    half = n // 2
    (_, low_hbm, k_s, v_s, khot_s, qT_ref, qhot_ref, gmT_ref, lse_ref, dl_ref, w_ref,
     gstart_ref, slow_ref, vec1_ref, vec2_ref, dib_ref, *refs) = refs
    evens, (odd_ref, small_ref, *refs) = refs[:half], refs[half:]
    (dkv_ref, dq_ref, low_s, kt_s, dqT_s, qb, db, dqa, dka, dva, keep, sems) = refs
    if weights:
        low_copy = pltpu.make_async_copy(low_hbm, low_s, sems.at[0])
        low_copy.start()
    for r in range(n):
        at = slice(r * BLK, (r + 1) * BLK)
        kt_s[:, at] = k_s[at, :].T
    me = me_ref[0]
    self_backward(
        n, me, qT_ref, k_s, kt_s, v_s, khot_s, qhot_ref, gmT_ref, lse_ref, dl_ref, dqT_s, dkv_ref,
        qb, db, dqa, dka, dva,
    )
    dq = dqT_s[...].astype(BF).T
    dq_ref[...] = dq
    mine = gstart_ref[...] + dot(dq, w_ref[:, 0:512], NT)
    sums = jnp.zeros((128, 512), F32)
    for r in range(n):
        at = slice(r * BLK, (r + 1) * BLK)
        part = dot(dkv_ref[at, :], w_ref[:, 512:1536], NT)
        if r == 0:
            part = jnp.concatenate([part[:HALF] + mine[:HALF], part[HALF:]], 0)
        if r == n - 1:
            part = jnp.concatenate([part[:HALF], part[HALF:] + mine[HALF:]], 0)
        part = part.astype(BF)
        sums = sums + dot(khot_s[at, :], part, TN)
        cut.write_tokens(r, part, evens, odd_ref)
    ids = lax.broadcasted_iota(jnp.int32, (NTAGS, 512), 0)
    table = jnp.zeros((NTAGS, 512), F32)
    for s in range(SEGS):
        table = table + jnp.where(ids == tag_ref[s], sums[s : s + 1, :], 0.0)
    v1, v2 = vec1_ref[...], vec2_ref[...]
    vectors = [v1[0:1], v2[0:1], v2[2:3], v1[1:2], v2[1:2], v2[3:4], v2[4:5], jnp.zeros((1, 512), F32)]
    if weights:
        zs = cut.zsize
        wide, lanes, tags = 2048 // zs, 512 // zs, NTAGS // zs
        for z in range(zs):
            rows = []
            for c in range(2):
                rows.append(table[tags * z : tags * (z + 1), 256 * c : 256 * c + 256])
            rows += [dib_ref[:, wide * z + 256 * c : wide * z + 256 * (c + 1)] for c in range(wide // 256)]
            cut_rows = [v[:, lanes * z : lanes * (z + 1)] for v in vectors]
            rows += [jnp.concatenate(cut_rows[2 * c : 2 * c + 2], 1) for c in range(4)]
            used = 2 * tags + wide // 256 + 4
            rows.append(jnp.zeros((16 - used, 256), F32))
            cut.write_extra(z, jnp.concatenate(rows, 0).astype(BF), evens, odd_ref)
        small_ref[...] = jnp.zeros(small_ref.shape, F32)
        keep[:, 0:512] = dot(slow_ref[...], dq_ref[...], TN).astype(BF)
        low_copy.wait()
        keep[:, 512:1536] = dot(low_s[...], dkv_ref[...], TN).astype(BF)
        for j in range(3):
            cut.write(j, keep.at[:, 512 * j : 512 * j + 512], me, evens, odd_ref)
    else:
        small_ref[...] = jnp.concatenate([table] + vectors, 0)


def self_back(cut, weights, me, tags, after, low, k, v, khot, *rest):
    S = k.shape[0]
    n = S // BLK
    more = [shape((S, 1024)), shape((BLK, 512))]
    outs = cut.outs() + [shape((24, 512), F32)] + ([] if weights else more)
    scratch = ([pltpu.VMEM(s.shape, s.dtype) for s in more] if weights else []) + [
        pltpu.VMEM((S if weights else 16, 512), BF), pltpu.VMEM((512, S), BF),
        pltpu.VMEM((512, BLK), F32), pltpu.VMEM((8, 256, 256), BF), pltpu.VMEM((8, 128, 256), BF),
        pltpu.VMEM((8, 128, 256), F32), pltpu.VMEM((S, 512), F32), pltpu.VMEM((S, 512), F32),
        pltpu.VMEM((512, 1536), BF), pltpu.SemaphoreType.DMA((1,)),
    ]
    got = call(
        lambda *refs: self_back_kernel(n, cut, weights, *refs), "self_back",
        (me, tags, after, low, k, v, khot, *rest), [SM, SM, HB, HB] + [VM] * 14, outs, None, scratch, n,
    )
    return got[: n // 2 + 1], got[n // 2 + 1 :]


def add_core(evens, got, after):
    count = len(evens)

    def kernel(*refs):
        ins, got_ref, (first, *outs) = refs[:count], refs[count], refs[count + 2 :]
        for j, out_ref in enumerate([first.ref] + outs):
            out_ref[...] = (ins[j][...].astype(F32) + got_ref[j].astype(F32)).astype(BF)
            if j == 0:
                first.send()

    return call(
        kernel, "add_core", (*evens, got, after), [VM] * (count + 1) + [ANY], [shape(e.shape) for e in evens],
        [SENT] + [VM] * (count - 1),
    )


def add_chips(cut, zme, terms, after, near=None, far=None, pinned=False):
    count, per = len(terms), cut.per_z
    extra = [] if near is None else [near, far]
    base = extra[0].shape[1] if extra else 0

    def kernel(z_ref, *refs):
        ins, (near_ref, far_ref, *outs) = refs[:count], refs[count + len(after) + len(extra) :]
        s, sems = outs[-2:]
        loads = []
        for j in range(count):
            rows = slice(cut.tokens, cut.rows)
            loads.append(pltpu.make_async_copy(ins[j].at[rows, :], s.at[j, rows, :], sems.at[0, j]))
        for j in range(count if cut.tokens else 0):
            rows = slice(0, cut.tokens)
            loads.append(pltpu.make_async_copy(ins[j].at[rows, :], s.at[j, rows, :], sems.at[1, j]))
        for copy in loads:
            copy.start()
        if extra:
            early = refs[count + len(after) : count + len(after) + 2]
            near_ref[:, 0:base, :] = early[0][...]
            far_ref[:, 0:base, :] = early[1][...]
        for copy in loads[:count]:
            copy.wait()
        for k in range(4):
            row = pl.multiple_of(cut.tokens + (z_ref[0] ^ k) * per, 16)
            value = total([s[j, pl.ds(row, per), :] for j in range(count)]).astype(BF)
            (near_ref if k < 2 else far_ref)[k % 2, base : base + per, :] = value
        for copy in loads[count:]:
            copy.wait()
        for c in range(2 if cut.tokens else 0):
            part = total([s[j, BLK * c : BLK * c + BLK, :] for j in range(count)])
            outs[0][:, 256 * c : 256 * c + 256] = part

    outs = [shape((2, base + per, 256)), shape((2, base + per, 256))] + [shape((BLK, 512), F32)] * (cut.tokens > 0)
    return call(
        kernel, "add_chips", (zme, *terms, *after, *extra),
        [SM, HB] + [ANY] * (count - 1) + [HB if pinned else ANY] * len(after) + [VM] * len(extra), outs, None,
        [pltpu.VMEM((count, cut.rows, 256), BF), pltpu.SemaphoreType.DMA((2, count))],
    )


def add_far(near, got):
    def kernel(near_ref, got_ref, send_ref, keep_ref):
        send_ref[...] = (near_ref[1].astype(F32) + got_ref[1].astype(F32)).astype(BF)
        keep_ref[...] = near_ref[0].astype(F32) + got_ref[0].astype(F32)

    outs = [shape(near.shape[1:]), shape(near.shape[1:], F32)]
    return call(kernel, "add_far", (near, got), [VM] * 2, outs)


def add_near(kept, sent):
    def kernel(kept_ref, sent_ref, out_ref):
        out_ref[...] = (kept_ref[...] + sent_ref[...].astype(F32)).astype(BF)

    return call(kernel, "add_near", (kept, sent), [VM] * 2, [shape(kept.shape)])[0]


def add_last(kept, sent, extra, after):
    rows = kept.shape[0] - extra

    def kernel(kept_ref, sent_ref, *refs):
        out_ref, small_ref = refs[-2:]
        value = kept_ref[...] + sent_ref[...].astype(F32)
        out_ref[...] = value[:rows].astype(BF)
        small_ref[...] = value[rows:]

    return call(kernel, "add_last", (kept, sent, *after), [VM] * 2 + [ANY] * len(after), [shape((rows, 256)), shape((extra, 256), F32)])


def unpack_shards(me, shards, shapes, layout):
    n = len(shards)
    chips = n // 2

    def kernel(me_ref, *refs):
        parts, outs = refs[:n], refs[n:]
        me = me_ref[0]
        for k in range(n):
            chip, core = (me >> 1) ^ (k >> 1), (me & 1) ^ (k & 1)
            for out, R, left, C, at in layout:
                size, half = R // chips, C // 2
                row = pl.multiple_of(chip * size, size)
                for c in range(half // 256):
                    col = pl.multiple_of(left + core * half + 256 * c, 256)
                    value = parts[k][at + c * size : at + (c + 1) * size, :].astype(F32)
                    outs[out][pl.ds(row, size), pl.ds(col, 256)] = value

    return call(kernel, "unpack_shards", (me, *shards), [SM] + [VM] * n, [shape(s, F32) for s in shapes])


def exchange(x, axis, k):
    size = lax.axis_size(axis)
    return lax.ppermute(x, axis, [(i, i ^ k) for i in range(size)])


def once(x, after):
    return lax.optimization_barrier((x, after))[0]


def gather(x, after=None):
    n = lax.axis_size("seq")
    parts = {0: x}
    for k in range(2, n, 2):
        parts[k] = exchange(x, "seq", k)
    for k in range(0, n, 2):
        held = parts[k] if after is None or k == 0 else once(parts[k], after)
        parts[k + 1] = exchange(held, "seq", 1)
    return [parts[k] for k in range(n)]


def across_chips(mine):
    return [mine[0]] + [exchange(mine[j], "seq", 2 * j) for j in range(1, len(mine))]


def plain_weights(pairs, small):
    zsize, zme = lax.axis_size("rows"), lax.axis_index("rows")
    outs = []
    for left, right, turned in pairs:
        whole = lax.psum(dot(left, right, ((1,) if turned else (0,), (0,))), ("seq", "rows"))
        size = whole.shape[0] // zsize
        outs.append(lax.dynamic_slice_in_dim(whole, zme * size, size, 0))
    whole = lax.psum(small, ("seq", "rows"))
    parts = []
    for x, dim in ((whole[:NTAGS], 0), (whole[NTAGS : NTAGS + 4].reshape(-1), 0), (whole[NTAGS + 4 :], 1)):
        size = x.shape[dim] // zsize
        parts.append(lax.dynamic_slice_in_dim(x, zme * size, size, dim))
    return outs, parts


def local(
    dec_input, encoded, segment_ids, pair_tags, enc_lengths, out_grad, tag_table, self_qkv, self_out, cross_query,
    cross_kv, cross_out, ffn_in, ffn_in_bias, ffn_out, ffn_out_bias, norm_gain, norm_bias,
):
    n, zsize = lax.axis_size("seq"), lax.axis_size("rows")
    chips = n // 2
    me, zme = lax.axis_index("seq").astype(jnp.int32)[None], lax.axis_index("rows").astype(jnp.int32)[None]
    mirror = n - 1
    weights = zsize == 4 and 512 // (zsize * chips) >= 16
    square = (512, 512)
    cut1 = Cut(chips, zsize, 0, [(512, 2048), (2048, 512)]) if weights else None
    cut2 = Cut(chips, zsize, 512, [(512, 1024), square, square, square] if weights else [])
    cut3 = Cut(chips, zsize, 512, [square] * 3 if weights else [], 16 if weights else 0)

    message = join_tokens(dec_input[0], segment_ids)
    b_in, b_out = ffn_in_bias[None], ffn_out_bias[None]
    oga, ogb = prepare(message, out_grad[0], b_in, b_out)
    xs = gather(message, oga)
    mine = once(encoded[0], xs[2::2])
    enc_parts = {0: encoded[0]} | {k: exchange(mine, "seq", k) for k in range(2, n, 2)}
    ogb = exchange(once(ogb, xs[2::2]), "seq", mirror)
    (low_all, K, V, khot, qhotT, qT, oT, lse, hat1, scale1, first, first_low, cqT, mixT, start_low) = self_front(
        me, pair_tags[0], xs, tag_table, self_qkv, self_out, cross_query, norm_gain, norm_bias
    )
    for k in range(0, n, 2):
        enc_parts[k + 1] = exchange(once(enc_parts[k], (cqT, ogb)) if k else encoded[0], "seq", 1)
    encs = [enc_parts[k] for k in range(n)]
    terms1, (la, lb, g_mid, g_cb, gcT, cdelta, clse, cmixT, vec2, dib, ehot, ek, ev, *back1) = middle(
        cut1, me, enc_lengths[0], encs, cross_kv, cqT, qhotT, first, cross_out, ffn_in, ffn_out,
        b_in, b_out, norm_gain, norm_bias, oga, ogb,
    )
    lb = exchange(lb, "seq", mirror)
    layer_out = jnp.concatenate([la, lb])[None]
    token = g_mid
    if weights:
        sums1 = add_core(terms1[:-1], exchange(terms1[-1], "seq", 1), token)
        token = sums1[0]
        sums1 = across_chips(sums1)
    terms2, (g_start, gmT, delta, vec1, *back2) = cross_back(
        cut2, weights, me, ek, ev, token, encs, cross_kv, cqT, ehot, qhotT, gcT, clse, cdelta, g_mid, cross_query,
        hat1, scale1, norm_gain, self_out, oT, cmixT, g_cb, first_low, mixT,
    )
    token = g_start
    if weights:
        near1, far1 = add_chips(cut1, zme, sums1, (terms2[0],), pinned=True)
        token = near1
    sums2 = add_core(terms2[:-1], exchange(terms2[-1], "seq", 1), token)
    token = sums2[0]
    sums2 = across_chips(sums2)
    terms3, (small, *back3) = self_back(
        cut3, weights, me, pair_tags[0], token, low_all, K, V, khot, qT, qhotT, gmT, lse, delta, self_qkv,
        g_start, start_low, vec1, vec2, dib,
    )
    if weights:
        near12, far12, encoded_grad = add_chips(cut2, zme, sums2, (terms3[0], lb), near1, far1)
        sums3 = add_core(terms3[:-1], exchange(terms3[-1], "seq", 1), near12)
        got12 = exchange(once(far12, sums3[0]), "rows", 2)
        sums3 = across_chips(sums3)
        send12, kept12 = add_far(near12, got12)
        near3, far3, input_grad = add_chips(cut3, zme, sums3, (kept12,))
        got3 = exchange(far3, "rows", 2)
        share12 = add_near(kept12, exchange(send12, "rows", 1))
        shards12 = gather(once(share12, near3))
        send3, kept3 = add_far(near3, got3)
        share3, small = add_last(kept3, exchange(send3, "rows", 1), 16, shards12[2::2])
        ins, outs = 512 // zsize, 2048 // zsize

        def layout(places):
            found, at = [], 0
            for out, R, left, C in places:
                found.append((out, R, left, C, at))
                at += R // chips * (C // 512)
            return found

        places = [(0, ins, 0, 2048), (1, outs, 0, 512), (2, ins, 0, 1024)] + [(j, ins, 0, 512) for j in (3, 4, 5)]
        shapes = [(ins, 2048), (outs, 512), (ins, 1024), (ins, 512), (ins, 512), (ins, 512)]
        d_fi, d_fo, d_ckv, d_co, d_cq, d_so = unpack_shards(me, shards12, shapes, layout(places))
        shards3 = gather(share3, d_fi)
        places = [(0, ins, 512 * j, 512) for j in range(3)]
        d_qkv = unpack_shards(me, shards3, [(ins, 1536)], layout(places))[0]
        tags, wide, lanes = NTAGS // zsize, outs // 256, 512 // zsize
        d_table = jnp.concatenate([small[0:tags], small[tags : 2 * tags]], axis=1)
        d_inner = small[2 * tags : 2 * tags + wide].reshape(-1)
        vectors = small[2 * tags + wide : 2 * tags + wide + 4].reshape(8, lanes)
    else:
        encoded_grad, input_grad = (
            total([jnp.concatenate([t[:BLK], t[BLK:]], axis=1) for t in terms])
            for terms in (sums2, across_chips(add_core(terms3[:-1], exchange(terms3[-1], "seq", 1), small)))
        )
        (hidden, second_low, g_ffn, g_pre), (edkv, dcq, g_branch), (dkv, dq) = back1, back2, back3
        enc_all = jnp.concatenate(encs)
        pairs = [
            (second_low, g_pre, False), (hidden, g_ffn, False), (enc_all, edkv, False), (cmixT, g_cb, True),
            (first_low, dcq, False), (mixT, g_branch, True), (start_low, dq, False), (low_all, dkv, False),
        ]
        small = jnp.concatenate([small[:NTAGS], dib.reshape(4, 512), small[NTAGS:]])
        (d_fi, d_fo, d_ckv, d_co, d_cq, d_so, dq, dkv), (d_table, d_inner, vectors) = plain_weights(pairs, small)
        d_qkv = jnp.concatenate([dq, dkv], axis=1)
    return (
        layer_out, input_grad[None], encoded_grad[None], d_table, d_qkv, d_so, d_cq, d_ckv, d_co, d_fi, d_inner, d_fo,
        vectors[6], vectors[0:3], vectors[3:6],
    )


def solution(mesh):
    tokens = P("rows", "seq", None)
    placed = (tokens, tokens, P("rows", "seq"), P("rows", None), P("rows", None), tokens) + (P(),) * 12
    rows = P("rows", None)
    return jax.shard_map(
        local,
        mesh=mesh,
        in_specs=placed,
        out_specs=(tokens, tokens, tokens)
        + (rows,) * 7
        + (P("rows"), rows, P("rows"), P(None, "rows"), P(None, "rows")),
        check_vma=False,
    )
```

```python
import jax
import jax.numpy as jnp
from jax import lax
from jax.experimental import pallas as pl
from jax.experimental.pallas import tpu as pltpu
from jax.sharding import PartitionSpec as P

F32 = jnp.float32
BF = jnp.bfloat16
SEGS = 4
NTAGS = 16
BLK = 256
HALF = 128
TILE = 512
BIG = -1e30
LEAST = 1e-25
EPS = 1e-5
TN = ((0,), (0,))
NT = ((1,), (1,))
VM = pl.BlockSpec(memory_space=pltpu.VMEM)
SM = pl.BlockSpec(memory_space=pltpu.SMEM)
ANY = pl.BlockSpec(memory_space=pl.ANY)
HB = pl.BlockSpec(memory_space=pltpu.HBM)
SENT = "sent"
TOKEN = jax.ShapeDtypeStruct((8, 128), F32)


def shape(dims, dtype=BF):
    return jax.ShapeDtypeStruct(dims, dtype)


TIMES = {
    "self_front": 16, "middle": 20, "cross_back": 18, "self_back": 18, "add_core": 3, "add_chips": 20, "prepare": 2,
    "join_tokens": 2, "add_far": 2, "add_near": 2, "add_last": 2, "unpack_shards": 3,
}


LIMITS = {
    "self_front": 20, "middle": 32, "cross_back": 28, "self_back": 34, "add_core": 8, "add_chips": 10, "prepare": 4,
    "join_tokens": 4, "add_far": 4, "add_near": 4, "add_last": 4, "unpack_shards": 12,
}


class Outgoing:
    def __init__(self, ref, target, sems):
        self.ref, self.target, self.sems, self.copies = ref, target, sems, []

    def send(self, *index):
        pair = (self.ref.at[index], self.target.at[index]) if index else (self.ref, self.target)
        self.copies.append(pltpu.make_async_copy(*pair, self.sems.at[len(self.copies)]))
        self.copies[-1].start()


def call(kernel, name, ins, specs, outs, out_specs=None, scratch=(), blocks=8):
    outs, out_specs = list(outs), list(out_specs or (VM,) * len(outs))
    ins = [pltpu.with_memory_space_constraint(x, pltpu.HBM) if spec is HB else x for x, spec in zip(ins, specs)]
    sent = [j for j, spec in enumerate(out_specs) if spec is SENT]
    more = [pltpu.VMEM(outs[j].shape, outs[j].dtype) for j in sent]
    more += [pltpu.SemaphoreType.DMA((len(sent), 2))] if sent else []

    def body(*refs):
        if not sent:
            return kernel(*refs)
        refs, mine, sems = list(refs[: -len(more)]), refs[-len(more) : -1], refs[-1]
        going = []
        for at, j in enumerate(sent):
            going.append(Outgoing(mine[at], refs[len(ins) + j], sems.at[at]))
            refs[len(ins) + j] = going[-1]
        kernel(*refs)
        for out in going:
            if not out.copies:
                out.send()
        for out in going:
            for copy in out.copies:
                copy.wait()

    return pl.pallas_call(
        body,
        out_shape=tuple(pltpu.HBM(o.shape, o.dtype) if s in (SENT, HB) else o for o, s in zip(outs, out_specs)),
        in_specs=list(specs),
        out_specs=tuple(HB if spec is SENT else spec for spec in out_specs),
        scratch_shapes=list(scratch) + more,
        compiler_params=pltpu.CompilerParams(vmem_limit_bytes=min(60, LIMITS[name] * blocks // 8) << 20),
        cost_estimate=pl.CostEstimate(flops=TIMES[name] * 10**9, bytes_accessed=1, transcendentals=0),
        name=name,
    )(*ins)


def dot(a, b, dims=((1,), (0,))):
    return lax.dot_general(a, b, (dims, ((), ())), preferred_element_type=F32)


def total(terms):
    out = terms[0].astype(F32)
    for term in terms[1:]:
        out = out + term.astype(F32)
    return out


def build_blocks(src_ref, extra_ref, dst_ref):
    z = jnp.zeros((64, HALF), BF)
    for p in range(4):
        for h in range(2):
            c = slice(h * HALF, (h + 1) * HALF)
            dst_ref[2 * p + h, 0:64, :] = jnp.concatenate([src_ref[128 * p : 128 * p + 64, c], z], 1)
            dst_ref[2 * p + h, 64:128, :] = jnp.concatenate([z, src_ref[128 * p + 64 : 128 * p + 128, c]], 1)
            if extra_ref is not None:
                e = extra_ref[:, c]
                dst_ref[2 * p + h, 128:144, :] = jnp.concatenate([e, e], 1)
                dst_ref[2 * p + h, 144:256, :] = jnp.zeros((112, 256), BF)


def bound_scores(q_ref, k_ref, qhot_ref, qb):
    S = k_ref.shape[0]
    top = jnp.zeros((1, 512), F32)
    for r in range(S // 512):
        rows = jnp.abs(k_ref[512 * r : 512 * r + 512, :].astype(F32))
        top = jnp.maximum(top, jnp.max(rows, axis=0, keepdims=True))
    head = lax.broadcasted_iota(jnp.int32, (16, 512), 1) // 64
    table = jnp.where(head == lax.broadcasted_iota(jnp.int32, (16, 512), 0), top * 1.02, 0.0).astype(BF)
    bound = (dot(table, jnp.abs(q_ref[...])) * 1.02).astype(BF).astype(F32)
    shift = []
    row = lax.broadcasted_iota(jnp.int32, (16, 256), 0)
    for p in range(4):
        for h in range(2):
            c = slice(h * HALF, (h + 1) * HALF)
            shift.append(jnp.concatenate([bound[2 * p : 2 * p + 1, c], bound[2 * p + 1 : 2 * p + 2, c]], 1))
            extra = jnp.concatenate([qhot_ref[:, c], qhot_ref[:, c]], 1).astype(F32)
            qb[2 * p + h, 128:144, :] = jnp.where(row == SEGS, -shift[-1], extra).astype(BF)
    return shift


def split_heads(j, a, o_ref):
    p, h = j // 2, j % 2
    if not isinstance(j, int):
        p, h = pl.multiple_of(128 * p, 128), pl.multiple_of(h * HALF, HALF)
    else:
        p, h = 128 * p, h * HALF
    o_ref[pl.ds(p, 64), pl.ds(h, HALF)] = a[0:64, 0:HALF]
    o_ref[pl.ds(p + 64, 64), pl.ds(h, HALF)] = a[64:128, HALF:]


def pair_of(p):
    return pl.ds(pl.multiple_of(128 * p, 128), 128)


def cross_forward(q_ref, k_ref, vt_ref, khot_ref, qhot_ref, o_ref, lse_ref, qb, least_ref):
    build_blocks(q_ref, qhot_ref, qb)
    shift = bound_scores(q_ref, k_ref, qhot_ref, qb)
    for j in range(8):
        lse_ref[j] = shift[j]

    @pl.loop(0, 4)
    def _(p):
        pair = pair_of(p)
        for h in range(2):
            j = 2 * p + h
            whole = jnp.zeros((1, 256), F32)
            acc = jnp.zeros((128, 256), F32)
            for t in range(k_ref.shape[0] // TILE):
                rows = slice(t * TILE, (t + 1) * TILE)
                kt = jnp.concatenate([k_ref[rows, pair], khot_ref[rows, :]], 1)
                e = jnp.exp(dot(kt, qb[j]))
                whole = whole + jnp.sum(e, axis=0, keepdims=True)
                acc = acc + dot(vt_ref[pair, rows], e.astype(BF))
            least_ref[j] = whole
            lse_ref[j] = lse_ref[j] + jnp.log(whole)
            split_heads(j, acc * (1.0 / whole), o_ref)

    @pl.when(jnp.min(least_ref[...]) < LEAST)
    def _():
        cross_forward_exact(q_ref, k_ref, vt_ref, khot_ref, qhot_ref, o_ref, lse_ref, qb)


def cross_forward_exact(q_ref, k_ref, vt_ref, khot_ref, qhot_ref, o_ref, lse_ref, qb):
    build_blocks(q_ref, qhot_ref, qb)
    tiles = k_ref.shape[0] // TILE

    @pl.loop(0, 8)
    def _(j):
        pair = pair_of(j // 2)

        def scores(t):
            rows = pl.ds(t * TILE, TILE)
            return dot(jnp.concatenate([k_ref[rows, pair], khot_ref[rows, :]], 1), qb[j])

        top = jnp.max(scores(0), axis=0, keepdims=True)
        for t in range(1, tiles):
            top = jnp.maximum(top, jnp.max(scores(t), axis=0, keepdims=True))
        whole = jnp.zeros((1, 256), F32)
        acc = jnp.zeros((128, 256), F32)
        for t in range(tiles):
            e = jnp.exp(scores(t) - top)
            whole = whole + jnp.sum(e, axis=0, keepdims=True)
            acc = acc + dot(vt_ref[pair, t * TILE : (t + 1) * TILE], e.astype(BF))
        lse_ref[j] = top + jnp.log(whole)
        split_heads(j, acc * (1.0 / whole), o_ref)


def cross_backward(q_ref, k_ref, v_ref, khot_ref, qhot_ref, do_ref, lse_ref, dl_ref, dq_ref, dkv_ref, qb, db):
    build_blocks(q_ref, qhot_ref, qb)
    build_blocks(do_ref, None, db)
    size = min(2048, k_ref.shape[0])

    @pl.loop(0, 4)
    def _(p):
        pair = pair_of(p)
        dq = [0.0, 0.0]
        for t in range(k_ref.shape[0] // size):
            rows = slice(t * size, (t + 1) * size)
            k, v = k_ref[rows, pair], v_ref[rows, pair]
            k_turned = k.T
            kt = jnp.concatenate([k, khot_ref[rows, :]], 1)
            dk = dv = 0.0
            for h in range(2):
                j = 2 * p + h
                pr = jnp.exp(dot(kt, qb[j]) - lse_ref[j])
                dp = dot(v, db[j])
                ds = (pr * (dp - dl_ref[j])).astype(BF)
                dv += dot(pr.astype(BF), db[j], NT)
                dk += dot(ds, qb[j, 0:128, :], NT)
                dq[h] += dot(k_turned, ds)
            dkv_ref[rows, pair] = dk.astype(BF)
            dkv_ref[rows, pl.ds(pl.multiple_of(512 + 128 * p, 128), 128)] = dv.astype(BF)
        for h in range(2):
            split_heads(2 * p + h, dq[h] * 0.125, dq_ref)


def work_item(t, i, blocks):
    first = (i + 2) // 2
    second = (t >= first).astype(jnp.int32)
    tile = t - second * first
    start = jnp.where(second == 1, (blocks - 1 - i) * BLK + HALF, i * BLK)
    return second, tile, start - tile * TILE


def relative_positions(swap):
    k = lax.broadcasted_iota(jnp.int32, (TILE, 2 * HALF), 0)
    q = lax.broadcasted_iota(jnp.int32, (TILE, 2 * HALF), 1) & (HALF - 1)
    return (k ^ swap) - q


def self_tiles(blocks, i, full, masked):
    for h, block in ((0, i), (1, blocks - 1 - i)):
        last = block >> 1
        place = lambda tile: pl.multiple_of((tile ^ (i >> 1)) * TILE, TILE)
        pl.loop(0, last)(lambda tile, h=h: full(h, place(tile)))
        masked(h, place(last), (block & 1) * BLK + h * HALF)


def self_forward(blocks, i, q_ref, k_ref, vt_ref, khot_ref, qhot_ref, o_ref, lse_ref, qb, m_s, l_s, acc):
    build_blocks(q_ref, qhot_ref, qb)
    shift = bound_scores(q_ref, k_ref, qhot_ref, qb)
    l_s[...] = jnp.zeros(l_s.shape, F32)
    acc[...] = jnp.zeros(acc.shape, F32)

    def visit(h, r0, offset=None):
        rows = pl.ds(r0, TILE)
        hot = khot_ref[rows, :]
        for p in range(4):
            j = 2 * p + h
            s = dot(jnp.concatenate([k_ref[rows, 128 * p : 128 * p + 128], hot], 1), qb[j])
            if offset is not None:
                s = jnp.where(relative_positions((i & 1) * BLK) <= offset, s, BIG)
            e = jnp.exp(s)
            l_s[j] += jnp.sum(e, axis=0, keepdims=True)
            acc[j] += dot(vt_ref[128 * p : 128 * p + 128, rows], e.astype(BF))

    self_tiles(blocks, i, visit, visit)
    for j in range(8):
        lse_ref[j] = shift[j] + jnp.log(l_s[j])
        split_heads(j, acc[j] * (1.0 / l_s[j]), o_ref)

    @pl.when(jnp.min(l_s[...]) < LEAST)
    def _():
        self_forward_exact(blocks, i, q_ref, k_ref, vt_ref, khot_ref, qhot_ref, o_ref, lse_ref, qb, m_s, l_s, acc)


def self_forward_exact(blocks, i, q_ref, k_ref, vt_ref, khot_ref, qhot_ref, o_ref, lse_ref, qb, m_s, l_s, acc):
    build_blocks(q_ref, qhot_ref, qb)
    swap = (i & 1) * BLK
    items = blocks // 2 + 1
    m_s[...] = jnp.full(m_s.shape, -3e38, F32)
    l_s[...] = jnp.zeros(l_s.shape, F32)
    acc[...] = jnp.zeros(acc.shape, F32)

    def scores(t, p):
        h, tile, offset = work_item(t, i, blocks)
        r0 = pl.multiple_of((tile ^ (i >> 1)) * TILE, TILE)
        kt = jnp.concatenate([k_ref[pl.ds(r0, TILE), pair_of(p)], khot_ref[pl.ds(r0, TILE), :]], 1)
        return jnp.where(relative_positions(swap) <= offset, dot(kt, qb[2 * p + h]), BIG), 2 * p + h, r0

    @pl.loop(0, 4 * items)
    def _(step):
        s, j, _ = scores(step // 4, step % 4)
        m_s[j] = jnp.maximum(m_s[j], jnp.max(s, axis=0, keepdims=True))

    @pl.loop(0, 4 * items)
    def _(step):
        s, j, r0 = scores(step // 4, step % 4)
        e = jnp.exp(s - m_s[j])
        l_s[j] += jnp.sum(e, axis=0, keepdims=True)
        acc[j] += dot(vt_ref[pair_of(step % 4), pl.ds(r0, TILE)], e.astype(BF))

    for j in range(8):
        lse_ref[j] = m_s[j] + jnp.log(l_s[j])
        split_heads(j, acc[j] * (1.0 / l_s[j]), o_ref)


def self_backward(
    blocks, i, q_ref, k_ref, kt_ref, v_ref, khot_ref, qhot_ref, do_ref, lse_ref, dl_ref, dq_ref, dkv_ref,
    qb, db, dqa, dka, dva,
):
    build_blocks(q_ref, qhot_ref, qb)
    build_blocks(do_ref, None, db)
    dqa[...] = jnp.zeros(dqa.shape, F32)
    dka[...] = jnp.zeros(dka.shape, F32)
    dva[...] = jnp.zeros(dva.shape, F32)

    def visit(h, r0, offset=None):
        rows = pl.ds(r0, TILE)
        hot = khot_ref[rows, :]
        for p in range(4):
            j = 2 * p + h
            lanes = slice(128 * p, 128 * p + 128)
            s = dot(jnp.concatenate([k_ref[rows, lanes], hot], 1), qb[j])
            if offset is not None:
                s = jnp.where(relative_positions((i & 1) * BLK) <= offset, s, BIG)
            pr = jnp.exp(s - lse_ref[j])
            dp = dot(v_ref[rows, lanes], db[j])
            ds = (pr * (dp - dl_ref[j])).astype(BF)
            dva[rows, lanes] += dot(pr.astype(BF), db[j], NT)
            dka[rows, lanes] += dot(ds, qb[j, 0:128, :], NT)
            dqa[j] += dot(kt_ref[lanes, rows], ds)

    self_tiles(blocks, i, visit, visit)
    dkv_ref[:, 0:512] = dka[...].astype(BF)
    dkv_ref[:, 512:1024] = dva[...].astype(BF)
    for j in range(8):
        split_heads(j, dqa[j] * 0.125, dq_ref)


def norm_forward(v, gain, bias):
    centered = v - jnp.mean(v, axis=-1, keepdims=True)
    scale = lax.rsqrt(jnp.mean(centered * centered, axis=-1, keepdims=True) + EPS)
    hat = centered * scale
    return hat * gain + bias, hat, scale


def norm_backward(g, hat, scale, gain):
    gh = g * gain
    out = scale * (gh - jnp.mean(gh, axis=-1, keepdims=True) - hat * jnp.mean(gh * hat, axis=-1, keepdims=True))
    return out, jnp.sum(g * hat, axis=0, keepdims=True), jnp.sum(g, axis=0, keepdims=True)


def gelu_both(x):
    c = 0.7978845608028654
    sq = x * x
    t = jnp.tanh(c * x * (1 + 0.044715 * sq))
    half = 0.5 * (1 + t)
    return x * half, half + 0.5 * x * (1 - t * t) * (c * (1 + 3 * 0.044715 * sq))


def inner_rows(g_refT, o_ref, dl_ref):
    for p in range(4):
        both = []
        for a in range(2):
            rows = slice(128 * p + 64 * a, 128 * p + 64 * a + 64)
            both.append(jnp.sum(g_refT[rows, :].astype(F32) * o_ref[rows, :], axis=0, keepdims=True))
        for h in range(2):
            cols = slice(h * HALF, (h + 1) * HALF)
            dl_ref[2 * p + h] = jnp.concatenate([both[0][:, cols], both[1][:, cols]], 1)


class Cut:
    def __init__(self, chips, zsize, tokens, sizes, extra=0):
        self.chips, self.zsize, self.tokens, self.extra = chips, zsize, tokens, extra
        self.at, rows = [], 0
        for R, C in sizes:
            self.at.append(rows)
            rows += R // (zsize * chips) * (C // 512)
        self.per_z = rows + extra
        self.rows = tokens + zsize * self.per_z

    def write(self, index, keep, me, evens, odd_ref):
        R, C = keep.shape
        core, chip = me & 1, me >> 1
        size, half = R // (self.zsize * self.chips), C // 2
        for turn in range(2):
            side = core if turn == 0 else 1 - core
            for j in range(self.chips):
                for z in range(self.zsize):
                    row = pl.multiple_of(z * (R // self.zsize) + (chip ^ j) * size, size)
                    for c in range(half // 256):
                        left = pl.multiple_of(side * half + 256 * c, 256)
                        at = self.tokens + z * self.per_z + self.at[index] + c * size
                        piece = keep[pl.ds(row, size), pl.ds(left, 256)]
                        if turn == 0:
                            evens[j][at : at + size, :] = piece
                        else:
                            odd_ref[j, at : at + size, :] = piece

    def write_tokens(self, r, part, evens, odd_ref):
        for c in range(2):
            piece = part[:, 256 * c : 256 * c + 256]
            if r % 2:
                odd_ref[r // 2, BLK * c : BLK * c + BLK, :] = piece
            else:
                evens[r // 2][BLK * c : BLK * c + BLK, :] = piece

    def write_extra(self, z, part, evens, odd_ref):
        at = self.tokens + z * self.per_z + self.per_z - self.extra
        for j in range(self.chips):
            evens[j][at : at + self.extra, :] = part
            odd_ref[j, at : at + self.extra, :] = part

    def outs(self):
        return [shape((self.rows, 256))] * self.chips + [shape((self.chips, self.rows, 256))]


def join_tokens(x, seg):
    def kernel(x_hbm, seg_hbm, out, seg_s, sems):
        loads = [
            pltpu.make_async_copy(x_hbm, out.ref.at[0:BLK, :], sems.at[0]),
            pltpu.make_async_copy(seg_hbm, seg_s, sems.at[1]),
        ]
        for copy in loads:
            copy.start()
        for copy in loads[::-1]:
            copy.wait()
            if copy is loads[1]:
                row = jnp.concatenate([seg_s[...].astype(F32), jnp.zeros((1, 256), F32)], 1)
                out.ref[BLK:, :] = jnp.broadcast_to(row, (16, 512)).astype(BF)

    scratch = [pltpu.VMEM((1, 256), jnp.int32), pltpu.SemaphoreType.DMA((2,))]
    return call(kernel, "join_tokens", (x, seg), [HB] * 2, [shape((BLK + 16, 512))], [SENT], scratch)[0]


def prepare(after, grad, *rest):
    def kernel(g_ref, *refs):
        ga_ref, gb_ref = refs[-2:]
        ga_ref[...] = g_ref[0:HALF, :]
        gb_ref[...] = g_ref[HALF:, :]

    ins = (grad, after, *rest)
    return call(
        kernel, "prepare", ins, [VM, HB] + [ANY] * (len(ins) - 2), [shape((HALF, 512)), shape((HALF, 512))], [VM, VM]
    )


def self_front_kernel(n, me_ref, tag_ref, *refs):
    xs, refs = refs[:n], refs[n:]
    (table_ref, w_ref, so_ref, cqw_ref, gain_ref, bias_ref,
     low_o, k_o, v_o, khot_o, qhot_ref, qT_o, oT_ref, lse_o, hat_ref, scale_ref, first_ref,
     flow_ref, cqT_ref, mixT_ref, slow_o, vt_s, start_s, qb, m_s, l_s, acc) = refs
    low_s, k_s, v_s, khot_s, qT_ref, lse_ref = (out.ref for out in (low_o, k_o, v_o, khot_o, qT_o, lse_o))
    segs = [x[BLK : BLK + 16, 0:BLK].astype(F32)[0:1].astype(jnp.int32) for x in xs]
    table = table_ref[...].astype(F32)
    ids = lax.broadcasted_iota(jnp.int32, (NTAGS, 512), 0)
    rows = [jnp.sum(jnp.where(ids == tag_ref[s], table, 0.0), axis=0, keepdims=True) for s in range(SEGS)]
    tag_rows = jnp.concatenate(rows + [jnp.zeros((128 - SEGS, 512), F32)], 0).astype(BF)
    for r in range(n):
        at = slice(r * BLK, (r + 1) * BLK)
        ids = lax.broadcasted_iota(jnp.int32, (128, BLK), 0)
        hot = (ids == segs[r]).astype(F32).T
        khot_s[at, :] = ((ids == segs[r]) | (ids == SEGS)).astype(F32).T.astype(BF)
        start = xs[r][0:BLK, :].astype(F32) + dot(hot.astype(BF), tag_rows)
        low = start.astype(BF)
        low_s[at, :] = low
        if r == 0:
            start_s[0:HALF, :] = start[0:HALF]
        if r == n - 1:
            start_s[HALF:, :] = start[HALF:]
        k_s[at, :] = dot(low, w_ref[:, 512:1024]).astype(BF)
        v = dot(low, w_ref[:, 1024:1536]).astype(BF)
        v_s[at, :] = v
        vt_s[:, at] = v.T
    for out in (low_o, k_o, v_o, khot_o):
        out.send()
    seg = jnp.concatenate([segs[0][:, 0:HALF], segs[n - 1][:, HALF:]], 1)
    ids = lax.broadcasted_iota(jnp.int32, (16, BLK), 0)
    qhot_ref[...] = jnp.where((ids != seg) & (ids < SEGS), BIG, 0.0).astype(BF)
    slow = start_s[...].astype(BF)
    slow_o.ref[...] = slow
    qT_ref[...] = (dot(slow, w_ref[:, 0:512]) * 0.125).astype(BF).T
    slow_o.send()
    qT_o.send()
    self_forward(n, me_ref[0], qT_ref, k_s, vt_s, khot_s, qhot_ref, oT_ref, lse_ref, qb, m_s, l_s, acc)
    mixT = oT_ref[...].astype(BF)
    mixT_ref[...] = mixT
    first, hat, scale = norm_forward(
        start_s[...] + dot(mixT, so_ref[...], TN), gain_ref[...].astype(F32)[0:1], bias_ref[...].astype(F32)[0:1]
    )
    hat_ref[...] = hat
    scale_ref[...] = jnp.broadcast_to(scale, (BLK, 128))
    first_ref[...] = first
    first_low = first.astype(BF)
    flow_ref[...] = first_low
    cqT_ref[...] = (dot(first_low, cqw_ref[...]) * 0.125).astype(BF).T


def self_front(me, tags, xs, table, w, so, cqw, gain, bias):
    n = len(xs)
    S = n * BLK
    big = [shape((S, 512)), shape((S, 512)), shape((S, 512)), shape((S, 128))]
    outs = big + [
        shape((16, BLK)), shape((512, BLK)), shape((512, BLK), F32), shape((8, 1, BLK), F32), shape((BLK, 512), F32),
        shape((BLK, 128), F32), shape((BLK, 512), F32), shape((BLK, 512)), shape((512, BLK)), shape((512, BLK)),
        shape((BLK, 512)),
    ]
    scratch = [
        pltpu.VMEM((512, S), BF), pltpu.VMEM((BLK, 512), F32), pltpu.VMEM((8, 256, 256), BF),
        pltpu.VMEM((8, 1, 256), F32), pltpu.VMEM((8, 1, 256), F32), pltpu.VMEM((8, 128, 256), F32),
    ]
    kinds = [SENT] * 4 + [VM, SENT, VM, SENT] + [VM] * 6 + [SENT]
    return call(
        lambda *refs: self_front_kernel(n, *refs), "self_front", (me, tags, *xs, table, w, so, cqw, gain, bias),
        [SM, SM] + [VM] * (n + 6), outs, kinds, scratch, n,
    )


def middle_kernel(n, cut, me_ref, len_ref, *refs):
    encs, refs = refs[:n], refs[n:]
    (w_ref, cqT_ref, qhot_ref, first_ref, co_ref, fi_ref, fo_ref, bi_ref, bo_ref, gain_ref, bias_ref,
     oga_ref, ogb_ref, *refs) = refs
    if cut:
        evens, (odd_ref, *refs) = refs[: cut.chips], refs[cut.chips :]
    (la_ref, lb_ref, gmid_ref, gcb_ref, gcT_ref, dl_ref, lse_ref, cmixT_ref, vec_o, dib_o, khot_ref, k_ref, v_ref,
     hid_ref, slow_ref, gffn_ref, gpre_ref, k_s, v_s, vt_s, oT_s, slope_s, qb, least_s, fi_s, fo_s, sems) = refs
    me, vec_ref, dib_ref = me_ref[0], vec_o.ref, dib_o.ref
    e0 = len_ref[0]
    e1 = e0 + len_ref[1]
    e2 = e1 + len_ref[2]
    for r in range(n):
        at = slice(r * BLK, (r + 1) * BLK)
        pos = lax.broadcasted_iota(jnp.int32, (BLK, 128), 0) + (me ^ r) * BLK
        seg = (pos >= e0).astype(jnp.int32) + (pos >= e1).astype(jnp.int32) + (pos >= e2).astype(jnp.int32)
        lane = lax.broadcasted_iota(jnp.int32, (BLK, 128), 1)
        khot_ref[at, :] = ((lane == seg) | (lane == SEGS)).astype(F32).astype(BF)
        enc = encs[r][...]
        k_s[at, :] = dot(enc, w_ref[:, 0:512]).astype(BF)
        v = dot(enc, w_ref[:, 512:1024]).astype(BF)
        v_s[at, :] = v
        vt_s[:, at] = v.T
    copies = [pltpu.make_async_copy(k_s, k_ref, sems.at[0]), pltpu.make_async_copy(v_s, v_ref, sems.at[1])]
    for copy in copies:
        copy.start()
    cross_forward(cqT_ref, k_s, vt_s, khot_ref, qhot_ref, oT_s, lse_ref, qb, least_s)
    cmixT = oT_s[...].astype(BF)
    cmixT_ref[...] = cmixT
    gain_rows, bias_rows = gain_ref[...].astype(F32), bias_ref[...].astype(F32)
    gains = [gain_rows[j : j + 1] for j in range(3)]
    shifts = [bias_rows[j : j + 1] for j in range(3)]
    second, hat2, scale2 = norm_forward(first_ref[...] + dot(cmixT, co_ref[...], TN), gains[1], shifts[1])
    second_low = second.astype(BF)
    slow_ref[...] = second_low
    out = second + bo_ref[...].astype(F32)
    for c in range(4):
        cols = slice(512 * c, 512 * c + 512)
        act, slope = gelu_both(dot(second_low, fi_ref[:, cols]) + bi_ref[:, cols].astype(F32))
        hidden = act.astype(BF)
        hid_ref[:, cols] = hidden
        slope_s[:, cols] = slope
        out = out + dot(hidden, fo_ref[cols, :])
    result, hat3, scale3 = norm_forward(out, gains[2], shifts[2])
    la_ref[...] = result[0:HALF].astype(BF)
    lb_ref[...] = result[HALF:].astype(BF)
    og = jnp.concatenate([oga_ref[...], ogb_ref[...]], 0).astype(F32)
    g3, gg3, gb3 = norm_backward(og, hat3, scale3, gains[2])
    g_ffn = g3.astype(BF)
    gffn_ref[...] = g_ffn
    d_out_bias = jnp.sum(g_ffn.astype(F32), axis=0, keepdims=True)
    g2 = g3
    for c in range(4):
        cols = slice(512 * c, 512 * c + 512)
        g_pre = (dot(g_ffn, fo_ref[cols, :], NT) * slope_s[:, cols]).astype(BF)
        gpre_ref[:, cols] = g_pre
        dib_ref[:, cols] = jnp.sum(g_pre.astype(F32), axis=0, keepdims=True)
        g2 = g2 + dot(g_pre, fi_ref[:, cols], NT)
        if cut:
            fi_s[:, cols] = dot(second_low, g_pre, TN).astype(BF)
            fo_s[cols, :] = dot(hid_ref[:, cols], g_ffn, TN).astype(BF)
    g_mid, gg2, gb2 = norm_backward(g2, hat2, scale2, gains[1])
    gmid_ref[...] = g_mid
    g_cb = g_mid.astype(BF)
    gcb_ref[...] = g_cb
    gcT_ref[...] = dot(co_ref[...], g_cb, NT).astype(BF)
    inner_rows(gcT_ref, oT_s, dl_ref)
    vec_ref[...] = jnp.concatenate([gg2, gb2, gg3, gb3, d_out_bias, jnp.zeros((3, 512), F32)], 0)
    if cut:
        cut.write(0, fi_s, me, evens, odd_ref)
        cut.write(1, fo_s, me, evens, odd_ref)
    for copy in copies:
        copy.wait()


def middle(cut, me, lens, encs, *rest):
    n = len(encs)
    S = n * BLK
    outs = (cut.outs() if cut else []) + [
        shape((HALF, 512)), shape((HALF, 512)), shape((BLK, 512), F32), shape((BLK, 512)), shape((512, BLK)),
        shape((8, 1, 256), F32), shape((8, 1, 256), F32), shape((512, BLK)), shape((8, 512), F32),
        shape((1, 2048), F32), shape((S, 128)), shape((S, 512)), shape((S, 512)),
    ]
    hold = [shape((BLK, 2048)), shape((BLK, 512)), shape((BLK, 512)), shape((BLK, 2048))]
    kinds = [VM] * (len(outs) - 5) + [SENT] * 2 + [VM] + [HB] * 2
    plain = [] if cut else hold
    outs += plain
    kinds += [VM] * len(plain)
    scratch = ([pltpu.VMEM(x.shape, BF) for x in hold] if cut else []) + [
        pltpu.VMEM((S, 512), BF), pltpu.VMEM((S, 512), BF), pltpu.VMEM((512, S), BF), pltpu.VMEM((512, BLK), F32),
        pltpu.VMEM((BLK, 2048), F32), pltpu.VMEM((8, 256, 256), BF), pltpu.VMEM((8, 1, 256), F32), pltpu.VMEM((512, 2048), BF),
        pltpu.VMEM((2048, 512), BF), pltpu.SemaphoreType.DMA((2,)),
    ]
    got = call(
        lambda *refs: middle_kernel(n, cut, *refs), "middle", (me, lens, *encs, *rest),
        [SM, SM] + [VM] * (n + 13), outs, kinds, scratch, n,
    )
    first = len(cut.outs()) if cut else 0
    return got[:first], got[first:]


def cross_back_kernel(n, cut, weights, me_ref, *refs):
    half = n // 2
    (k_s, v_s, _, *refs) = refs
    encs, refs = refs[:n], refs[n:]
    (w_ref, cqT_ref, khot_ref, qhot_ref, gcT_ref, lse_ref, dl_ref, gmid_ref, cqw_ref, hat_ref, scale_ref, gain_ref,
     so_ref, oT_ref, cmixT_ref, gcb_ref, flow_ref, mixT_ref, *refs) = refs
    going, (odd_ref, gstart, gmT, dl1, vec, *refs) = refs[:half], refs[half:]
    evens = [out.ref for out in going]
    gstart_ref, gmT_ref, dl1_ref, vec_ref = gstart.ref, gmT.ref, dl1.ref, vec.ref
    dkv_ref, dq_ref, gbr_ref, dqT_s, qb, db, enc_s, keep, kv_keep, sems = refs
    late = []
    if weights:
        for j in range(n):
            rows = slice(BLK * j, BLK * (j + 1))
            late.append(pltpu.make_async_copy(encs[j], enc_s.at[rows, :], sems.at[j]))
    for copy in late:
        copy.start()
    cross_backward(
        cqT_ref, k_s, v_s, khot_ref, qhot_ref, gcT_ref, lse_ref, dl_ref, dqT_s, dkv_ref, qb, db
    )
    me = me_ref[0]
    for r in range(n):
        at = slice(r * BLK, (r + 1) * BLK)
        part = dot(dkv_ref[at, :], w_ref[...], NT)
        cut.write_tokens(r, part.astype(BF), evens, odd_ref)
    if weights:
        for out in going:
            out.send(slice(0, 512))
    dq = dqT_s[...].astype(BF).T
    dq_ref[...] = dq
    g1 = gmid_ref[...] + dot(dq, cqw_ref[...], NT)
    g_start, gg1, gb1 = norm_backward(g1, hat_ref[...], scale_ref[:, 0:1], gain_ref[...].astype(F32)[0:1])
    gstart_ref[...] = g_start
    g_branch = g_start.astype(BF)
    gbr_ref[...] = g_branch
    gmT_ref[...] = dot(so_ref[...], g_branch, NT).astype(BF)
    inner_rows(gmT_ref, oT_ref, dl1_ref)
    vec_ref[...] = jnp.concatenate([gg1, gb1, jnp.zeros((6, 512), F32)], 0)
    for out in (gstart, gmT, dl1, vec):
        out.send()
    if weights:
        keep[0] = dot(cmixT_ref[...], gcb_ref[...]).astype(BF)
        keep[1] = dot(flow_ref[...], dq_ref[...], TN).astype(BF)
        keep[2] = dot(mixT_ref[...], g_branch).astype(BF)
        for j in range(3):
            cut.write(1 + j, keep.at[j], me, evens, odd_ref)
        for copy in late:
            copy.wait()
        kv_keep[...] = dot(enc_s[...], dkv_ref[...], TN).astype(BF)
        cut.write(0, kv_keep, me, evens, odd_ref)
        for out in going:
            out.send(slice(512, cut.rows))


def cross_back(cut, weights, me, k, v, after, encs, *rest):
    n = len(encs)
    S = n * BLK
    more = [shape((S, 1024)), shape((BLK, 512)), shape((BLK, 512))]
    outs = cut.outs() + [
        shape((BLK, 512), F32), shape((512, BLK)), shape((8, 1, 256), F32), shape((8, 512), F32)
    ] + ([] if weights else more)
    scratch = ([pltpu.VMEM(s.shape, s.dtype) for s in more] if weights else []) + [
        pltpu.VMEM((512, BLK), F32), pltpu.VMEM((8, 256, 256), BF), pltpu.VMEM((8, 128, 256), BF),
        pltpu.VMEM((S if weights else 16, 512), BF), pltpu.VMEM((3, 512, 512), BF), pltpu.VMEM((512, 1024), BF),
        pltpu.SemaphoreType.DMA((n,)),
    ]
    got = call(
        lambda *refs: cross_back_kernel(n, cut, weights, *refs), "cross_back", (me, k, v, after, *encs, *rest),
        [SM, VM, VM, HB if weights else ANY] + [ANY] * n + [VM] * 18,
        outs, [SENT] * (n // 2) + [VM] + [SENT] * 4 + [VM] * (len(outs) - n // 2 - 5), scratch, n,
    )
    return got[: n // 2 + 1], got[n // 2 + 1 :]


def self_back_kernel(n, cut, weights, me_ref, tag_ref, *refs):
    half = n // 2
    (_, low_hbm, k_s, v_s, khot_s, qT_ref, qhot_ref, gmT_ref, lse_ref, dl_ref, w_ref,
     gstart_ref, slow_ref, vec1_ref, vec2_ref, dib_ref, *refs) = refs
    evens, (odd_ref, small_ref, *refs) = refs[:half], refs[half:]
    (dkv_ref, dq_ref, low_s, kt_s, dqT_s, qb, db, dqa, dka, dva, keep, sems) = refs
    if weights:
        low_copy = pltpu.make_async_copy(low_hbm, low_s, sems.at[0])
        low_copy.start()
    for r in range(n):
        at = slice(r * BLK, (r + 1) * BLK)
        kt_s[:, at] = k_s[at, :].T
    me = me_ref[0]
    self_backward(
        n, me, qT_ref, k_s, kt_s, v_s, khot_s, qhot_ref, gmT_ref, lse_ref, dl_ref, dqT_s, dkv_ref,
        qb, db, dqa, dka, dva,
    )
    dq = dqT_s[...].astype(BF).T
    dq_ref[...] = dq
    mine = gstart_ref[...] + dot(dq, w_ref[:, 0:512], NT)
    sums = jnp.zeros((128, 512), F32)
    for r in range(n):
        at = slice(r * BLK, (r + 1) * BLK)
        part = dot(dkv_ref[at, :], w_ref[:, 512:1536], NT)
        if r == 0:
            part = jnp.concatenate([part[:HALF] + mine[:HALF], part[HALF:]], 0)
        if r == n - 1:
            part = jnp.concatenate([part[:HALF], part[HALF:] + mine[HALF:]], 0)
        part = part.astype(BF)
        sums = sums + dot(khot_s[at, :], part, TN)
        cut.write_tokens(r, part, evens, odd_ref)
    ids = lax.broadcasted_iota(jnp.int32, (NTAGS, 512), 0)
    table = jnp.zeros((NTAGS, 512), F32)
    for s in range(SEGS):
        table = table + jnp.where(ids == tag_ref[s], sums[s : s + 1, :], 0.0)
    v1, v2 = vec1_ref[...], vec2_ref[...]
    vectors = [v1[0:1], v2[0:1], v2[2:3], v1[1:2], v2[1:2], v2[3:4], v2[4:5], jnp.zeros((1, 512), F32)]
    if weights:
        zs = cut.zsize
        wide, lanes, tags = 2048 // zs, 512 // zs, NTAGS // zs
        for z in range(zs):
            rows = []
            for c in range(2):
                rows.append(table[tags * z : tags * (z + 1), 256 * c : 256 * c + 256])
            rows += [dib_ref[:, wide * z + 256 * c : wide * z + 256 * (c + 1)] for c in range(wide // 256)]
            cut_rows = [v[:, lanes * z : lanes * (z + 1)] for v in vectors]
            rows += [jnp.concatenate(cut_rows[2 * c : 2 * c + 2], 1) for c in range(4)]
            used = 2 * tags + wide // 256 + 4
            rows.append(jnp.zeros((16 - used, 256), F32))
            cut.write_extra(z, jnp.concatenate(rows, 0).astype(BF), evens, odd_ref)
        small_ref[...] = jnp.zeros(small_ref.shape, F32)
        keep[:, 0:512] = dot(slow_ref[...], dq_ref[...], TN).astype(BF)
        low_copy.wait()
        keep[:, 512:1536] = dot(low_s[...], dkv_ref[...], TN).astype(BF)
        for j in range(3):
            cut.write(j, keep.at[:, 512 * j : 512 * j + 512], me, evens, odd_ref)
    else:
        small_ref[...] = jnp.concatenate([table] + vectors, 0)


def self_back(cut, weights, me, tags, after, low, k, v, khot, *rest):
    S = k.shape[0]
    n = S // BLK
    more = [shape((S, 1024)), shape((BLK, 512))]
    outs = cut.outs() + [shape((24, 512), F32)] + ([] if weights else more)
    scratch = ([pltpu.VMEM(s.shape, s.dtype) for s in more] if weights else []) + [
        pltpu.VMEM((S if weights else 16, 512), BF), pltpu.VMEM((512, S), BF),
        pltpu.VMEM((512, BLK), F32), pltpu.VMEM((8, 256, 256), BF), pltpu.VMEM((8, 128, 256), BF),
        pltpu.VMEM((8, 128, 256), F32), pltpu.VMEM((S, 512), F32), pltpu.VMEM((S, 512), F32),
        pltpu.VMEM((512, 1536), BF), pltpu.SemaphoreType.DMA((1,)),
    ]
    got = call(
        lambda *refs: self_back_kernel(n, cut, weights, *refs), "self_back",
        (me, tags, after, low, k, v, khot, *rest), [SM, SM, HB, HB] + [VM] * 14, outs, None, scratch, n,
    )
    return got[: n // 2 + 1], got[n // 2 + 1 :]


def add_core(evens, got, after):
    count = len(evens)

    def kernel(*refs):
        ins, got_ref, (first, *outs) = refs[:count], refs[count], refs[count + 2 :]
        for j, out_ref in enumerate([first.ref] + outs):
            out_ref[...] = (ins[j][...].astype(F32) + got_ref[j].astype(F32)).astype(BF)
            if j == 0:
                first.send()

    return call(
        kernel, "add_core", (*evens, got, after), [VM] * (count + 1) + [ANY], [shape(e.shape) for e in evens],
        [SENT] + [VM] * (count - 1),
    )


def add_chips(cut, zme, terms, after, near=None, far=None, pinned=False):
    count, per = len(terms), cut.per_z
    extra = [] if near is None else [near, far]
    base = extra[0].shape[1] if extra else 0

    def kernel(z_ref, *refs):
        ins, (near_ref, far_ref, *outs) = refs[:count], refs[count + len(after) + len(extra) :]
        s, sems = outs[-2:]
        loads = []
        for j in range(count):
            rows = slice(cut.tokens, cut.rows)
            loads.append(pltpu.make_async_copy(ins[j].at[rows, :], s.at[j, rows, :], sems.at[0, j]))
        for j in range(count if cut.tokens else 0):
            rows = slice(0, cut.tokens)
            loads.append(pltpu.make_async_copy(ins[j].at[rows, :], s.at[j, rows, :], sems.at[1, j]))
        for copy in loads:
            copy.start()
        if extra:
            early = refs[count + len(after) : count + len(after) + 2]
            near_ref[:, 0:base, :] = early[0][...]
            far_ref[:, 0:base, :] = early[1][...]
        for copy in loads[:count]:
            copy.wait()
        for k in range(4):
            row = pl.multiple_of(cut.tokens + (z_ref[0] ^ k) * per, 16)
            value = total([s[j, pl.ds(row, per), :] for j in range(count)]).astype(BF)
            (near_ref if k < 2 else far_ref)[k % 2, base : base + per, :] = value
        for copy in loads[count:]:
            copy.wait()
        for c in range(2 if cut.tokens else 0):
            part = total([s[j, BLK * c : BLK * c + BLK, :] for j in range(count)])
            outs[0][:, 256 * c : 256 * c + 256] = part

    outs = [shape((2, base + per, 256)), shape((2, base + per, 256))] + [shape((BLK, 512), F32)] * (cut.tokens > 0)
    return call(
        kernel, "add_chips", (zme, *terms, *after, *extra),
        [SM, HB] + [ANY] * (count - 1) + [HB if pinned else ANY] * len(after) + [VM] * len(extra), outs, None,
        [pltpu.VMEM((count, cut.rows, 256), BF), pltpu.SemaphoreType.DMA((2, count))],
    )


def add_far(near, got):
    def kernel(near_ref, got_ref, send_ref, keep_ref):
        send_ref[...] = (near_ref[1].astype(F32) + got_ref[1].astype(F32)).astype(BF)
        keep_ref[...] = near_ref[0].astype(F32) + got_ref[0].astype(F32)

    outs = [shape(near.shape[1:]), shape(near.shape[1:], F32)]
    return call(kernel, "add_far", (near, got), [VM] * 2, outs)


def add_near(kept, sent):
    def kernel(kept_ref, sent_ref, out_ref):
        out_ref[...] = (kept_ref[...] + sent_ref[...].astype(F32)).astype(BF)

    return call(kernel, "add_near", (kept, sent), [VM] * 2, [shape(kept.shape)])[0]


def add_last(kept, sent, extra, after):
    rows = kept.shape[0] - extra

    def kernel(kept_ref, sent_ref, *refs):
        out_ref, small_ref = refs[-2:]
        value = kept_ref[...] + sent_ref[...].astype(F32)
        out_ref[...] = value[:rows].astype(BF)
        small_ref[...] = value[rows:]

    return call(kernel, "add_last", (kept, sent, *after), [VM] * 2 + [ANY] * len(after), [shape((rows, 256)), shape((extra, 256), F32)])


def unpack_shards(me, shards, shapes, layout):
    n = len(shards)
    chips = n // 2

    def kernel(me_ref, *refs):
        parts, outs = refs[:n], refs[n:]
        me = me_ref[0]
        for k in range(n):
            chip, core = (me >> 1) ^ (k >> 1), (me & 1) ^ (k & 1)
            for out, R, left, C, at in layout:
                size, half = R // chips, C // 2
                row = pl.multiple_of(chip * size, size)
                for c in range(half // 256):
                    col = pl.multiple_of(left + core * half + 256 * c, 256)
                    value = parts[k][at + c * size : at + (c + 1) * size, :].astype(F32)
                    outs[out][pl.ds(row, size), pl.ds(col, 256)] = value

    return call(kernel, "unpack_shards", (me, *shards), [SM] + [VM] * n, [shape(s, F32) for s in shapes])


def exchange(x, axis, k):
    size = lax.axis_size(axis)
    return lax.ppermute(x, axis, [(i, i ^ k) for i in range(size)])


def once(x, after):
    return lax.optimization_barrier((x, after))[0]


def gather(x, after=None):
    n = lax.axis_size("seq")
    parts = {0: x}
    for k in range(2, n, 2):
        parts[k] = exchange(x, "seq", k)
    for k in range(0, n, 2):
        held = parts[k] if after is None or k == 0 else once(parts[k], after)
        parts[k + 1] = exchange(held, "seq", 1)
    return [parts[k] for k in range(n)]


def across_chips(mine):
    return [mine[0]] + [exchange(mine[j], "seq", 2 * j) for j in range(1, len(mine))]


def plain_weights(pairs, small):
    zsize, zme = lax.axis_size("rows"), lax.axis_index("rows")
    outs = []
    for left, right, turned in pairs:
        whole = lax.psum(dot(left, right, ((1,) if turned else (0,), (0,))), ("seq", "rows"))
        size = whole.shape[0] // zsize
        outs.append(lax.dynamic_slice_in_dim(whole, zme * size, size, 0))
    whole = lax.psum(small, ("seq", "rows"))
    parts = []
    for x, dim in ((whole[:NTAGS], 0), (whole[NTAGS : NTAGS + 4].reshape(-1), 0), (whole[NTAGS + 4 :], 1)):
        size = x.shape[dim] // zsize
        parts.append(lax.dynamic_slice_in_dim(x, zme * size, size, dim))
    return outs, parts


def local(
    dec_input, encoded, segment_ids, pair_tags, enc_lengths, out_grad, tag_table, self_qkv, self_out, cross_query,
    cross_kv, cross_out, ffn_in, ffn_in_bias, ffn_out, ffn_out_bias, norm_gain, norm_bias,
):
    n, zsize = lax.axis_size("seq"), lax.axis_size("rows")
    chips = n // 2
    me, zme = lax.axis_index("seq").astype(jnp.int32)[None], lax.axis_index("rows").astype(jnp.int32)[None]
    mirror = n - 1
    weights = zsize == 4 and 512 // (zsize * chips) >= 16
    square = (512, 512)
    cut1 = Cut(chips, zsize, 0, [(512, 2048), (2048, 512)]) if weights else None
    cut2 = Cut(chips, zsize, 512, [(512, 1024), square, square, square] if weights else [])
    cut3 = Cut(chips, zsize, 512, [square] * 3 if weights else [], 16 if weights else 0)

    message = join_tokens(dec_input[0], segment_ids)
    b_in, b_out = ffn_in_bias[None], ffn_out_bias[None]
    oga, ogb = prepare(message, out_grad[0], b_in, b_out)
    xs = gather(message, oga)
    mine = once(encoded[0], xs[2::2])
    enc_parts = {0: encoded[0]} | {k: exchange(mine, "seq", k) for k in range(2, n, 2)}
    ogb = exchange(once(ogb, xs[2::2]), "seq", mirror)
    (low_all, K, V, khot, qhotT, qT, oT, lse, hat1, scale1, first, first_low, cqT, mixT, start_low) = self_front(
        me, pair_tags[0], xs, tag_table, self_qkv, self_out, cross_query, norm_gain, norm_bias
    )
    for k in range(0, n, 2):
        enc_parts[k + 1] = exchange(once(enc_parts[k], (cqT, ogb)) if k else encoded[0], "seq", 1)
    encs = [enc_parts[k] for k in range(n)]
    terms1, (la, lb, g_mid, g_cb, gcT, cdelta, clse, cmixT, vec2, dib, ehot, ek, ev, *back1) = middle(
        cut1, me, enc_lengths[0], encs, cross_kv, cqT, qhotT, first, cross_out, ffn_in, ffn_out,
        b_in, b_out, norm_gain, norm_bias, oga, ogb,
    )
    lb = exchange(lb, "seq", mirror)
    layer_out = jnp.concatenate([la, lb])[None]
    token = g_mid
    if weights:
        sums1 = add_core(terms1[:-1], exchange(terms1[-1], "seq", 1), token)
        token = sums1[0]
        sums1 = across_chips(sums1)
    terms2, (g_start, gmT, delta, vec1, *back2) = cross_back(
        cut2, weights, me, ek, ev, token, encs, cross_kv, cqT, ehot, qhotT, gcT, clse, cdelta, g_mid, cross_query,
        hat1, scale1, norm_gain, self_out, oT, cmixT, g_cb, first_low, mixT,
    )
    token = g_start
    if weights:
        near1, far1 = add_chips(cut1, zme, sums1, (terms2[0],), pinned=True)
        token = near1
    sums2 = add_core(terms2[:-1], exchange(terms2[-1], "seq", 1), token)
    token = sums2[0]
    sums2 = across_chips(sums2)
    terms3, (small, *back3) = self_back(
        cut3, weights, me, pair_tags[0], token, low_all, K, V, khot, qT, qhotT, gmT, lse, delta, self_qkv,
        g_start, start_low, vec1, vec2, dib,
    )
    if weights:
        near12, far12, encoded_grad = add_chips(cut2, zme, sums2, (terms3[0], lb), near1, far1)
        sums3 = add_core(terms3[:-1], exchange(terms3[-1], "seq", 1), near12)
        got12 = exchange(once(far12, sums3[0]), "rows", 2)
        sums3 = across_chips(sums3)
        send12, kept12 = add_far(near12, got12)
        near3, far3, input_grad = add_chips(cut3, zme, sums3, (kept12,))
        got3 = exchange(far3, "rows", 2)
        share12 = add_near(kept12, exchange(send12, "rows", 1))
        shards12 = gather(once(share12, near3))
        send3, kept3 = add_far(near3, got3)
        share3, small = add_last(kept3, exchange(send3, "rows", 1), 16, shards12[2::2])
        ins, outs = 512 // zsize, 2048 // zsize

        def layout(places):
            found, at = [], 0
            for out, R, left, C in places:
                found.append((out, R, left, C, at))
                at += R // chips * (C // 512)
            return found

        places = [(0, ins, 0, 2048), (1, outs, 0, 512), (2, ins, 0, 1024)] + [(j, ins, 0, 512) for j in (3, 4, 5)]
        shapes = [(ins, 2048), (outs, 512), (ins, 1024), (ins, 512), (ins, 512), (ins, 512)]
        d_fi, d_fo, d_ckv, d_co, d_cq, d_so = unpack_shards(me, shards12, shapes, layout(places))
        shards3 = gather(share3, d_fi)
        places = [(0, ins, 512 * j, 512) for j in range(3)]
        d_qkv = unpack_shards(me, shards3, [(ins, 1536)], layout(places))[0]
        tags, wide, lanes = NTAGS // zsize, outs // 256, 512 // zsize
        d_table = jnp.concatenate([small[0:tags], small[tags : 2 * tags]], axis=1)
        d_inner = small[2 * tags : 2 * tags + wide].reshape(-1)
        vectors = small[2 * tags + wide : 2 * tags + wide + 4].reshape(8, lanes)
    else:
        encoded_grad, input_grad = (
            total([jnp.concatenate([t[:BLK], t[BLK:]], axis=1) for t in terms])
            for terms in (sums2, across_chips(add_core(terms3[:-1], exchange(terms3[-1], "seq", 1), small)))
        )
        (hidden, second_low, g_ffn, g_pre), (edkv, dcq, g_branch), (dkv, dq) = back1, back2, back3
        enc_all = jnp.concatenate(encs)
        pairs = [
            (second_low, g_pre, False), (hidden, g_ffn, False), (enc_all, edkv, False), (cmixT, g_cb, True),
            (first_low, dcq, False), (mixT, g_branch, True), (start_low, dq, False), (low_all, dkv, False),
        ]
        small = jnp.concatenate([small[:NTAGS], dib.reshape(4, 512), small[NTAGS:]])
        (d_fi, d_fo, d_ckv, d_co, d_cq, d_so, dq, dkv), (d_table, d_inner, vectors) = plain_weights(pairs, small)
        d_qkv = jnp.concatenate([dq, dkv], axis=1)
    return (
        layer_out, input_grad[None], encoded_grad[None], d_table, d_qkv, d_so, d_cq, d_ckv, d_co, d_fi, d_inner, d_fo,
        vectors[6], vectors[0:3], vectors[3:6],
    )


def solution(mesh):
    tokens = P("rows", "seq", None)
    placed = (tokens, tokens, P("rows", "seq"), P("rows", None), P("rows", None), tokens) + (P(),) * 12
    rows = P("rows", None)
    return jax.shard_map(
        local,
        mesh=mesh,
        in_specs=placed,
        out_specs=(tokens, tokens, tokens)
        + (rows,) * 7
        + (P("rows"), rows, P("rows"), P(None, "rows"), P(None, "rows")),
        check_vma=False,
    )
```

```python
import jax
import jax.numpy as jnp
from jax import lax
from jax.experimental import pallas as pl
from jax.experimental.pallas import tpu as pltpu
from jax.sharding import PartitionSpec as P

F32 = jnp.float32
BF = jnp.bfloat16
SEGS = 4
NTAGS = 16
BLK = 256
HALF = 128
TILE = 512
BIG = -1e30
LEAST = 1e-25
EPS = 1e-5
TN = ((0,), (0,))
NT = ((1,), (1,))
VM = pl.BlockSpec(memory_space=pltpu.VMEM)
SM = pl.BlockSpec(memory_space=pltpu.SMEM)
ANY = pl.BlockSpec(memory_space=pl.ANY)
HB = pl.BlockSpec(memory_space=pltpu.HBM)
SENT = "sent"
TOKEN = jax.ShapeDtypeStruct((8, 128), F32)


def shape(dims, dtype=BF):
    return jax.ShapeDtypeStruct(dims, dtype)


TIMES = {
    "self_front": 16, "middle": 20, "cross_back": 18, "self_back": 18, "add_core": 3, "add_chips": 20, "gate": 20, "prepare": 2,
    "join_tokens": 2, "add_far": 2, "add_near": 2, "add_last": 2, "unpack_shards": 3,
}


LIMITS = {
    "self_front": 20, "middle": 32, "cross_back": 28, "self_back": 34, "add_core": 8, "add_chips": 10, "prepare": 4,
    "join_tokens": 4, "gate": 2, "add_far": 4, "add_near": 4, "add_last": 4, "unpack_shards": 12,
}


class Outgoing:
    def __init__(self, ref, target, sems):
        self.ref, self.target, self.sems, self.copies = ref, target, sems, []

    def send(self, *index):
        pair = (self.ref.at[index], self.target.at[index]) if index else (self.ref, self.target)
        self.copies.append(pltpu.make_async_copy(*pair, self.sems.at[len(self.copies)]))
        self.copies[-1].start()


def call(kernel, name, ins, specs, outs, out_specs=None, scratch=(), blocks=8):
    outs, out_specs = list(outs), list(out_specs or (VM,) * len(outs))
    ins = [pltpu.with_memory_space_constraint(x, pltpu.HBM) if spec is HB else x for x, spec in zip(ins, specs)]
    sent = [j for j, spec in enumerate(out_specs) if spec is SENT]
    more = [pltpu.VMEM(outs[j].shape, outs[j].dtype) for j in sent]
    more += [pltpu.SemaphoreType.DMA((len(sent), 2))] if sent else []

    def body(*refs):
        if not sent:
            return kernel(*refs)
        refs, mine, sems = list(refs[: -len(more)]), refs[-len(more) : -1], refs[-1]
        going = []
        for at, j in enumerate(sent):
            going.append(Outgoing(mine[at], refs[len(ins) + j], sems.at[at]))
            refs[len(ins) + j] = going[-1]
        kernel(*refs)
        for out in going:
            if not out.copies:
                out.send()
        for out in going:
            for copy in out.copies:
                copy.wait()

    return pl.pallas_call(
        body,
        out_shape=tuple(pltpu.HBM(o.shape, o.dtype) if s in (SENT, HB) else o for o, s in zip(outs, out_specs)),
        in_specs=list(specs),
        out_specs=tuple(HB if spec is SENT else spec for spec in out_specs),
        scratch_shapes=list(scratch) + more,
        compiler_params=pltpu.CompilerParams(vmem_limit_bytes=min(60, LIMITS[name] * blocks // 8) << 20),
        cost_estimate=pl.CostEstimate(flops=TIMES[name] * 10**9, bytes_accessed=1, transcendentals=0),
        name=name,
    )(*ins)


def dot(a, b, dims=((1,), (0,))):
    return lax.dot_general(a, b, (dims, ((), ())), preferred_element_type=F32)


def total(terms):
    out = terms[0].astype(F32)
    for term in terms[1:]:
        out = out + term.astype(F32)
    return out


def build_blocks(src_ref, extra_ref, dst_ref):
    z = jnp.zeros((64, HALF), BF)
    for p in range(4):
        for h in range(2):
            c = slice(h * HALF, (h + 1) * HALF)
            dst_ref[2 * p + h, 0:64, :] = jnp.concatenate([src_ref[128 * p : 128 * p + 64, c], z], 1)
            dst_ref[2 * p + h, 64:128, :] = jnp.concatenate([z, src_ref[128 * p + 64 : 128 * p + 128, c]], 1)
            if extra_ref is not None:
                e = extra_ref[:, c]
                dst_ref[2 * p + h, 128:144, :] = jnp.concatenate([e, e], 1)
                dst_ref[2 * p + h, 144:256, :] = jnp.zeros((112, 256), BF)


def bound_scores(q_ref, k_ref, qhot_ref, qb):
    S = k_ref.shape[0]
    top = jnp.zeros((1, 512), F32)
    for r in range(S // 512):
        rows = jnp.abs(k_ref[512 * r : 512 * r + 512, :].astype(F32))
        top = jnp.maximum(top, jnp.max(rows, axis=0, keepdims=True))
    head = lax.broadcasted_iota(jnp.int32, (16, 512), 1) // 64
    table = jnp.where(head == lax.broadcasted_iota(jnp.int32, (16, 512), 0), top * 1.02, 0.0).astype(BF)
    bound = (dot(table, jnp.abs(q_ref[...])) * 1.02).astype(BF).astype(F32)
    shift = []
    row = lax.broadcasted_iota(jnp.int32, (16, 256), 0)
    for p in range(4):
        for h in range(2):
            c = slice(h * HALF, (h + 1) * HALF)
            shift.append(jnp.concatenate([bound[2 * p : 2 * p + 1, c], bound[2 * p + 1 : 2 * p + 2, c]], 1))
            extra = jnp.concatenate([qhot_ref[:, c], qhot_ref[:, c]], 1).astype(F32)
            qb[2 * p + h, 128:144, :] = jnp.where(row == SEGS, -shift[-1], extra).astype(BF)
    return shift


def split_heads(j, a, o_ref):
    p, h = j // 2, j % 2
    if not isinstance(j, int):
        p, h = pl.multiple_of(128 * p, 128), pl.multiple_of(h * HALF, HALF)
    else:
        p, h = 128 * p, h * HALF
    o_ref[pl.ds(p, 64), pl.ds(h, HALF)] = a[0:64, 0:HALF]
    o_ref[pl.ds(p + 64, 64), pl.ds(h, HALF)] = a[64:128, HALF:]


def pair_of(p):
    return pl.ds(pl.multiple_of(128 * p, 128), 128)


def cross_forward(q_ref, k_ref, vt_ref, khot_ref, qhot_ref, o_ref, lse_ref, qb, least_ref):
    build_blocks(q_ref, qhot_ref, qb)
    shift = bound_scores(q_ref, k_ref, qhot_ref, qb)
    for j in range(8):
        lse_ref[j] = shift[j]

    @pl.loop(0, 4)
    def _(p):
        pair = pair_of(p)
        for h in range(2):
            j = 2 * p + h
            whole = jnp.zeros((1, 256), F32)
            acc = jnp.zeros((128, 256), F32)
            for t in range(k_ref.shape[0] // TILE):
                rows = slice(t * TILE, (t + 1) * TILE)
                kt = jnp.concatenate([k_ref[rows, pair], khot_ref[rows, :]], 1)
                e = jnp.exp(dot(kt, qb[j]))
                whole = whole + jnp.sum(e, axis=0, keepdims=True)
                acc = acc + dot(vt_ref[pair, rows], e.astype(BF))
            least_ref[j] = whole
            lse_ref[j] = lse_ref[j] + jnp.log(whole)
            split_heads(j, acc * (1.0 / whole), o_ref)

    @pl.when(jnp.min(least_ref[...]) < LEAST)
    def _():
        cross_forward_exact(q_ref, k_ref, vt_ref, khot_ref, qhot_ref, o_ref, lse_ref, qb)


def cross_forward_exact(q_ref, k_ref, vt_ref, khot_ref, qhot_ref, o_ref, lse_ref, qb):
    build_blocks(q_ref, qhot_ref, qb)
    tiles = k_ref.shape[0] // TILE

    @pl.loop(0, 8)
    def _(j):
        pair = pair_of(j // 2)

        def scores(t):
            rows = pl.ds(t * TILE, TILE)
            return dot(jnp.concatenate([k_ref[rows, pair], khot_ref[rows, :]], 1), qb[j])

        top = jnp.max(scores(0), axis=0, keepdims=True)
        for t in range(1, tiles):
            top = jnp.maximum(top, jnp.max(scores(t), axis=0, keepdims=True))
        whole = jnp.zeros((1, 256), F32)
        acc = jnp.zeros((128, 256), F32)
        for t in range(tiles):
            e = jnp.exp(scores(t) - top)
            whole = whole + jnp.sum(e, axis=0, keepdims=True)
            acc = acc + dot(vt_ref[pair, t * TILE : (t + 1) * TILE], e.astype(BF))
        lse_ref[j] = top + jnp.log(whole)
        split_heads(j, acc * (1.0 / whole), o_ref)


def cross_backward(q_ref, k_ref, v_ref, khot_ref, qhot_ref, do_ref, lse_ref, dl_ref, dq_ref, dkv_ref, qb, db):
    build_blocks(q_ref, qhot_ref, qb)
    build_blocks(do_ref, None, db)
    size = min(2048, k_ref.shape[0])

    @pl.loop(0, 4)
    def _(p):
        pair = pair_of(p)
        dq = [0.0, 0.0]
        for t in range(k_ref.shape[0] // size):
            rows = slice(t * size, (t + 1) * size)
            k, v = k_ref[rows, pair], v_ref[rows, pair]
            k_turned = k.T
            kt = jnp.concatenate([k, khot_ref[rows, :]], 1)
            dk = dv = 0.0
            for h in range(2):
                j = 2 * p + h
                pr = jnp.exp(dot(kt, qb[j]) - lse_ref[j])
                dp = dot(v, db[j])
                ds = (pr * (dp - dl_ref[j])).astype(BF)
                dv += dot(pr.astype(BF), db[j], NT)
                dk += dot(ds, qb[j, 0:128, :], NT)
                dq[h] += dot(k_turned, ds)
            dkv_ref[rows, pair] = dk.astype(BF)
            dkv_ref[rows, pl.ds(pl.multiple_of(512 + 128 * p, 128), 128)] = dv.astype(BF)
        for h in range(2):
            split_heads(2 * p + h, dq[h] * 0.125, dq_ref)


def work_item(t, i, blocks):
    first = (i + 2) // 2
    second = (t >= first).astype(jnp.int32)
    tile = t - second * first
    start = jnp.where(second == 1, (blocks - 1 - i) * BLK + HALF, i * BLK)
    return second, tile, start - tile * TILE


def relative_positions(swap):
    k = lax.broadcasted_iota(jnp.int32, (TILE, 2 * HALF), 0)
    q = lax.broadcasted_iota(jnp.int32, (TILE, 2 * HALF), 1) & (HALF - 1)
    return (k ^ swap) - q


def self_tiles(blocks, i, full, masked):
    for h, block in ((0, i), (1, blocks - 1 - i)):
        last = block >> 1
        place = lambda tile: pl.multiple_of((tile ^ (i >> 1)) * TILE, TILE)
        pl.loop(0, last)(lambda tile, h=h: full(h, place(tile)))
        masked(h, place(last), (block & 1) * BLK + h * HALF)


def self_forward(blocks, i, q_ref, k_ref, vt_ref, khot_ref, qhot_ref, o_ref, lse_ref, qb, m_s, l_s, acc):
    build_blocks(q_ref, qhot_ref, qb)
    shift = bound_scores(q_ref, k_ref, qhot_ref, qb)
    l_s[...] = jnp.zeros(l_s.shape, F32)
    acc[...] = jnp.zeros(acc.shape, F32)

    def visit(h, r0, offset=None):
        rows = pl.ds(r0, TILE)
        hot = khot_ref[rows, :]
        for p in range(4):
            j = 2 * p + h
            s = dot(jnp.concatenate([k_ref[rows, 128 * p : 128 * p + 128], hot], 1), qb[j])
            if offset is not None:
                s = jnp.where(relative_positions((i & 1) * BLK) <= offset, s, BIG)
            e = jnp.exp(s)
            l_s[j] += jnp.sum(e, axis=0, keepdims=True)
            acc[j] += dot(vt_ref[128 * p : 128 * p + 128, rows], e.astype(BF))

    self_tiles(blocks, i, visit, visit)
    for j in range(8):
        lse_ref[j] = shift[j] + jnp.log(l_s[j])
        split_heads(j, acc[j] * (1.0 / l_s[j]), o_ref)

    @pl.when(jnp.min(l_s[...]) < LEAST)
    def _():
        self_forward_exact(blocks, i, q_ref, k_ref, vt_ref, khot_ref, qhot_ref, o_ref, lse_ref, qb, m_s, l_s, acc)


def self_forward_exact(blocks, i, q_ref, k_ref, vt_ref, khot_ref, qhot_ref, o_ref, lse_ref, qb, m_s, l_s, acc):
    build_blocks(q_ref, qhot_ref, qb)
    swap = (i & 1) * BLK
    items = blocks // 2 + 1
    m_s[...] = jnp.full(m_s.shape, -3e38, F32)
    l_s[...] = jnp.zeros(l_s.shape, F32)
    acc[...] = jnp.zeros(acc.shape, F32)

    def scores(t, p):
        h, tile, offset = work_item(t, i, blocks)
        r0 = pl.multiple_of((tile ^ (i >> 1)) * TILE, TILE)
        kt = jnp.concatenate([k_ref[pl.ds(r0, TILE), pair_of(p)], khot_ref[pl.ds(r0, TILE), :]], 1)
        return jnp.where(relative_positions(swap) <= offset, dot(kt, qb[2 * p + h]), BIG), 2 * p + h, r0

    @pl.loop(0, 4 * items)
    def _(step):
        s, j, _ = scores(step // 4, step % 4)
        m_s[j] = jnp.maximum(m_s[j], jnp.max(s, axis=0, keepdims=True))

    @pl.loop(0, 4 * items)
    def _(step):
        s, j, r0 = scores(step // 4, step % 4)
        e = jnp.exp(s - m_s[j])
        l_s[j] += jnp.sum(e, axis=0, keepdims=True)
        acc[j] += dot(vt_ref[pair_of(step % 4), pl.ds(r0, TILE)], e.astype(BF))

    for j in range(8):
        lse_ref[j] = m_s[j] + jnp.log(l_s[j])
        split_heads(j, acc[j] * (1.0 / l_s[j]), o_ref)


def self_backward(
    blocks, i, q_ref, k_ref, kt_ref, v_ref, khot_ref, qhot_ref, do_ref, lse_ref, dl_ref, dq_ref, dkv_ref,
    qb, db, dqa, dka, dva,
):
    build_blocks(q_ref, qhot_ref, qb)
    build_blocks(do_ref, None, db)
    dqa[...] = jnp.zeros(dqa.shape, F32)
    dka[...] = jnp.zeros(dka.shape, F32)
    dva[...] = jnp.zeros(dva.shape, F32)

    def visit(h, r0, offset=None):
        rows = pl.ds(r0, TILE)
        hot = khot_ref[rows, :]
        for p in range(4):
            j = 2 * p + h
            lanes = slice(128 * p, 128 * p + 128)
            s = dot(jnp.concatenate([k_ref[rows, lanes], hot], 1), qb[j])
            if offset is not None:
                s = jnp.where(relative_positions((i & 1) * BLK) <= offset, s, BIG)
            pr = jnp.exp(s - lse_ref[j])
            dp = dot(v_ref[rows, lanes], db[j])
            ds = (pr * (dp - dl_ref[j])).astype(BF)
            dva[rows, lanes] += dot(pr.astype(BF), db[j], NT)
            dka[rows, lanes] += dot(ds, qb[j, 0:128, :], NT)
            dqa[j] += dot(kt_ref[lanes, rows], ds)

    self_tiles(blocks, i, visit, visit)
    dkv_ref[:, 0:512] = dka[...].astype(BF)
    dkv_ref[:, 512:1024] = dva[...].astype(BF)
    for j in range(8):
        split_heads(j, dqa[j] * 0.125, dq_ref)


def norm_forward(v, gain, bias):
    centered = v - jnp.mean(v, axis=-1, keepdims=True)
    scale = lax.rsqrt(jnp.mean(centered * centered, axis=-1, keepdims=True) + EPS)
    hat = centered * scale
    return hat * gain + bias, hat, scale


def norm_backward(g, hat, scale, gain):
    gh = g * gain
    out = scale * (gh - jnp.mean(gh, axis=-1, keepdims=True) - hat * jnp.mean(gh * hat, axis=-1, keepdims=True))
    return out, jnp.sum(g * hat, axis=0, keepdims=True), jnp.sum(g, axis=0, keepdims=True)


def gelu_both(x):
    c = 0.7978845608028654
    sq = x * x
    t = jnp.tanh(c * x * (1 + 0.044715 * sq))
    half = 0.5 * (1 + t)
    return x * half, half + 0.5 * x * (1 - t * t) * (c * (1 + 3 * 0.044715 * sq))


def inner_rows(g_refT, o_ref, dl_ref):
    for p in range(4):
        both = []
        for a in range(2):
            rows = slice(128 * p + 64 * a, 128 * p + 64 * a + 64)
            both.append(jnp.sum(g_refT[rows, :].astype(F32) * o_ref[rows, :], axis=0, keepdims=True))
        for h in range(2):
            cols = slice(h * HALF, (h + 1) * HALF)
            dl_ref[2 * p + h] = jnp.concatenate([both[0][:, cols], both[1][:, cols]], 1)


class Cut:
    def __init__(self, chips, zsize, tokens, sizes, extra=0):
        self.chips, self.zsize, self.tokens, self.extra = chips, zsize, tokens, extra
        self.at, rows = [], 0
        for R, C in sizes:
            self.at.append(rows)
            rows += R // (zsize * chips) * (C // 512)
        self.per_z = rows + extra
        self.rows = tokens + zsize * self.per_z

    def write(self, index, keep, me, evens, odd_ref):
        R, C = keep.shape
        core, chip = me & 1, me >> 1
        size, half = R // (self.zsize * self.chips), C // 2
        for turn in range(2):
            side = core if turn == 0 else 1 - core
            for j in range(self.chips):
                for z in range(self.zsize):
                    row = pl.multiple_of(z * (R // self.zsize) + (chip ^ j) * size, size)
                    for c in range(half // 256):
                        left = pl.multiple_of(side * half + 256 * c, 256)
                        at = self.tokens + z * self.per_z + self.at[index] + c * size
                        piece = keep[pl.ds(row, size), pl.ds(left, 256)]
                        if turn == 0:
                            evens[j][at : at + size, :] = piece
                        else:
                            odd_ref[j, at : at + size, :] = piece

    def write_tokens(self, r, part, evens, odd_ref):
        for c in range(2):
            piece = part[:, 256 * c : 256 * c + 256]
            if r % 2:
                odd_ref[r // 2, BLK * c : BLK * c + BLK, :] = piece
            else:
                evens[r // 2][BLK * c : BLK * c + BLK, :] = piece

    def write_extra(self, z, part, evens, odd_ref):
        at = self.tokens + z * self.per_z + self.per_z - self.extra
        for j in range(self.chips):
            evens[j][at : at + self.extra, :] = part
            odd_ref[j, at : at + self.extra, :] = part

    def outs(self):
        return [shape((self.rows, 256))] * self.chips + [shape((self.chips, self.rows, 256))]


def join_tokens(x, seg):
    def kernel(x_hbm, seg_hbm, out, seg_s, sems):
        loads = [
            pltpu.make_async_copy(x_hbm, out.ref.at[0:BLK, :], sems.at[0]),
            pltpu.make_async_copy(seg_hbm, seg_s, sems.at[1]),
        ]
        for copy in loads:
            copy.start()
        for copy in loads[::-1]:
            copy.wait()
            if copy is loads[1]:
                row = jnp.concatenate([seg_s[...].astype(F32), jnp.zeros((1, 256), F32)], 1)
                out.ref[BLK:, :] = jnp.broadcast_to(row, (16, 512)).astype(BF)

    scratch = [pltpu.VMEM((1, 256), jnp.int32), pltpu.SemaphoreType.DMA((2,))]
    return call(kernel, "join_tokens", (x, seg), [HB] * 2, [shape((BLK + 16, 512))], [SENT], scratch)[0]


def prepare(after, grad, *rest):
    def kernel(g_ref, *refs):
        ga_ref, gb_ref = refs[-2:]
        ga_ref[...] = g_ref[0:HALF, :]
        gb_ref[...] = g_ref[HALF:, :]

    ins = (grad, after, *rest)
    return call(
        kernel, "prepare", ins, [VM, HB] + [ANY] * (len(ins) - 2), [shape((HALF, 512)), shape((HALF, 512))], [VM, VM]
    )


def self_front_kernel(n, me_ref, tag_ref, *refs):
    xs, refs = refs[:n], refs[n:]
    (table_ref, w_ref, so_ref, cqw_ref, gain_ref, bias_ref,
     low_o, k_o, v_o, khot_o, qhot_ref, qT_o, oT_ref, lse_o, hat_ref, scale_ref, first_ref,
     flow_ref, cqT_ref, mixT_ref, slow_o, vt_s, start_s, qb, m_s, l_s, acc) = refs
    low_s, k_s, v_s, khot_s, qT_ref, lse_ref = (out.ref for out in (low_o, k_o, v_o, khot_o, qT_o, lse_o))
    segs = [x[BLK : BLK + 16, 0:BLK].astype(F32)[0:1].astype(jnp.int32) for x in xs]
    table = table_ref[...].astype(F32)
    ids = lax.broadcasted_iota(jnp.int32, (NTAGS, 512), 0)
    rows = [jnp.sum(jnp.where(ids == tag_ref[s], table, 0.0), axis=0, keepdims=True) for s in range(SEGS)]
    tag_rows = jnp.concatenate(rows + [jnp.zeros((128 - SEGS, 512), F32)], 0).astype(BF)
    for r in range(n):
        at = slice(r * BLK, (r + 1) * BLK)
        ids = lax.broadcasted_iota(jnp.int32, (128, BLK), 0)
        hot = (ids == segs[r]).astype(F32).T
        khot_s[at, :] = ((ids == segs[r]) | (ids == SEGS)).astype(F32).T.astype(BF)
        start = xs[r][0:BLK, :].astype(F32) + dot(hot.astype(BF), tag_rows)
        low = start.astype(BF)
        low_s[at, :] = low
        if r == 0:
            start_s[0:HALF, :] = start[0:HALF]
        if r == n - 1:
            start_s[HALF:, :] = start[HALF:]
        k_s[at, :] = dot(low, w_ref[:, 512:1024]).astype(BF)
        v = dot(low, w_ref[:, 1024:1536]).astype(BF)
        v_s[at, :] = v
        vt_s[:, at] = v.T
    for out in (low_o, k_o, v_o, khot_o):
        out.send()
    seg = jnp.concatenate([segs[0][:, 0:HALF], segs[n - 1][:, HALF:]], 1)
    ids = lax.broadcasted_iota(jnp.int32, (16, BLK), 0)
    qhot_ref[...] = jnp.where((ids != seg) & (ids < SEGS), BIG, 0.0).astype(BF)
    slow = start_s[...].astype(BF)
    slow_o.ref[...] = slow
    qT_ref[...] = (dot(slow, w_ref[:, 0:512]) * 0.125).astype(BF).T
    slow_o.send()
    qT_o.send()
    self_forward(n, me_ref[0], qT_ref, k_s, vt_s, khot_s, qhot_ref, oT_ref, lse_ref, qb, m_s, l_s, acc)
    mixT = oT_ref[...].astype(BF)
    mixT_ref[...] = mixT
    first, hat, scale = norm_forward(
        start_s[...] + dot(mixT, so_ref[...], TN), gain_ref[...].astype(F32)[0:1], bias_ref[...].astype(F32)[0:1]
    )
    hat_ref[...] = hat
    scale_ref[...] = jnp.broadcast_to(scale, (BLK, 128))
    first_ref[...] = first
    first_low = first.astype(BF)
    flow_ref[...] = first_low
    cqT_ref[...] = (dot(first_low, cqw_ref[...]) * 0.125).astype(BF).T


def self_front(me, tags, xs, table, w, so, cqw, gain, bias):
    n = len(xs)
    S = n * BLK
    big = [shape((S, 512)), shape((S, 512)), shape((S, 512)), shape((S, 128))]
    outs = big + [
        shape((16, BLK)), shape((512, BLK)), shape((512, BLK), F32), shape((8, 1, BLK), F32), shape((BLK, 512), F32),
        shape((BLK, 128), F32), shape((BLK, 512), F32), shape((BLK, 512)), shape((512, BLK)), shape((512, BLK)),
        shape((BLK, 512)),
    ]
    scratch = [
        pltpu.VMEM((512, S), BF), pltpu.VMEM((BLK, 512), F32), pltpu.VMEM((8, 256, 256), BF),
        pltpu.VMEM((8, 1, 256), F32), pltpu.VMEM((8, 1, 256), F32), pltpu.VMEM((8, 128, 256), F32),
    ]
    kinds = [SENT] * 4 + [VM, SENT, VM, SENT] + [VM] * 6 + [SENT]
    return call(
        lambda *refs: self_front_kernel(n, *refs), "self_front", (me, tags, *xs, table, w, so, cqw, gain, bias),
        [SM, SM] + [VM] * (n + 6), outs, kinds, scratch, n,
    )


def middle_kernel(n, cut, me_ref, len_ref, *refs):
    encs, refs = refs[:n], refs[n:]
    (w_ref, cqT_ref, qhot_ref, first_ref, co_ref, fi_ref, fo_ref, bi_ref, bo_ref, gain_ref, bias_ref,
     oga_ref, ogb_ref, *refs) = refs
    if cut:
        evens, (odd_ref, *refs) = refs[: cut.chips], refs[cut.chips :]
    (la_ref, lb_ref, gmid_ref, gcb_ref, gcT_ref, dl_ref, lse_ref, cmixT_ref, vec_o, dib_o, khot_ref, k_ref, v_ref,
     hid_ref, slow_ref, gffn_ref, gpre_ref, k_s, v_s, vt_s, oT_s, slope_s, qb, least_s, fi_s, fo_s, sems) = refs
    me, vec_ref, dib_ref = me_ref[0], vec_o.ref, dib_o.ref
    e0 = len_ref[0]
    e1 = e0 + len_ref[1]
    e2 = e1 + len_ref[2]
    for r in range(n):
        at = slice(r * BLK, (r + 1) * BLK)
        pos = lax.broadcasted_iota(jnp.int32, (BLK, 128), 0) + (me ^ r) * BLK
        seg = (pos >= e0).astype(jnp.int32) + (pos >= e1).astype(jnp.int32) + (pos >= e2).astype(jnp.int32)
        lane = lax.broadcasted_iota(jnp.int32, (BLK, 128), 1)
        khot_ref[at, :] = ((lane == seg) | (lane == SEGS)).astype(F32).astype(BF)
        enc = encs[r][...]
        k_s[at, :] = dot(enc, w_ref[:, 0:512]).astype(BF)
        v = dot(enc, w_ref[:, 512:1024]).astype(BF)
        v_s[at, :] = v
        vt_s[:, at] = v.T
    copies = [pltpu.make_async_copy(k_s, k_ref, sems.at[0]), pltpu.make_async_copy(v_s, v_ref, sems.at[1])]
    for copy in copies:
        copy.start()
    cross_forward(cqT_ref, k_s, vt_s, khot_ref, qhot_ref, oT_s, lse_ref, qb, least_s)
    cmixT = oT_s[...].astype(BF)
    cmixT_ref[...] = cmixT
    gain_rows, bias_rows = gain_ref[...].astype(F32), bias_ref[...].astype(F32)
    gains = [gain_rows[j : j + 1] for j in range(3)]
    shifts = [bias_rows[j : j + 1] for j in range(3)]
    second, hat2, scale2 = norm_forward(first_ref[...] + dot(cmixT, co_ref[...], TN), gains[1], shifts[1])
    second_low = second.astype(BF)
    slow_ref[...] = second_low
    out = second + bo_ref[...].astype(F32)
    for c in range(4):
        cols = slice(512 * c, 512 * c + 512)
        act, slope = gelu_both(dot(second_low, fi_ref[:, cols]) + bi_ref[:, cols].astype(F32))
        hidden = act.astype(BF)
        hid_ref[:, cols] = hidden
        slope_s[:, cols] = slope
        out = out + dot(hidden, fo_ref[cols, :])
    result, hat3, scale3 = norm_forward(out, gains[2], shifts[2])
    la_ref[...] = result[0:HALF].astype(BF)
    lb_ref[...] = result[HALF:].astype(BF)
    og = jnp.concatenate([oga_ref[...], ogb_ref[...]], 0).astype(F32)
    g3, gg3, gb3 = norm_backward(og, hat3, scale3, gains[2])
    g_ffn = g3.astype(BF)
    gffn_ref[...] = g_ffn
    d_out_bias = jnp.sum(g_ffn.astype(F32), axis=0, keepdims=True)
    g2 = g3
    for c in range(4):
        cols = slice(512 * c, 512 * c + 512)
        g_pre = (dot(g_ffn, fo_ref[cols, :], NT) * slope_s[:, cols]).astype(BF)
        gpre_ref[:, cols] = g_pre
        dib_ref[:, cols] = jnp.sum(g_pre.astype(F32), axis=0, keepdims=True)
        g2 = g2 + dot(g_pre, fi_ref[:, cols], NT)
        if cut:
            fi_s[:, cols] = dot(second_low, g_pre, TN).astype(BF)
            fo_s[cols, :] = dot(hid_ref[:, cols], g_ffn, TN).astype(BF)
    g_mid, gg2, gb2 = norm_backward(g2, hat2, scale2, gains[1])
    gmid_ref[...] = g_mid
    g_cb = g_mid.astype(BF)
    gcb_ref[...] = g_cb
    gcT_ref[...] = dot(co_ref[...], g_cb, NT).astype(BF)
    inner_rows(gcT_ref, oT_s, dl_ref)
    vec_ref[...] = jnp.concatenate([gg2, gb2, gg3, gb3, d_out_bias, jnp.zeros((3, 512), F32)], 0)
    if cut:
        cut.write(0, fi_s, me, evens, odd_ref)
        cut.write(1, fo_s, me, evens, odd_ref)
    for copy in copies:
        copy.wait()


def middle(cut, me, lens, encs, *rest):
    n = len(encs)
    S = n * BLK
    outs = (cut.outs() if cut else []) + [
        shape((HALF, 512)), shape((HALF, 512)), shape((BLK, 512), F32), shape((BLK, 512)), shape((512, BLK)),
        shape((8, 1, 256), F32), shape((8, 1, 256), F32), shape((512, BLK)), shape((8, 512), F32),
        shape((1, 2048), F32), shape((S, 128)), shape((S, 512)), shape((S, 512)),
    ]
    hold = [shape((BLK, 2048)), shape((BLK, 512)), shape((BLK, 512)), shape((BLK, 2048))]
    kinds = [VM] * (len(outs) - 5) + [SENT] * 2 + [VM] + [HB] * 2
    plain = [] if cut else hold
    outs += plain
    kinds += [VM] * len(plain)
    scratch = ([pltpu.VMEM(x.shape, BF) for x in hold] if cut else []) + [
        pltpu.VMEM((S, 512), BF), pltpu.VMEM((S, 512), BF), pltpu.VMEM((512, S), BF), pltpu.VMEM((512, BLK), F32),
        pltpu.VMEM((BLK, 2048), F32), pltpu.VMEM((8, 256, 256), BF), pltpu.VMEM((8, 1, 256), F32), pltpu.VMEM((512, 2048), BF),
        pltpu.VMEM((2048, 512), BF), pltpu.SemaphoreType.DMA((2,)),
    ]
    got = call(
        lambda *refs: middle_kernel(n, cut, *refs), "middle", (me, lens, *encs, *rest),
        [SM, SM] + [VM] * (n + 13), outs, kinds, scratch, n,
    )
    first = len(cut.outs()) if cut else 0
    return got[:first], got[first:]


def cross_back_kernel(n, cut, weights, me_ref, *refs):
    half = n // 2
    (k_s, v_s, _, *refs) = refs
    encs, refs = refs[:n], refs[n:]
    (w_ref, cqT_ref, khot_ref, qhot_ref, gcT_ref, lse_ref, dl_ref, gmid_ref, cqw_ref, hat_ref, scale_ref, gain_ref,
     so_ref, oT_ref, cmixT_ref, gcb_ref, flow_ref, mixT_ref, *refs) = refs
    going, (odd_ref, gstart, gmT, dl1, vec, *refs) = refs[:half], refs[half:]
    evens = [out.ref for out in going]
    gstart_ref, gmT_ref, dl1_ref, vec_ref = gstart.ref, gmT.ref, dl1.ref, vec.ref
    dkv_ref, dq_ref, gbr_ref, dqT_s, qb, db, enc_s, keep, kv_keep, sems = refs
    late = []
    if weights:
        for j in range(n):
            rows = slice(BLK * j, BLK * (j + 1))
            late.append(pltpu.make_async_copy(encs[j], enc_s.at[rows, :], sems.at[j]))
    for copy in late:
        copy.start()
    cross_backward(
        cqT_ref, k_s, v_s, khot_ref, qhot_ref, gcT_ref, lse_ref, dl_ref, dqT_s, dkv_ref, qb, db
    )
    me = me_ref[0]
    for r in range(n):
        at = slice(r * BLK, (r + 1) * BLK)
        part = dot(dkv_ref[at, :], w_ref[...], NT)
        cut.write_tokens(r, part.astype(BF), evens, odd_ref)
    if weights:
        for out in going:
            out.send(slice(0, 512))
    dq = dqT_s[...].astype(BF).T
    dq_ref[...] = dq
    g1 = gmid_ref[...] + dot(dq, cqw_ref[...], NT)
    g_start, gg1, gb1 = norm_backward(g1, hat_ref[...], scale_ref[:, 0:1], gain_ref[...].astype(F32)[0:1])
    gstart_ref[...] = g_start
    g_branch = g_start.astype(BF)
    gbr_ref[...] = g_branch
    gmT_ref[...] = dot(so_ref[...], g_branch, NT).astype(BF)
    inner_rows(gmT_ref, oT_ref, dl1_ref)
    vec_ref[...] = jnp.concatenate([gg1, gb1, jnp.zeros((6, 512), F32)], 0)
    for out in (gstart, gmT, dl1, vec):
        out.send()
    if weights:
        keep[0] = dot(cmixT_ref[...], gcb_ref[...]).astype(BF)
        keep[1] = dot(flow_ref[...], dq_ref[...], TN).astype(BF)
        keep[2] = dot(mixT_ref[...], g_branch).astype(BF)
        for j in range(3):
            cut.write(1 + j, keep.at[j], me, evens, odd_ref)
        for copy in late:
            copy.wait()
        kv_keep[...] = dot(enc_s[...], dkv_ref[...], TN).astype(BF)
        cut.write(0, kv_keep, me, evens, odd_ref)
        for out in going:
            out.send(slice(512, cut.rows))


def cross_back(cut, weights, me, k, v, after, encs, *rest):
    n = len(encs)
    S = n * BLK
    more = [shape((S, 1024)), shape((BLK, 512)), shape((BLK, 512))]
    outs = cut.outs() + [
        shape((BLK, 512), F32), shape((512, BLK)), shape((8, 1, 256), F32), shape((8, 512), F32)
    ] + ([] if weights else more)
    scratch = ([pltpu.VMEM(s.shape, s.dtype) for s in more] if weights else []) + [
        pltpu.VMEM((512, BLK), F32), pltpu.VMEM((8, 256, 256), BF), pltpu.VMEM((8, 128, 256), BF),
        pltpu.VMEM((S if weights else 16, 512), BF), pltpu.VMEM((3, 512, 512), BF), pltpu.VMEM((512, 1024), BF),
        pltpu.SemaphoreType.DMA((n,)),
    ]
    got = call(
        lambda *refs: cross_back_kernel(n, cut, weights, *refs), "cross_back", (me, k, v, after, *encs, *rest),
        [SM, VM, VM, HB if weights else ANY] + [ANY] * n + [VM] * 18,
        outs, [SENT] * (n // 2) + [VM] + [SENT] * 4 + [VM] * (len(outs) - n // 2 - 5), scratch, n,
    )
    return got[: n // 2 + 1], got[n // 2 + 1 :]


def self_back_kernel(n, cut, weights, me_ref, tag_ref, *refs):
    half = n // 2
    (_, low_hbm, k_s, v_s, khot_s, qT_ref, qhot_ref, gmT_ref, lse_ref, dl_ref, w_ref,
     gstart_ref, slow_ref, vec1_ref, vec2_ref, dib_ref, *refs) = refs
    evens, (odd_ref, small_ref, *refs) = refs[:half], refs[half:]
    (dkv_ref, dq_ref, low_s, kt_s, dqT_s, qb, db, dqa, dka, dva, keep, sems) = refs
    if weights:
        low_copy = pltpu.make_async_copy(low_hbm, low_s, sems.at[0])
        low_copy.start()
    for r in range(n):
        at = slice(r * BLK, (r + 1) * BLK)
        kt_s[:, at] = k_s[at, :].T
    me = me_ref[0]
    self_backward(
        n, me, qT_ref, k_s, kt_s, v_s, khot_s, qhot_ref, gmT_ref, lse_ref, dl_ref, dqT_s, dkv_ref,
        qb, db, dqa, dka, dva,
    )
    dq = dqT_s[...].astype(BF).T
    dq_ref[...] = dq
    mine = gstart_ref[...] + dot(dq, w_ref[:, 0:512], NT)
    sums = jnp.zeros((128, 512), F32)
    for r in range(n):
        at = slice(r * BLK, (r + 1) * BLK)
        part = dot(dkv_ref[at, :], w_ref[:, 512:1536], NT)
        if r == 0:
            part = jnp.concatenate([part[:HALF] + mine[:HALF], part[HALF:]], 0)
        if r == n - 1:
            part = jnp.concatenate([part[:HALF], part[HALF:] + mine[HALF:]], 0)
        part = part.astype(BF)
        sums = sums + dot(khot_s[at, :], part, TN)
        cut.write_tokens(r, part, evens, odd_ref)
    ids = lax.broadcasted_iota(jnp.int32, (NTAGS, 512), 0)
    table = jnp.zeros((NTAGS, 512), F32)
    for s in range(SEGS):
        table = table + jnp.where(ids == tag_ref[s], sums[s : s + 1, :], 0.0)
    v1, v2 = vec1_ref[...], vec2_ref[...]
    vectors = [v1[0:1], v2[0:1], v2[2:3], v1[1:2], v2[1:2], v2[3:4], v2[4:5], jnp.zeros((1, 512), F32)]
    if weights:
        zs = cut.zsize
        wide, lanes, tags = 2048 // zs, 512 // zs, NTAGS // zs
        for z in range(zs):
            rows = []
            for c in range(2):
                rows.append(table[tags * z : tags * (z + 1), 256 * c : 256 * c + 256])
            rows += [dib_ref[:, wide * z + 256 * c : wide * z + 256 * (c + 1)] for c in range(wide // 256)]
            cut_rows = [v[:, lanes * z : lanes * (z + 1)] for v in vectors]
            rows += [jnp.concatenate(cut_rows[2 * c : 2 * c + 2], 1) for c in range(4)]
            used = 2 * tags + wide // 256 + 4
            rows.append(jnp.zeros((16 - used, 256), F32))
            cut.write_extra(z, jnp.concatenate(rows, 0).astype(BF), evens, odd_ref)
        small_ref[...] = jnp.zeros(small_ref.shape, F32)
        keep[:, 0:512] = dot(slow_ref[...], dq_ref[...], TN).astype(BF)
        low_copy.wait()
        keep[:, 512:1536] = dot(low_s[...], dkv_ref[...], TN).astype(BF)
        for j in range(3):
            cut.write(j, keep.at[:, 512 * j : 512 * j + 512], me, evens, odd_ref)
    else:
        small_ref[...] = jnp.concatenate([table] + vectors, 0)


def self_back(cut, weights, me, tags, after, low, k, v, khot, *rest):
    S = k.shape[0]
    n = S // BLK
    more = [shape((S, 1024)), shape((BLK, 512))]
    outs = cut.outs() + [shape((24, 512), F32)] + ([] if weights else more)
    scratch = ([pltpu.VMEM(s.shape, s.dtype) for s in more] if weights else []) + [
        pltpu.VMEM((S if weights else 16, 512), BF), pltpu.VMEM((512, S), BF),
        pltpu.VMEM((512, BLK), F32), pltpu.VMEM((8, 256, 256), BF), pltpu.VMEM((8, 128, 256), BF),
        pltpu.VMEM((8, 128, 256), F32), pltpu.VMEM((S, 512), F32), pltpu.VMEM((S, 512), F32),
        pltpu.VMEM((512, 1536), BF), pltpu.SemaphoreType.DMA((1,)),
    ]
    got = call(
        lambda *refs: self_back_kernel(n, cut, weights, *refs), "self_back",
        (me, tags, after, low, k, v, khot, *rest), [SM, SM, HB, HB] + [VM] * 14, outs, None, scratch, n,
    )
    return got[: n // 2 + 1], got[n // 2 + 1 :]


def add_core(evens, got, after):
    count = len(evens)

    def kernel(*refs):
        ins, got_ref, (first, *outs) = refs[:count], refs[count], refs[count + 2 :]
        for j, out_ref in enumerate([first.ref] + outs):
            out_ref[...] = (ins[j][...].astype(F32) + got_ref[j].astype(F32)).astype(BF)
            if j == 0:
                first.send()

    return call(
        kernel, "add_core", (*evens, got, after), [VM] * (count + 1) + [ANY], [shape(e.shape) for e in evens],
        [SENT] + [VM] * (count - 1),
    )


def gate(kept, *arrays):
    def kernel(*refs):
        refs[-1][...] = jnp.zeros(refs[-1].shape, F32)

    return call(kernel, "gate", (kept, *arrays), [HB] + [ANY] * len(arrays), [TOKEN])[0]


def add_chips(cut, zme, terms, after, near=None, far=None, pinned=False):
    count, per = len(terms), cut.per_z
    extra = [] if near is None else [near, far]
    base = extra[0].shape[1] if extra else 0

    def kernel(z_ref, *refs):
        ins, (near_ref, far_ref, *outs) = refs[:count], refs[count + len(after) + len(extra) :]
        s, sems = outs[-2:]
        loads = []
        for j in range(count):
            rows = slice(cut.tokens, cut.rows)
            loads.append(pltpu.make_async_copy(ins[j].at[rows, :], s.at[j, rows, :], sems.at[0, j]))
        for j in range(count if cut.tokens else 0):
            rows = slice(0, cut.tokens)
            loads.append(pltpu.make_async_copy(ins[j].at[rows, :], s.at[j, rows, :], sems.at[1, j]))
        for copy in loads:
            copy.start()
        if extra:
            early = refs[count + len(after) : count + len(after) + 2]
            near_ref[:, 0:base, :] = early[0][...]
            far_ref[:, 0:base, :] = early[1][...]
        for copy in loads[:count]:
            copy.wait()
        for k in range(4):
            row = pl.multiple_of(cut.tokens + (z_ref[0] ^ k) * per, 16)
            value = total([s[j, pl.ds(row, per), :] for j in range(count)]).astype(BF)
            (near_ref if k < 2 else far_ref)[k % 2, base : base + per, :] = value
        for copy in loads[count:]:
            copy.wait()
        for c in range(2 if cut.tokens else 0):
            part = total([s[j, BLK * c : BLK * c + BLK, :] for j in range(count)])
            outs[0][:, 256 * c : 256 * c + 256] = part

    outs = [shape((2, base + per, 256)), shape((2, base + per, 256))] + [shape((BLK, 512), F32)] * (cut.tokens > 0)
    return call(
        kernel, "add_chips", (zme, *terms, *after, *extra),
        [SM, HB] + [ANY] * (count - 1) + [HB if pinned else ANY] * len(after) + [VM] * len(extra), outs, None,
        [pltpu.VMEM((count, cut.rows, 256), BF), pltpu.SemaphoreType.DMA((2, count))],
    )


def add_far(near, got):
    def kernel(near_ref, got_ref, send_ref, keep_ref):
        send_ref[...] = (near_ref[1].astype(F32) + got_ref[1].astype(F32)).astype(BF)
        keep_ref[...] = near_ref[0].astype(F32) + got_ref[0].astype(F32)

    outs = [shape(near.shape[1:]), shape(near.shape[1:], F32)]
    return call(kernel, "add_far", (near, got), [VM] * 2, outs)


def add_near(kept, sent):
    def kernel(kept_ref, sent_ref, out_ref):
        out_ref[...] = (kept_ref[...] + sent_ref[...].astype(F32)).astype(BF)

    return call(kernel, "add_near", (kept, sent), [VM] * 2, [shape(kept.shape)])[0]


def add_last(kept, sent, extra, after):
    rows = kept.shape[0] - extra

    def kernel(kept_ref, sent_ref, *refs):
        out_ref, small_ref = refs[-2:]
        value = kept_ref[...] + sent_ref[...].astype(F32)
        out_ref[...] = value[:rows].astype(BF)
        small_ref[...] = value[rows:]

    return call(kernel, "add_last", (kept, sent, *after), [VM] * 2 + [ANY] * len(after), [shape((rows, 256)), shape((extra, 256), F32)])


def unpack_shards(me, shards, shapes, layout):
    n = len(shards)
    chips = n // 2

    def kernel(me_ref, *refs):
        parts, outs = refs[:n], refs[n:]
        me = me_ref[0]
        for k in range(n):
            chip, core = (me >> 1) ^ (k >> 1), (me & 1) ^ (k & 1)
            for out, R, left, C, at in layout:
                size, half = R // chips, C // 2
                row = pl.multiple_of(chip * size, size)
                for c in range(half // 256):
                    col = pl.multiple_of(left + core * half + 256 * c, 256)
                    value = parts[k][at + c * size : at + (c + 1) * size, :].astype(F32)
                    outs[out][pl.ds(row, size), pl.ds(col, 256)] = value

    return call(kernel, "unpack_shards", (me, *shards), [SM] + [VM] * n, [shape(s, F32) for s in shapes])


def exchange(x, axis, k):
    size = lax.axis_size(axis)
    return lax.ppermute(x, axis, [(i, i ^ k) for i in range(size)])


def once(x, after):
    return lax.optimization_barrier((x, after))[0]


def gather(x, after=None):
    n = lax.axis_size("seq")
    parts = {0: x}
    for k in range(2, n, 2):
        parts[k] = exchange(x, "seq", k)
    for k in range(0, n, 2):
        held = parts[k] if after is None or k == 0 else once(parts[k], after)
        parts[k + 1] = exchange(held, "seq", 1)
    return [parts[k] for k in range(n)]


def across_chips(mine):
    return [mine[0]] + [exchange(mine[j], "seq", 2 * j) for j in range(1, len(mine))]


def plain_weights(pairs, small):
    zsize, zme = lax.axis_size("rows"), lax.axis_index("rows")
    outs = []
    for left, right, turned in pairs:
        whole = lax.psum(dot(left, right, ((1,) if turned else (0,), (0,))), ("seq", "rows"))
        size = whole.shape[0] // zsize
        outs.append(lax.dynamic_slice_in_dim(whole, zme * size, size, 0))
    whole = lax.psum(small, ("seq", "rows"))
    parts = []
    for x, dim in ((whole[:NTAGS], 0), (whole[NTAGS : NTAGS + 4].reshape(-1), 0), (whole[NTAGS + 4 :], 1)):
        size = x.shape[dim] // zsize
        parts.append(lax.dynamic_slice_in_dim(x, zme * size, size, dim))
    return outs, parts


def local(
    dec_input, encoded, segment_ids, pair_tags, enc_lengths, out_grad, tag_table, self_qkv, self_out, cross_query,
    cross_kv, cross_out, ffn_in, ffn_in_bias, ffn_out, ffn_out_bias, norm_gain, norm_bias,
):
    n, zsize = lax.axis_size("seq"), lax.axis_size("rows")
    chips = n // 2
    me, zme = lax.axis_index("seq").astype(jnp.int32)[None], lax.axis_index("rows").astype(jnp.int32)[None]
    mirror = n - 1
    weights = zsize == 4 and 512 // (zsize * chips) >= 16
    square = (512, 512)
    cut1 = Cut(chips, zsize, 0, [(512, 2048), (2048, 512)]) if weights else None
    cut2 = Cut(chips, zsize, 512, [(512, 1024), square, square, square] if weights else [])
    cut3 = Cut(chips, zsize, 512, [square] * 3 if weights else [], 16 if weights else 0)

    message = join_tokens(dec_input[0], segment_ids)
    b_in, b_out = ffn_in_bias[None], ffn_out_bias[None]
    oga, ogb = prepare(message, out_grad[0], b_in, b_out)
    xs = gather(message, oga)
    mine = once(encoded[0], xs[2::2])
    enc_parts = {0: encoded[0]} | {k: exchange(mine, "seq", k) for k in range(2, n, 2)}
    ogb = exchange(once(ogb, xs[2::2]), "seq", mirror)
    (low_all, K, V, khot, qhotT, qT, oT, lse, hat1, scale1, first, first_low, cqT, mixT, start_low) = self_front(
        me, pair_tags[0], xs, tag_table, self_qkv, self_out, cross_query, norm_gain, norm_bias
    )
    for k in range(0, n, 2):
        enc_parts[k + 1] = exchange(once(enc_parts[k], (cqT, ogb)) if k else encoded[0], "seq", 1)
    encs = [enc_parts[k] for k in range(n)]
    terms1, (la, lb, g_mid, g_cb, gcT, cdelta, clse, cmixT, vec2, dib, ehot, ek, ev, *back1) = middle(
        cut1, me, enc_lengths[0], encs, cross_kv, cqT, qhotT, first, cross_out, ffn_in, ffn_out,
        b_in, b_out, norm_gain, norm_bias, oga, ogb,
    )
    lb = exchange(lb, "seq", mirror)
    layer_out = jnp.concatenate([la, lb])[None]
    token = g_mid
    if weights:
        sums1 = add_core(terms1[:-1], exchange(terms1[-1], "seq", 1), token)
        token = sums1[0]
        sums1 = across_chips(sums1)
    terms2, (g_start, gmT, delta, vec1, *back2) = cross_back(
        cut2, weights, me, ek, ev, token, encs, cross_kv, cqT, ehot, qhotT, gcT, clse, cdelta, g_mid, cross_query,
        hat1, scale1, norm_gain, self_out, oT, cmixT, g_cb, first_low, mixT,
    )
    token = g_start
    if weights:
        token = gate(terms2[0], *sums1[1:])
    sums2 = add_core(terms2[:-1], exchange(terms2[-1], "seq", 1), token)
    token = sums2[0]
    sums2 = across_chips(sums2)
    terms3, (small, *back3) = self_back(
        cut3, weights, me, pair_tags[0], token, low_all, K, V, khot, qT, qhotT, gmT, lse, delta, self_qkv,
        g_start, start_low, vec1, vec2, dib,
    )
    if weights:
        near1, far1 = add_chips(cut1, zme, sums1, (terms3[0],))
        near12, far12, encoded_grad = add_chips(cut2, zme, sums2, (terms3[0], lb), near1, far1)
        sums3 = add_core(terms3[:-1], exchange(terms3[-1], "seq", 1), near12)
        got12 = exchange(once(far12, sums3[0]), "rows", 2)
        sums3 = across_chips(sums3)
        send12, kept12 = add_far(near12, got12)
        near3, far3, input_grad = add_chips(cut3, zme, sums3, (kept12,))
        got3 = exchange(far3, "rows", 2)
        share12 = add_near(kept12, exchange(send12, "rows", 1))
        shards12 = gather(once(share12, near3))
        send3, kept3 = add_far(near3, got3)
        share3, small = add_last(kept3, exchange(send3, "rows", 1), 16, shards12[2::2])
        ins, outs = 512 // zsize, 2048 // zsize

        def layout(places):
            found, at = [], 0
            for out, R, left, C in places:
                found.append((out, R, left, C, at))
                at += R // chips * (C // 512)
            return found

        places = [(0, ins, 0, 2048), (1, outs, 0, 512), (2, ins, 0, 1024)] + [(j, ins, 0, 512) for j in (3, 4, 5)]
        shapes = [(ins, 2048), (outs, 512), (ins, 1024), (ins, 512), (ins, 512), (ins, 512)]
        d_fi, d_fo, d_ckv, d_co, d_cq, d_so = unpack_shards(me, shards12, shapes, layout(places))
        shards3 = gather(share3, d_fi)
        places = [(0, ins, 512 * j, 512) for j in range(3)]
        d_qkv = unpack_shards(me, shards3, [(ins, 1536)], layout(places))[0]
        tags, wide, lanes = NTAGS // zsize, outs // 256, 512 // zsize
        d_table = jnp.concatenate([small[0:tags], small[tags : 2 * tags]], axis=1)
        d_inner = small[2 * tags : 2 * tags + wide].reshape(-1)
        vectors = small[2 * tags + wide : 2 * tags + wide + 4].reshape(8, lanes)
    else:
        encoded_grad, input_grad = (
            total([jnp.concatenate([t[:BLK], t[BLK:]], axis=1) for t in terms])
            for terms in (sums2, across_chips(add_core(terms3[:-1], exchange(terms3[-1], "seq", 1), small)))
        )
        (hidden, second_low, g_ffn, g_pre), (edkv, dcq, g_branch), (dkv, dq) = back1, back2, back3
        enc_all = jnp.concatenate(encs)
        pairs = [
            (second_low, g_pre, False), (hidden, g_ffn, False), (enc_all, edkv, False), (cmixT, g_cb, True),
            (first_low, dcq, False), (mixT, g_branch, True), (start_low, dq, False), (low_all, dkv, False),
        ]
        small = jnp.concatenate([small[:NTAGS], dib.reshape(4, 512), small[NTAGS:]])
        (d_fi, d_fo, d_ckv, d_co, d_cq, d_so, dq, dkv), (d_table, d_inner, vectors) = plain_weights(pairs, small)
        d_qkv = jnp.concatenate([dq, dkv], axis=1)
    return (
        layer_out, input_grad[None], encoded_grad[None], d_table, d_qkv, d_so, d_cq, d_ckv, d_co, d_fi, d_inner, d_fo,
        vectors[6], vectors[0:3], vectors[3:6],
    )


def solution(mesh):
    tokens = P("rows", "seq", None)
    placed = (tokens, tokens, P("rows", "seq"), P("rows", None), P("rows", None), tokens) + (P(),) * 12
    rows = P("rows", None)
    return jax.shard_map(
        local,
        mesh=mesh,
        in_specs=placed,
        out_specs=(tokens, tokens, tokens)
        + (rows,) * 7
        + (P("rows"), rows, P("rows"), P(None, "rows"), P(None, "rows")),
        check_vma=False,
    )
```
